256 devices in a mesh: fsdp: 32 (over y, x, core), tp: 8 (over z).
Axes of the slice: x: 4, y: 4, z: 8, core: 2. Of those that a mesh axis runs over, the one named last changes fastest.
Arguments:
- gradient: bfloat16 [2, 8192, 8192], P(None, 'fsdp', 'tp'), may hold values from -188 to 188
- momentum: float32 [2, 8192, 8192], P(None, 'fsdp', 'tp'), may hold values from -6 to 6
- right_basis: float32 [2, 512, 8192], P(None, 'fsdp', 'tp'), may hold values from -6 to 6
Outputs:
- update: bfloat16 [2, 8192, 8192], P(None, 'fsdp', 'tp')
- momentum_next: float32 [2, 8192, 8192], P(None, 'fsdp', 'tp')
- basis_next: float32 [2, 512, 8192], P(None, 'fsdp', 'tp')
The draws below stay inside these ranges and needn't reach their ends.
All inputs are finite; a program needn't handle non-finite values.
Results may differ from the reference program's by a relative error of at most 0.001.
Values sent between devices are 32-bit elements; how exact they have to be, the bound alone decides.
A program may use at most 64 MiB of HBM per device.

```python
import math
import jax
import jax.numpy as jnp
from jax import lax

D = 8192
RANK = 512
MATS = 2


def draw_gradient(key, part):
    key = jax.random.fold_in(key, 11)
    keys = jax.random.split(key, 3)
    row_scale = jnp.exp(math.log(10.0) * jax.random.uniform(keys[0], (MATS, D, 1), jnp.float32))
    col_ramp = jnp.exp(math.log(3.0) * jnp.arange(D, dtype=jnp.float32) / D)
    col_scale = jnp.exp(math.log(10.0) * jax.random.uniform(keys[1], (MATS, 1, D), jnp.float32)) * col_ramp[None, None, :]
    values = jnp.clip(jax.random.normal(keys[2], (MATS, D, D), jnp.float32), -5.0, 5.0)
    return (values * row_scale * col_scale / 8.0).astype(jnp.bfloat16)


def block_scale(rng, dims, shards, smallest, largest):
    gain, own = 1.0, jax.random.fold_in(rng, 6)
    for dim, blocks in shards:
        heights = jnp.exp(jax.random.uniform(jax.random.fold_in(own, dim), (blocks,), jnp.float32, smallest / len(shards), largest / len(shards)))
        gain = gain * jnp.repeat(heights, dims[dim] // blocks).reshape([-1 if axis == dim else 1 for axis in range(len(dims))])
    return gain


def bell_draw(key, shape, scale, most, cuts=(), held_as=jnp.bfloat16):
    level = block_scale(key, shape, cuts, -0.22, 0.18) if cuts else 1.0
    values = jax.random.normal(key, shape, jnp.float32) * scale * level
    return jnp.minimum(jnp.maximum(values, -most), most).astype(held_as)


def setup_inputs(seed: int = 0) -> dict:
    key_of = jax.random.split(jax.random.key(seed), 4)
    gradient = draw_gradient(jax.random.fold_in(key_of[3], 71), 0)
    momentum = bell_draw(key_of[1], (MATS, D, D), 1.0, 6.0, ((1, 32), (2, 8)), jnp.float32)
    right_basis = bell_draw(key_of[2], (MATS, RANK, D), 1.0, 6.0, ((1, 32), (2, 8)), jnp.float32)
    return {"gradient": gradient, "momentum": momentum, "right_basis": right_basis}


momentum_decay = 0.8
epsilon_sq = 1e-06

def one_matrix(grad_one, moment_one, basis_one):
    highest = lax.Precision.HIGHEST
    blended = moment_one + grad_one.astype(jnp.float32)
    left = jnp.dot(blended.astype(jnp.float32), basis_one.T.astype(jnp.float32), precision=highest, preferred_element_type=jnp.float32)
    gram = jnp.dot(left.T.astype(jnp.float32), left.astype(jnp.float32), precision=highest, preferred_element_type=jnp.float32)
    triangle = jnp.linalg.cholesky(gram)
    left_orth = jax.scipy.linalg.solve_triangular(triangle, left.T, lower=True).T
    right_raw = jnp.dot(left_orth.T.astype(jnp.float32), blended.astype(jnp.float32), precision=highest, preferred_element_type=jnp.float32)
    inverse = lax.rsqrt(lax.optimization_barrier(jnp.mean(right_raw * right_raw, axis=1)) + epsilon_sq)
    basis_next = right_raw * inverse[:, None]
    momentum_next = blended - (1.0 - momentum_decay) * jnp.dot(left_orth.astype(jnp.float32), right_raw.astype(jnp.float32), precision=highest, preferred_element_type=jnp.float32)
    update = (math.sqrt(D / RANK) * jnp.dot(left_orth.astype(jnp.float32), basis_next.astype(jnp.float32), precision=highest, preferred_element_type=jnp.float32)).astype(jnp.bfloat16)
    return (update, momentum_next, basis_next)

def reference(gradient, momentum, right_basis):
    updates = []
    moments = []
    bases = []
    for index in range(MATS):
        update, moment_new, basis_new = one_matrix(gradient[index], momentum[index], right_basis[index])
        updates.append(update)
        moments.append(moment_new)
        bases.append(basis_new)
    return (jnp.stack(updates), jnp.stack(moments), jnp.stack(bases))
```

```python
import math

import jax
import jax.numpy as jnp
from jax import lax
from jax.experimental import pallas as pl
from jax.experimental.pallas import tpu as pltpu
from jax.sharding import PartitionSpec as P

D = 8192
RANK = 512
momentum_decay = 0.8
epsilon_sq = 1e-06
MESH = pl.DeviceIdType.MESH
F32 = jnp.float32
HIGH = lax.Precision.HIGH
HIGHEST = lax.Precision.HIGHEST
VMEM_BYTES = 56 * 1024 * 1024


def dot(a, b, ca, cb, precision):
    return lax.dot_general(
        a, b, (((ca,), (cb,)), ((), ())), precision=precision, preferred_element_type=F32
    )


class Place:
    def __init__(self, send_sem, recv_sem):
        f = lax.axis_index("fsdp")
        self.f = f
        self.z = lax.axis_index("tp")
        self.c = lax.rem(f, 2)
        self.x = lax.rem(f // 2, 4)
        self.y = f // 8
        self.send_sem, self.recv_sem = send_sem, recv_sem
        self.count = 0
        self.open = []

    def dev(self, y=None, x=None, z=None, c=None):
        y = self.y if y is None else y
        x = self.x if x is None else x
        c = self.c if c is None else c
        z = self.z if z is None else z
        return ((y * 4 + x) * 2 + c, z)

    def partner(self):
        return self.dev(c=1 - self.c)

    def xs(self, d):
        return lax.rem(self.x + d, 4)

    def ys(self, d):
        return lax.rem(self.y + d, 4)

    def zs(self, d):
        return lax.rem(self.z + d, 8)

    def copy(self, src, dst, to):
        i = self.count
        self.count += 1
        cp = pltpu.make_async_remote_copy(
            src_ref=src,
            dst_ref=dst,
            send_sem=self.send_sem.at[i],
            recv_sem=self.recv_sem.at[i],
            device_id=to,
            device_id_type=MESH,
        )
        cp.start()
        self.open.append(cp)
        return cp

    def barrier(self, peers):
        sem = pltpu.get_barrier_semaphore()
        for p in peers:
            pl.semaphore_signal(sem, inc=1, device_id=p, device_id_type=MESH)
        pl.semaphore_wait(sem, len(peers))

    def drain(self):
        for cp in self.open:
            cp.wait_send()
        self.open = []


def received(copies):
    for cp in copies:
        cp.wait_recv()


class Gather:
    def __init__(self, pc, buf):
        self.pc, self.buf = pc, buf

    def first(self):
        pc, buf = self.pc, self.buf
        self.one = []
        for d in (1, 3, 2):
            a, b = buf.at[pc.y, pc.x, 0], buf.at[pc.y, pc.x, 1]
            self.one.append(pc.copy(a, a, pc.dev(x=pc.xs(d))))
            self.one.append(pc.copy(b, b, pc.dev(y=pc.ys(d))))

    def second(self):
        pc, buf = self.pc, self.buf
        received(self.one)
        self.two = []
        for d in (1, 3, 2):
            a, b = buf.at[pc.y, :, 0], buf.at[:, pc.x, 1]
            self.two.append(pc.copy(a, a, pc.dev(y=pc.ys(d))))
            self.two.append(pc.copy(b, b, pc.dev(x=pc.xs(d))))

    def finish(self):
        received(self.two)


class Scatter:
    def __init__(self, pc, buf, r1, acc, r2):
        self.pc, self.buf, self.r1, self.acc, self.r2 = pc, buf, r1, acc, r2

    def first(self):
        pc, buf = self.pc, self.buf
        self.one = []
        for d in (1, 3, 2):
            self.one.append(pc.copy(buf.at[pc.ys(d), :, 0], self.r1.at[0, d - 1], pc.dev(y=pc.ys(d))))
            self.one.append(pc.copy(buf.at[:, pc.xs(d), 1], self.r1.at[1, d - 1], pc.dev(x=pc.xs(d))))

    def second(self):
        pc, buf, r1, acc = self.pc, self.buf, self.r1, self.acc
        received(self.one)
        acc[0] = buf[pc.y, :, 0] + r1[0, 0] + r1[0, 1] + r1[0, 2]
        acc[1] = buf[:, pc.x, 1] + r1[1, 0] + r1[1, 1] + r1[1, 2]
        self.two = []
        for d in (1, 3, 2):
            self.two.append(pc.copy(acc.at[0, pc.xs(d)], self.r2.at[0, d - 1], pc.dev(x=pc.xs(d))))
            self.two.append(pc.copy(acc.at[1, pc.ys(d)], self.r2.at[1, d - 1], pc.dev(y=pc.ys(d))))

    def finish(self):
        pc, acc, r2 = self.pc, self.acc, self.r2
        received(self.two)
        own0 = acc[0, pc.x] + r2[0, 0] + r2[0, 1] + r2[0, 2]
        own1 = acc[1, pc.y] + r2[1, 0] + r2[1, 1] + r2[1, 2]
        return own0, own1


def reduce_kernel(
    grad, mom, rb, g_out, w_out, left_out,
    blend, blend_send, basis, lpart, lrecv, left,
    gbuf, gr1, gacc, gr2, zbuf, gfull,
    wbuf, wr1, wacc, wr2, wall, left_all,
    send_sem, recv_sem, local_sem,
):
    pc = Place(send_sem, recv_sem)
    c, x, y, z = pc.c, pc.x, pc.y, pc.z
    peers = [pc.partner()]
    peers += [pc.dev(x=pc.xs(d)) for d in (1, 2, 3)]
    peers += [pc.dev(y=pc.ys(d)) for d in (1, 2, 3)]
    peers += [pc.dev(z=pc.zs(d)) for d in range(1, 8)]
    pc.barrier(peers)

    basis_swap = pc.copy(rb.at[1 - c], basis.at[y, x, c], pc.partner())
    basis[y, x, c] = rb[c]
    blend_send[...] = mom[1 - c] + grad[1 - c].astype(F32)
    blend_swap = pc.copy(blend_send, blend.at[c], pc.partner())
    blend[c] = mom[c] + grad[c].astype(F32)
    basis_swap.wait_recv()
    gather = Gather(pc, basis)
    gather.first()
    gather.second()
    blend_swap.wait_recv()
    gather.finish()

    for half in range(2):
        part = dot(blend[half], basis[...].reshape(RANK, 1024), 1, 1, HIGHEST)
        lpart[4 * half:4 * half + 4] = part.reshape(4, 64, RANK)
    sums = []
    for d in (4, 3, 5, 2, 6, 1, 7):
        sums.append(pc.copy(lpart.at[pc.zs(d)], lrecv.at[d - 1], pc.dev(z=pc.zs(d))))
    received(sums)
    own = lpart[z]
    for d in range(7):
        own = own + lrecv[d]
    left[z] = own
    lefts = []
    for d in (1, 7, 2, 6, 3, 5, 4):
        lefts.append(pc.copy(left.at[z], left.at[z], pc.dev(z=pc.zs(d))))

    blocks = []
    for i in range(4):
        row = dot(own[:, 128 * i:128 * i + 128], own[:, :128 * i + 128], 0, 0, HIGHEST)
        blocks += [row[:, 128 * j:128 * j + 128] for j in range(i + 1)]
    gbuf[...] = jnp.concatenate(blocks, axis=0).reshape(4, 4, 2, 40, 128)
    gscatter = Scatter(pc, gbuf, gr1, gacc, gr2)
    gscatter.first()
    gscatter.second()
    own0, own1 = gscatter.finish()
    zbuf[z, 0] = own0
    zbuf[z, 1] = own1
    zs = []
    for d in (4, 3, 5, 2, 6, 1, 7):
        zs.append(pc.copy(zbuf.at[z], zbuf.at[z], pc.dev(z=pc.zs(d))))
    received(zs)
    total = zbuf[0]
    for d in range(1, 8):
        total = total + zbuf[d]
    gfull[y, x] = total
    ggather = Gather(pc, gfull)
    ggather.first()
    ggather.second()
    ggather.finish()
    g_copy = pltpu.make_async_copy(gfull, g_out, local_sem.at[0])
    g_copy.start()

    received(lefts)
    left_all[c] = left[pl.ds(4 * c, 4)]
    left_swap = pc.copy(left.at[pl.ds(4 * (1 - c), 4)], left_all.at[c], pc.partner())
    for i in range(4):
        lt = left[:, :, 128 * i:128 * i + 128].reshape(RANK, 128)
        part = dot(lt, blend[...].reshape(512, 1024), 0, 0, HIGHEST)
        wbuf[i] = part.reshape(4, 2, 16, 1024)
    wscatter = Scatter(pc, wbuf, wr1, wacc, wr2)
    wscatter.first()
    wscatter.second()
    own0, own1 = wscatter.finish()
    wall[c, y, x, 0] = own0
    wall[c, y, x, 1] = own1
    wgather = Gather(pc, wall.at[c])
    wgather.first()
    wgather.second()
    wgather.finish()
    w_swap = pc.copy(wall.at[c], wall.at[c], pc.partner())
    left_swap.wait_recv()
    left_copy = pltpu.make_async_copy(left_all, left_out, local_sem.at[1])
    left_copy.start()
    w_swap.wait_recv()
    w_copy = pltpu.make_async_copy(wall, w_out, local_sem.at[2])
    w_copy.start()
    g_copy.wait()
    left_copy.wait()
    w_copy.wait()
    pc.drain()


def factor_block(load):
    groups = 16
    a = [load(r) for r in range(groups)]
    lane = lax.broadcasted_iota(jnp.int32, (8, 128), 1)
    sub = lax.broadcasted_iota(jnp.int32, (8, 128), 0)
    out = [None] * groups

    def column(v, j):
        return jnp.broadcast_to(v[:, j:j + 1], (8, 128))

    for q in range(32):
        r0, s0, j0 = q // 2, 4 * (q % 2), 4 * q
        rows = [jnp.broadcast_to(a[r0][s0 + s:s0 + s + 1, :], (8, 128)) for s in range(4)]
        p = {(s, t): column(rows[s], j0 + t) for s in range(4) for t in range(s, 4)}
        inside = (lane >= j0) & (lane < j0 + 4)
        v = [jnp.where(inside, jnp.where(lane == j0 + s, 1.0, 0.0), rows[s]) for s in range(4)]
        low, inv = {}, []
        for s in range(4):
            inv.append(1.0 / p[s, s])
            for t in range(s + 1, 4):
                low[t, s] = p[s, t] * inv[s]
            for u in range(s + 1, 4):
                for t in range(u, 4):
                    p[u, t] = p[u, t] - low[u, s] * p[s, t]
        for t in range(1, 4):
            for s in range(t):
                v[t] = v[t] - low[t, s] * v[s]
        w = [v[s] * inv[s] for s in range(4)]
        for s in (2, 1, 0):
            for t in range(s + 1, 4):
                w[s] = w[s] - low[t, s] * w[t]
        done = [v[s] * lax.rsqrt(p[s, s]) for s in range(4)]
        o = done[0]
        for s in range(1, 4):
            o = jnp.where(sub == s0 + s, done[s], o)
        out[r0] = o if s0 == 0 else jnp.where(sub < 4, out[r0], o)
        for r in range(r0 if s0 == 0 else r0 + 1, groups):
            cols = [column(a[r], j0 + t) for t in range(4)]
            new = jnp.where(inside, 0.0, a[r])
            for s in range(4):
                new = new - cols[s] * w[s]
            a[r] = new
    return out


def factor_kernel(g, linv, work, tri):
    flat = g[...].reshape(1280, 128)
    k = 0
    for i in range(4):
        for j in range(i + 1):
            work[j, 128 * i:128 * i + 128] = flat[128 * k:128 * k + 128]
            k += 1
    row = lax.broadcasted_iota(jnp.int32, (RANK, 128), 0)
    col = lax.broadcasted_iota(jnp.int32, (RANK, 128), 1)
    for j in range(4):
        linv[j] = jnp.where(row == col + 128 * j, 1.0, 0.0)

    def panel(k, carry):
        off = pl.multiple_of(k * 128, 128)
        rows = factor_block(lambda r: work[k, pl.ds(off + 8 * r, 8), :])
        for r in range(16):
            tri[8 * r:8 * r + 8, :] = rows[r]
        own = jnp.where(row[:128] >= col[:128], tri[...], 0.0)
        below = jnp.where(row >= off + 128, dot(work[k], own, 1, 1, HIGHEST), 0.0)
        tri[...] = own
        for j in range(4):
            step = dot(own, linv[j, pl.ds(off, 128), :], 1, 0, HIGHEST)
            linv[j, pl.ds(off, 128), :] = step
            linv[j] = linv[j] - dot(below, step, 1, 0, HIGHEST)
            work[j] = work[j] - dot(below, below[128 * j:128 * j + 128], 1, 1, HIGHEST)
        return carry

    lax.fori_loop(0, 4, panel, 0)


def finish_kernel(
    grad, mom, linv, w, left, update, momentum_next, basis_next,
    tri, right, orth, sums, squares, send_sem, recv_sem,
):
    pc = Place(send_sem, recv_sem)
    c, z = pc.c, pc.z
    pc.barrier([pc.partner()] + [pc.dev(z=pc.zs(d)) for d in range(1, 8)])
    swap = pc.copy(linv, tri.at[c], pc.partner())
    tri[c] = linv[...]

    def whole(m):
        return jnp.concatenate([tri[m, j] for j in range(4)], axis=1)

    def raw(m):
        t = whole(m)

        def part(j, carry):
            cols = pl.ds(pl.multiple_of(j * 256, 256), 256)
            wj = w[m, :, :, :, :, cols].reshape(RANK, 256)
            right[m, :, cols] = dot(t, wj, 1, 0, HIGH)
            return carry

        lax.fori_loop(0, 4, part, 0)
        r = right[m]
        sums[m] = dot(jnp.ones((8, 1024), F32), r * r, 1, 1, HIGHEST)

    raw(c)
    swap.wait_recv()
    raw(1 - c)
    pieces = [sums[m, 0:1, 128 * j:128 * j + 128] for m in range(2) for j in range(4)]
    squares[z] = jnp.concatenate(pieces, axis=0)
    zs = []
    for d in (4, 3, 5, 2, 6, 1, 7):
        zs.append(pc.copy(squares.at[z], squares.at[z], pc.dev(z=pc.zs(d))))
    for m in range(2):
        orth[m] = dot(left[m].reshape(256, RANK), whole(m), 1, 1, HIGH)

        def feed(j, carry, m=m):
            cols = pl.ds(pl.multiple_of(j * 256, 256), 256)
            back = dot(orth[m], right[m, :, cols], 1, 0, HIGH)
            blended = mom[m, :, cols] + grad[m, :, cols].astype(F32)
            momentum_next[m, :, cols] = blended - (1.0 - momentum_decay) * back
            return carry

        lax.fori_loop(0, 4, feed, 0)
    received(zs)
    total = squares[0]
    for d in range(1, 8):
        total = total + squares[d]
    inverse = lax.rsqrt(total / D + epsilon_sq)
    lane = lax.broadcasted_iota(jnp.int32, (16, RANK), 1)
    sub = lax.broadcasted_iota(jnp.int32, (16, RANK), 0)
    for m in range(2):
        inv = jnp.concatenate([inverse[4 * m + j:4 * m + j + 1] for j in range(4)], axis=1)
        orth[m] = orth[m] * inv
        pick = jnp.where(lane == pc.f * 16 + sub, inv, 0.0)

        def direction(j, carry, m=m, pick=pick):
            cols = pl.ds(pl.multiple_of(j * 256, 256), 256)
            rj = right[m, :, cols]
            out = math.sqrt(D / RANK) * dot(orth[m], rj, 1, 0, HIGH)
            update[m, :, cols] = out.astype(jnp.bfloat16)
            basis_next[m, :, cols] = dot(pick, rj, 1, 0, HIGHEST)
            return carry

        lax.fori_loop(0, 4, direction, 0)
    pc.drain()


def shards(gradient, momentum, right_basis):
    vmem = pl.BlockSpec(memory_space=pltpu.VMEM)
    anywhere = pl.BlockSpec(memory_space=pl.ANY)
    shape = lambda s: jax.ShapeDtypeStruct(s, F32)
    buf = lambda *s: pltpu.VMEM(s, F32)
    n1 = 85
    gram, w, left = pl.pallas_call(
        reduce_kernel,
        out_shape=(shape((4, 4, 2, 40, 128)), shape((2, 4, 4, 2, 16, 1024)), shape((2, 4, 64, RANK))),
        in_specs=[vmem] * 3,
        out_specs=[anywhere] * 3,
        scratch_shapes=[
            buf(2, 256, 1024), buf(256, 1024), buf(4, 4, 2, 16, 1024),
            buf(8, 64, RANK), buf(7, 64, RANK), buf(8, 64, RANK),
            buf(4, 4, 2, 40, 128), buf(2, 3, 4, 40, 128), buf(2, 4, 40, 128), buf(2, 3, 40, 128),
            buf(8, 2, 40, 128), buf(4, 4, 2, 40, 128),
            buf(4, 4, 2, 16, 1024), buf(2, 3, 4, 16, 1024), buf(2, 4, 16, 1024), buf(2, 3, 16, 1024),
            buf(2, 4, 4, 2, 16, 1024), buf(2, 4, 64, RANK),
            pltpu.SemaphoreType.DMA((n1,)), pltpu.SemaphoreType.DMA((n1,)), pltpu.SemaphoreType.DMA((3,)),
        ],
        compiler_params=pltpu.CompilerParams(
            collective_id=0, has_side_effects=True, vmem_limit_bytes=VMEM_BYTES
        ),
        name="reduce",
    )(gradient, momentum, right_basis)
    linv = pl.pallas_call(
        factor_kernel,
        out_shape=shape((4, RANK, 128)),
        in_specs=[vmem],
        out_specs=vmem,
        scratch_shapes=[buf(4, RANK, 128), buf(128, 128)],
        compiler_params=pltpu.CompilerParams(vmem_limit_bytes=VMEM_BYTES),
        name="factor",
    )(gram)
    n2 = 8
    return pl.pallas_call(
        finish_kernel,
        out_shape=(
            jax.ShapeDtypeStruct((2, 256, 1024), jnp.bfloat16), shape((2, 256, 1024)), shape((2, 16, 1024))
        ),
        in_specs=[vmem] * 5,
        out_specs=[vmem] * 3,
        scratch_shapes=[
            buf(2, 4, RANK, 128), buf(2, RANK, 1024), buf(2, 256, RANK), buf(2, 8, RANK), buf(8, 8, 128),
            pltpu.SemaphoreType.DMA((n2,)), pltpu.SemaphoreType.DMA((n2,)),
        ],
        compiler_params=pltpu.CompilerParams(
            collective_id=1, has_side_effects=True, vmem_limit_bytes=VMEM_BYTES
        ),
        name="finish",
    )(gradient, momentum, linv, w, left)


def solution(mesh):
    placed = (P(None, "fsdp", "tp"), P(None, "fsdp", "tp"), P(None, "fsdp", "tp"))
    return jax.shard_map(
        shards,
        mesh=mesh,
        in_specs=placed,
        out_specs=placed,
        check_vma=False,
    )
```

```python
import math

import jax
import jax.numpy as jnp
from jax import lax
from jax.experimental import pallas as pl
from jax.experimental.pallas import tpu as pltpu
from jax.sharding import PartitionSpec as P

D = 8192
RANK = 512
momentum_decay = 0.8
epsilon_sq = 1e-06
MESH = pl.DeviceIdType.MESH
F32 = jnp.float32
HIGH = lax.Precision.HIGH
HIGHEST = lax.Precision.HIGHEST
VMEM_BYTES = 56 * 1024 * 1024


def dot(a, b, ca, cb, precision):
    return lax.dot_general(
        a, b, (((ca,), (cb,)), ((), ())), precision=precision, preferred_element_type=F32
    )


class Place:
    def __init__(self, send_sem, recv_sem):
        f = lax.axis_index("fsdp")
        self.f = f
        self.z = lax.axis_index("tp")
        self.c = lax.rem(f, 2)
        self.x = lax.rem(f // 2, 4)
        self.y = f // 8
        self.send_sem, self.recv_sem = send_sem, recv_sem
        self.count = 0
        self.open = []

    def dev(self, y=None, x=None, z=None, c=None):
        y = self.y if y is None else y
        x = self.x if x is None else x
        c = self.c if c is None else c
        z = self.z if z is None else z
        return ((y * 4 + x) * 2 + c, z)

    def partner(self):
        return self.dev(c=1 - self.c)

    def xs(self, d):
        return lax.rem(self.x + d, 4)

    def ys(self, d):
        return lax.rem(self.y + d, 4)

    def zs(self, d):
        return lax.rem(self.z + d, 8)

    def copy(self, src, dst, to):
        i = self.count
        self.count += 1
        cp = pltpu.make_async_remote_copy(
            src_ref=src,
            dst_ref=dst,
            send_sem=self.send_sem.at[i],
            recv_sem=self.recv_sem.at[i],
            device_id=to,
            device_id_type=MESH,
        )
        cp.start()
        self.open.append(cp)
        return cp

    def barrier(self, peers):
        sem = pltpu.get_barrier_semaphore()
        for p in peers:
            pl.semaphore_signal(sem, inc=1, device_id=p, device_id_type=MESH)
        pl.semaphore_wait(sem, len(peers))

    def drain(self):
        for cp in self.open:
            cp.wait_send()
        self.open = []


def received(copies):
    for cp in copies:
        cp.wait_recv()


class Gather:
    def __init__(self, pc, buf):
        self.pc, self.buf = pc, buf

    def first(self):
        pc, buf = self.pc, self.buf
        self.one = []
        for d in (1, 3, 2):
            a, b = buf.at[pc.y, pc.x, 0], buf.at[pc.y, pc.x, 1]
            self.one.append(pc.copy(a, a, pc.dev(x=pc.xs(d))))
            self.one.append(pc.copy(b, b, pc.dev(y=pc.ys(d))))

    def second(self):
        pc, buf = self.pc, self.buf
        received(self.one)
        self.two = {}
        for d in (1, 3, 2):
            a, b = buf.at[pc.y, :, 0], buf.at[:, pc.x, 1]
            self.two[d] = (pc.copy(a, a, pc.dev(y=pc.ys(d))), pc.copy(b, b, pc.dev(x=pc.xs(d))))

    def finish(self):
        for d in (1, 3, 2):
            received(self.two[d])


class Scatter:
    def __init__(self, pc, buf, r1, acc, r2):
        self.pc, self.buf, self.r1, self.acc, self.r2 = pc, buf, r1, acc, r2

    def first(self):
        pc, buf = self.pc, self.buf
        self.one = []
        for d in (1, 3, 2):
            self.one.append(pc.copy(buf.at[pc.ys(d), :, 0], self.r1.at[0, d - 1], pc.dev(y=pc.ys(d))))
            self.one.append(pc.copy(buf.at[:, pc.xs(d), 1], self.r1.at[1, d - 1], pc.dev(x=pc.xs(d))))

    def second(self):
        pc, buf, r1, acc = self.pc, self.buf, self.r1, self.acc
        received(self.one)
        acc[0] = buf[pc.y, :, 0] + r1[0, 0] + r1[0, 1] + r1[0, 2]
        acc[1] = buf[:, pc.x, 1] + r1[1, 0] + r1[1, 1] + r1[1, 2]
        self.two = []
        for d in (1, 3, 2):
            self.two.append(pc.copy(acc.at[0, pc.xs(d)], self.r2.at[0, d - 1], pc.dev(x=pc.xs(d))))
            self.two.append(pc.copy(acc.at[1, pc.ys(d)], self.r2.at[1, d - 1], pc.dev(y=pc.ys(d))))

    def finish(self):
        pc, acc, r2 = self.pc, self.acc, self.r2
        received(self.two)
        own0 = acc[0, pc.x] + r2[0, 0] + r2[0, 1] + r2[0, 2]
        own1 = acc[1, pc.y] + r2[1, 0] + r2[1, 1] + r2[1, 2]
        return own0, own1


def factor_block(load, tick):
    groups = 16
    a = [load(r) for r in range(groups)]
    lane = lax.broadcasted_iota(jnp.int32, (8, 128), 1)
    sub = lax.broadcasted_iota(jnp.int32, (8, 128), 0)
    out = [None] * groups

    def column(v, j):
        return jnp.broadcast_to(v[:, j:j + 1], (8, 128))

    for q in range(32):
        r0, s0, j0 = q // 2, 4 * (q % 2), 4 * q
        rows = [jnp.broadcast_to(a[r0][s0 + s:s0 + s + 1, :], (8, 128)) for s in range(4)]
        p = {(s, t): column(rows[s], j0 + t) for s in range(4) for t in range(s, 4)}
        inside = (lane >= j0) & (lane < j0 + 4)
        v = [jnp.where(inside, jnp.where(lane == j0 + s, 1.0, 0.0), rows[s]) for s in range(4)]
        low, inv = {}, []
        for s in range(4):
            inv.append(1.0 / p[s, s])
            for t in range(s + 1, 4):
                low[t, s] = p[s, t] * inv[s]
            for u in range(s + 1, 4):
                for t in range(u, 4):
                    p[u, t] = p[u, t] - low[u, s] * p[s, t]
        for t in range(1, 4):
            for s in range(t):
                v[t] = v[t] - low[t, s] * v[s]
        w = [v[s] * inv[s] for s in range(4)]
        for s in (2, 1, 0):
            for t in range(s + 1, 4):
                w[s] = w[s] - low[t, s] * w[t]
        done = [v[s] * lax.rsqrt(p[s, s]) for s in range(4)]
        o = done[0]
        for s in range(1, 4):
            o = jnp.where(sub == s0 + s, done[s], o)
        out[r0] = o if s0 == 0 else jnp.where(sub < 4, out[r0], o)
        for r in range(r0 if s0 == 0 else r0 + 1, groups):
            cols = [column(a[r], j0 + t) for t in range(4)]
            new = jnp.where(inside, 0.0, a[r])
            for s in range(4):
                new = new - cols[s] * w[s]
            a[r] = new
        tick(q)
    return out


def kernel(
    grad, mom, rb, update, momentum_next, basis_next,
    blend, blend_send, basis, lpart, lrecv, left, perm,
    gbuf, gr1, gacc, gr2, zbuf, gfull,
    wbuf, wr1, wacc, wr2, wall, left_all,
    work, ybuf, tri, right, orth, sums, squares,
    send_sem, recv_sem,
):
    pc = Place(send_sem, recv_sem)
    c, x, y, z = pc.c, pc.x, pc.y, pc.z
    peers = [pc.partner()]
    peers += [pc.dev(x=pc.xs(d)) for d in (1, 2, 3)]
    peers += [pc.dev(y=pc.ys(d)) for d in (1, 2, 3)]
    peers += [pc.dev(z=pc.zs(d)) for d in range(1, 8)]
    pc.barrier(peers)

    basis_swap = pc.copy(rb.at[1 - c], basis.at[y, x, c], pc.partner())
    basis[y, x, c] = rb[c]
    basis_swap.wait_recv()
    gather = Gather(pc, basis)
    gather.first()
    blend_send[...] = mom[1 - c] + grad[1 - c].astype(F32)
    blend_swap = pc.copy(blend_send, blend.at[c], pc.partner())
    blend[c] = mom[c] + grad[c].astype(F32)
    gather.second()
    at = lax.broadcasted_iota(jnp.int32, (RANK, RANK), 0)
    group, half = at // 128, (at // 64) % 2
    index, low = (at // 16) % 4, at % 16
    py = jnp.where(half == 0, (y + group) % 4, index)
    px = jnp.where(half == 0, index, (x + group) % 4)
    rank = ((py * 4 + px) * 2 + half) * 16 + low
    perm[...] = jnp.where(lax.broadcasted_iota(jnp.int32, (RANK, RANK), 1) == rank, 1.0, 0.0)
    blend_swap.wait_recv()
    sums_in = []
    for d in (0, 3, 1, 2):
        if d:
            received(gather.two[4 - d])
        rows = jnp.concatenate(
            [basis[pc.ys(d), :, 0].reshape(64, 1024), basis[:, pc.xs(d), 1].reshape(64, 1024)], axis=0
        )
        part = dot(blend[...].reshape(512, 1024), rows, 1, 1, HIGH)
        lpart[d] = part.reshape(8, 64, 128)
        for e in (4, 3, 5, 2, 6, 1, 7):
            sums_in.append(pc.copy(lpart.at[d, pc.zs(e)], lrecv.at[e - 1, d], pc.dev(z=pc.zs(e))))
    received(sums_in)
    own = []
    for d in range(4):
        s = lpart[d, z]
        for e in range(7):
            s = s + lrecv[e, d]
        own.append(s)
    own = dot(jnp.concatenate(own, axis=1), perm[...], 1, 0, HIGHEST)
    left[z] = own

    def ring(step):
        up, down = pc.dev(z=pc.zs(1)), pc.dev(z=pc.zs(7))
        a, b = left.at[pc.zs(9 - step)], left.at[pc.zs(step - 1)]
        if step == 4:
            a, b = a.at[pl.ds(0, 32)], b.at[pl.ds(32, 32)]
        return [pc.copy(a, a, up), pc.copy(b, b, down)]

    blocks = []
    for i in range(4):
        row = dot(own[:, 128 * i:128 * i + 128], own[:, :128 * i + 128], 0, 0, HIGHEST)
        blocks += [row[:, 128 * j:128 * j + 128] for j in range(i + 1)]
    gbuf[...] = jnp.concatenate(blocks, axis=0).reshape(4, 4, 2, 40, 128)
    gscatter = Scatter(pc, gbuf, gr1, gacc, gr2)
    gscatter.first()
    lefts = ring(1)
    gscatter.second()
    received(lefts)
    lefts = ring(2)
    own0, own1 = gscatter.finish()
    zbuf[z, 0] = own0
    zbuf[z, 1] = own1
    zs = []
    for d in (4, 3, 5, 2, 6, 1, 7):
        zs.append(pc.copy(zbuf.at[z], zbuf.at[z], pc.dev(z=pc.zs(d))))
    received(lefts)
    lefts = ring(3)
    received(zs)
    total = zbuf[0]
    for d in range(1, 8):
        total = total + zbuf[d]
    gfull[y, x] = total
    ggather = Gather(pc, gfull)
    ggather.first()
    received(lefts)
    lefts = ring(4)
    ggather.second()
    received(lefts)
    for i in range(4):
        lt = left[:, :, 128 * i:128 * i + 128].reshape(RANK, 128)
        part = dot(lt, blend[...].reshape(512, 1024), 0, 0, HIGH)
        wbuf[i] = part.reshape(4, 2, 16, 1024)
    wscatter = Scatter(pc, wbuf, wr1, wacc, wr2)
    wscatter.first()
    left_all[c] = left[pl.ds(4 * c, 4)]
    left_swap = pc.copy(left.at[pl.ds(4 * (1 - c), 4)], left_all.at[c], pc.partner())
    ggather.finish()

    wgather = Gather(pc, wall.at[c])
    w_swaps = []

    def w_second():
        wscatter.second()

    def w_gather():
        o0, o1 = wscatter.finish()
        wall[c, y, x, 0] = o0
        wall[c, y, x, 1] = o1
        wgather.first()

    def w_gather_second():
        wgather.second()
        for a in (wall.at[c, y, :, 0], wall.at[c, :, x, 1]):
            w_swaps.append(pc.copy(a, a, pc.partner()))

    def w_last():
        for d in (1, 3, 2):
            received(wgather.two[d])
            for a in (wall.at[c, pc.ys(4 - d), :, 0], wall.at[c, :, pc.xs(4 - d), 1]):
                w_swaps.append(pc.copy(a, a, pc.partner()))

    events = {(1, 16): w_second, (2, 2): w_gather, (2, 20): w_gather_second}
    flat = gfull[...].reshape(1280, 128)
    for b in range(10):
        work[b] = flat[128 * b:128 * b + 128]
    at = lambda i, j: i * (i + 1) // 2 + j
    yat = lambda i, j: i * (i - 1) // 2 + j
    rowi = lax.broadcasted_iota(jnp.int32, (128, 128), 0)
    coli = lax.broadcasted_iota(jnp.int32, (128, 128), 1)
    tri_swaps = []
    pending = []

    def tri_row(k, inv):
        for j in range(4):
            cols = pl.ds(128 * j, 128)
            if j < k:
                tri[c, pl.ds(128 * k, 128), cols] = dot(inv, ybuf[yat(k, j)], 1, 0, HIGHEST)
            elif j == k:
                tri[c, pl.ds(128 * k, 128), cols] = inv
            else:
                tri[c, pl.ds(128 * k, 128), cols] = jnp.zeros((128, 128), F32)
        a = tri.at[c, pl.ds(128 * k, 128)]
        tri_swaps.append(pc.copy(a, a, pc.partner()))

    def later(k, inv):
        def solve(i):
            work[at(i, k)] = dot(work[at(i, k)], inv, 1, 1, HIGHEST)

        def trail(i, j):
            work[at(i, j)] = work[at(i, j)] - dot(work[at(i, k)], work[at(j, k)], 1, 1, HIGHEST)

        def inverse(i, j):
            new = dot(work[at(i, k)], tri[c, pl.ds(128 * k, 128), pl.ds(128 * j, 128)], 1, 0, HIGHEST)
            ybuf[yat(i, j)] = -new if j == k else ybuf[yat(i, j)] - new

        jobs = [lambda: tri_row(k, inv)]
        for i in range(k + 2, 4):
            jobs.append(lambda i=i: solve(i))
        for i in range(k + 2, 4):
            for j in range(k + 1, i + 1):
                jobs.append(lambda i=i, j=j: trail(i, j))
        for i in range(k + 1, 4):
            for j in range(k + 1):
                jobs.append(lambda i=i, j=j: inverse(i, j))
        return jobs

    for k in range(4):

        def tick(q, k=k):
            if (k, q) in events:
                events[k, q]()
            if pending and q >= 1:
                pending.pop(0)()

        rows = factor_block(lambda r: work[at(k, k), 8 * r:8 * r + 8, :], tick)
        while pending:
            pending.pop(0)()
        inv = jnp.where(rowi >= coli, jnp.concatenate(rows, axis=0), 0.0)
        if k < 3:
            below = dot(work[at(k + 1, k)], inv, 1, 1, HIGHEST)
            work[at(k + 1, k)] = below
            work[at(k + 1, k + 1)] = work[at(k + 1, k + 1)] - dot(below, below, 1, 1, HIGHEST)
            pending = later(k, inv)
        else:
            tri_row(k, inv)
    w_last()

    def raw(m):
        def part(j, carry):
            cols = pl.ds(pl.multiple_of(j * 256, 256), 256)
            wj = wall[m, :, :, :, :, cols].reshape(RANK, 256)
            for i in range(4):
                n = 128 * (i + 1)
                t = tri[m, pl.ds(128 * i, 128), pl.ds(0, n)]
                right[m, pl.ds(128 * i, 128), cols] = dot(t, wj[:n], 1, 0, HIGH)
            return carry

        lax.fori_loop(0, 4, part, 0)
        r = right[m]
        sums[m] = dot(jnp.ones((8, 1024), F32), r * r, 1, 1, HIGHEST)

    raw(c)
    received(w_swaps)
    received(tri_swaps)
    raw(1 - c)
    left_swap.wait_recv()
    pieces = [sums[m, 0:1, 128 * j:128 * j + 128] for m in range(2) for j in range(4)]
    squares[z] = jnp.concatenate(pieces, axis=0)
    zs = []
    for d in (4, 3, 5, 2, 6, 1, 7):
        zs.append(pc.copy(squares.at[z], squares.at[z], pc.dev(z=pc.zs(d))))
    for m in range(2):
        orth[m] = dot(left_all[m].reshape(256, RANK), tri[m], 1, 1, HIGH)

        def feed(j, carry, m=m):
            cols = pl.ds(pl.multiple_of(j * 256, 256), 256)
            back = dot(orth[m], right[m, :, cols], 1, 0, HIGH)
            blended = mom[m, :, cols] + grad[m, :, cols].astype(F32)
            momentum_next[m, :, cols] = blended - (1.0 - momentum_decay) * back
            return carry

        lax.fori_loop(0, 4, feed, 0)
    received(zs)
    total = squares[0]
    for d in range(1, 8):
        total = total + squares[d]
    inverse = lax.rsqrt(total / D + epsilon_sq)
    lane = lax.broadcasted_iota(jnp.int32, (16, RANK), 1)
    sub = lax.broadcasted_iota(jnp.int32, (16, RANK), 0)
    for m in range(2):
        inv = jnp.concatenate([inverse[4 * m + j:4 * m + j + 1] for j in range(4)], axis=1)
        orth[m] = orth[m] * inv
        pick = jnp.where(lane == pc.f * 16 + sub, inv, 0.0)

        def direction(j, carry, m=m, pick=pick):
            cols = pl.ds(pl.multiple_of(j * 256, 256), 256)
            rj = right[m, :, cols]
            out = math.sqrt(D / RANK) * dot(orth[m], rj, 1, 0, HIGH)
            update[m, :, cols] = out.astype(jnp.bfloat16)
            basis_next[m, :, cols] = dot(pick, rj, 1, 0, HIGHEST)
            return carry

        lax.fori_loop(0, 4, direction, 0)
    pc.drain()


def shards(gradient, momentum, right_basis):
    vmem = pl.BlockSpec(memory_space=pltpu.VMEM)
    shape = lambda s: jax.ShapeDtypeStruct(s, F32)
    buf = lambda *s: pltpu.VMEM(s, F32)
    n = 126
    return pl.pallas_call(
        kernel,
        out_shape=(
            jax.ShapeDtypeStruct((2, 256, 1024), jnp.bfloat16), shape((2, 256, 1024)), shape((2, 16, 1024))
        ),
        in_specs=[vmem] * 3,
        out_specs=[vmem] * 3,
        scratch_shapes=[
            buf(2, 256, 1024), buf(256, 1024), buf(4, 4, 2, 16, 1024),
            buf(4, 8, 64, 128), buf(7, 4, 64, 128), buf(8, 64, RANK), buf(RANK, RANK),
            buf(4, 4, 2, 40, 128), buf(2, 3, 4, 40, 128), buf(2, 4, 40, 128), buf(2, 3, 40, 128),
            buf(8, 2, 40, 128), buf(4, 4, 2, 40, 128),
            buf(4, 4, 2, 16, 1024), buf(2, 3, 4, 16, 1024), buf(2, 4, 16, 1024), buf(2, 3, 16, 1024),
            buf(2, 4, 4, 2, 16, 1024), buf(2, 4, 64, RANK),
            buf(10, 128, 128), buf(6, 128, 128), buf(2, RANK, RANK),
            buf(2, RANK, 1024), buf(2, 256, RANK), buf(2, 8, RANK), buf(8, 8, 128),
            pltpu.SemaphoreType.DMA((n,)), pltpu.SemaphoreType.DMA((n,)),
        ],
        compiler_params=pltpu.CompilerParams(
            collective_id=0, has_side_effects=True, vmem_limit_bytes=VMEM_BYTES
        ),
        name="dion",
    )(gradient, momentum, right_basis)


def solution(mesh):
    placed = (P(None, "fsdp", "tp"), P(None, "fsdp", "tp"), P(None, "fsdp", "tp"))
    return jax.shard_map(
        shards,
        mesh=mesh,
        in_specs=placed,
        out_specs=placed,
        check_vma=False,
    )
```

```python
import math

import jax
import jax.numpy as jnp
from jax import lax
from jax.experimental import pallas as pl
from jax.experimental.pallas import tpu as pltpu
from jax.sharding import PartitionSpec as P

D = 8192
RANK = 512
momentum_decay = 0.8
epsilon_sq = 1e-06
MESH = pl.DeviceIdType.MESH
F32 = jnp.float32
HIGH = lax.Precision.HIGH
HIGHEST = lax.Precision.HIGHEST
VMEM_BYTES = 56 * 1024 * 1024


def dot(a, b, ca, cb, precision):
    return lax.dot_general(
        a, b, (((ca,), (cb,)), ((), ())), precision=precision, preferred_element_type=F32
    )


class Place:
    def __init__(self, send_sem, recv_sem):
        f = lax.axis_index("fsdp")
        self.f = f
        self.z = lax.axis_index("tp")
        self.c = lax.rem(f, 2)
        self.x = lax.rem(f // 2, 4)
        self.y = f // 8
        self.send_sem, self.recv_sem = send_sem, recv_sem
        self.count = 0
        self.open = []

    def dev(self, y=None, x=None, z=None, c=None):
        y = self.y if y is None else y
        x = self.x if x is None else x
        c = self.c if c is None else c
        z = self.z if z is None else z
        return ((y * 4 + x) * 2 + c, z)

    def partner(self):
        return self.dev(c=1 - self.c)

    def xs(self, d):
        return lax.rem(self.x + d, 4)

    def ys(self, d):
        return lax.rem(self.y + d, 4)

    def zs(self, d):
        return lax.rem(self.z + d, 8)

    def copy(self, src, dst, to):
        i = self.count
        self.count += 1
        cp = pltpu.make_async_remote_copy(
            src_ref=src,
            dst_ref=dst,
            send_sem=self.send_sem.at[i],
            recv_sem=self.recv_sem.at[i],
            device_id=to,
            device_id_type=MESH,
        )
        cp.start()
        self.open.append(cp)
        return cp

    def barrier(self, peers):
        sem = pltpu.get_barrier_semaphore()
        for p in peers:
            pl.semaphore_signal(sem, inc=1, device_id=p, device_id_type=MESH)
        pl.semaphore_wait(sem, len(peers))

    def drain(self):
        for cp in self.open:
            cp.wait_send()
        self.open = []


def received(copies):
    for cp in copies:
        cp.wait_recv()


class Gather:
    def __init__(self, pc, buf):
        self.pc, self.buf = pc, buf

    def first(self):
        pc, buf = self.pc, self.buf
        self.one = []
        for d in (1, 3, 2):
            a, b = buf.at[pc.y, pc.x, 0], buf.at[pc.y, pc.x, 1]
            self.one.append(pc.copy(a, a, pc.dev(x=pc.xs(d))))
            self.one.append(pc.copy(b, b, pc.dev(y=pc.ys(d))))

    def second(self):
        pc, buf = self.pc, self.buf
        received(self.one)
        self.two = {}
        for d in (1, 3, 2):
            a, b = buf.at[pc.y, :, 0], buf.at[:, pc.x, 1]
            self.two[d] = (pc.copy(a, a, pc.dev(y=pc.ys(d))), pc.copy(b, b, pc.dev(x=pc.xs(d))))

    def finish(self):
        for d in (1, 3, 2):
            received(self.two[d])


class Scatter:
    def __init__(self, pc, buf, r1, acc, r2):
        self.pc, self.buf, self.r1, self.acc, self.r2 = pc, buf, r1, acc, r2

    def first(self):
        pc, buf = self.pc, self.buf
        self.one = []
        for d in (1, 3, 2):
            self.one.append(pc.copy(buf.at[pc.ys(d), :, 0], self.r1.at[0, d - 1], pc.dev(y=pc.ys(d))))
            self.one.append(pc.copy(buf.at[:, pc.xs(d), 1], self.r1.at[1, d - 1], pc.dev(x=pc.xs(d))))

    def second(self):
        pc, buf, r1, acc = self.pc, self.buf, self.r1, self.acc
        received(self.one)
        acc[0] = buf[pc.y, :, 0] + r1[0, 0] + r1[0, 1] + r1[0, 2]
        acc[1] = buf[:, pc.x, 1] + r1[1, 0] + r1[1, 1] + r1[1, 2]
        self.two = []
        for d in (1, 3, 2):
            self.two.append(pc.copy(acc.at[0, pc.xs(d)], self.r2.at[0, d - 1], pc.dev(x=pc.xs(d))))
            self.two.append(pc.copy(acc.at[1, pc.ys(d)], self.r2.at[1, d - 1], pc.dev(y=pc.ys(d))))

    def finish(self):
        pc, acc, r2 = self.pc, self.acc, self.r2
        received(self.two)
        own0 = acc[0, pc.x] + r2[0, 0] + r2[0, 1] + r2[0, 2]
        own1 = acc[1, pc.y] + r2[1, 0] + r2[1, 1] + r2[1, 2]
        return own0, own1


def factor_block(load, tick):
    groups = 16
    a = [load(r) for r in range(groups)]
    lane = lax.broadcasted_iota(jnp.int32, (8, 128), 1)
    sub = lax.broadcasted_iota(jnp.int32, (8, 128), 0)
    out = [None] * groups

    def column(v, j):
        return jnp.broadcast_to(v[:, j:j + 1], (8, 128))

    def recip(v):
        return pl.reciprocal(v, approx=True)

    for q in range(32):
        r0, s0, j0 = q // 2, 4 * (q % 2), 4 * q
        rows = [jnp.broadcast_to(a[r0][s0 + s:s0 + s + 1, :], (8, 128)) for s in range(4)]
        p = {(s, t): column(rows[s], j0 + t) for s in range(4) for t in range(s, 4)}
        inside = (lane >= j0) & (lane < j0 + 4)
        sc = [lax.rsqrt(p[s, s]) for s in range(4)]
        v = [jnp.where(inside, jnp.where(lane == j0 + s, 1.0, 0.0), rows[s]) * sc[s] for s in range(4)]
        r = {(s, t): p[s, t] * (sc[s] * sc[t]) for s in range(4) for t in range(s + 1, 4)}
        l10, l20, l30 = r[0, 1], r[0, 2], r[0, 3]
        u11, u22, u33 = 1.0 - l10 * l10, 1.0 - l20 * l20, 1.0 - l30 * l30
        u12, u13, u23 = r[1, 2] - l10 * l20, r[1, 3] - l10 * l30, r[2, 3] - l20 * l30
        v22, v23, v33 = u11 * u22 - u12 * u12, u11 * u23 - u12 * u13, u11 * u33 - u13 * u13
        w33 = v22 * v33 - v23 * v23
        i1, i2, i3 = recip(u11), recip(v22), recip(w33)
        l21, l31, l32 = u12 * i1, u13 * i1, v23 * i2
        d1, d2, d3 = i1, u11 * i2, (u11 * v22) * i3
        n10, n21, n32 = -l10, -l21, -l32
        n20 = l21 * l10 - l20
        n31 = l32 * l21 - l31
        n30 = l31 * l10 - l30 - l32 * n20
        n = [[None] * 4, [n10], [n20, n21], [n30, n31, n32]]
        m = {}
        e1 = d1 * n10
        e20, e21 = d2 * n20, d2 * n21
        m[0, 0] = (1.0 + e1 * n10 + e20 * n20) + d3 * (n30 * n30)
        m[0, 1] = (e1 + e20 * n21) + d3 * (n30 * n31)
        m[0, 2] = e20 + d3 * (n30 * n32)
        m[0, 3] = d3 * n30
        m[1, 1] = (d1 + e21 * n21) + d3 * (n31 * n31)
        m[1, 2] = e21 + d3 * (n31 * n32)
        m[1, 3] = d3 * n31
        m[2, 2] = d2 + d3 * (n32 * n32)
        m[2, 3] = d3 * n32
        m[3, 3] = d3
        w = []
        for s in range(4):
            t = [m[min(s, t), max(s, t)] * v[t] for t in range(4)]
            w.append(((t[0] + t[1]) + (t[2] + t[3])) * sc[s])
        f = [None, d1 * lax.rsqrt(d1), d2 * lax.rsqrt(d2), d3 * lax.rsqrt(d3)]
        done = [v[0]]
        for s in range(1, 4):
            t = v[s]
            for k in range(s):
                t = t + n[s][k] * v[k]
            done.append(f[s] * t)
        o = done[0]
        for s in range(1, 4):
            o = jnp.where(sub == s0 + s, done[s], o)
        out[r0] = o if s0 == 0 else jnp.where(sub < 4, out[r0], o)
        for g in range(r0 if s0 == 0 else r0 + 1, groups):
            t = [column(a[g], j0 + t) * w[t] for t in range(4)]
            a[g] = jnp.where(inside, 0.0, a[g]) - ((t[0] + t[1]) + (t[2] + t[3]))
        tick(q)
    return out


def kernel(
    grad, mom, rb, update, momentum_next, basis_next,
    blend, blend_send, basis, lpart, lrecv, left, perm,
    gbuf, gr1, gacc, gr2, zbuf, gfull,
    wbuf, wr1, wacc, wr2, wall, left_all,
    work, ybuf, tri, right, orth, sums, squares,
    send_sem, recv_sem,
):
    pc = Place(send_sem, recv_sem)
    c, x, y, z = pc.c, pc.x, pc.y, pc.z
    peers = [pc.partner()]
    peers += [pc.dev(x=pc.xs(d)) for d in (1, 2, 3)]
    peers += [pc.dev(y=pc.ys(d)) for d in (1, 2, 3)]
    peers += [pc.dev(z=pc.zs(d)) for d in range(1, 8)]
    pc.barrier(peers)

    basis_swap = pc.copy(rb.at[1 - c], basis.at[y, x, c], pc.partner())
    basis[y, x, c] = rb[c]
    basis_swap.wait_recv()
    gather = Gather(pc, basis)
    gather.first()
    blend_send[...] = mom[1 - c] + grad[1 - c].astype(F32)
    blend_swap = pc.copy(blend_send, blend.at[c], pc.partner())
    blend[c] = mom[c] + grad[c].astype(F32)
    gather.second()
    at = lax.broadcasted_iota(jnp.int32, (RANK, RANK), 0)
    group, half = at // 128, (at // 64) % 2
    index, low = (at // 16) % 4, at % 16
    py = jnp.where(half == 0, (y + group) % 4, index)
    px = jnp.where(half == 0, index, (x + group) % 4)
    rank = ((py * 4 + px) * 2 + half) * 16 + low
    perm[...] = jnp.where(lax.broadcasted_iota(jnp.int32, (RANK, RANK), 1) == rank, 1.0, 0.0)
    blend_swap.wait_recv()
    sums_in = []
    for d in (0, 3, 1, 2):
        if d:
            received(gather.two[4 - d])
        rows = jnp.concatenate(
            [basis[pc.ys(d), :, 0].reshape(64, 1024), basis[:, pc.xs(d), 1].reshape(64, 1024)], axis=0
        )
        part = dot(blend[...].reshape(512, 1024), rows, 1, 1, HIGH)
        lpart[d] = part.reshape(8, 64, 128)
        for e in (4, 3, 5, 2, 6, 1, 7):
            sums_in.append(pc.copy(lpart.at[d, pc.zs(e)], lrecv.at[e - 1, d], pc.dev(z=pc.zs(e))))
    received(sums_in)
    own = []
    for d in range(4):
        s = lpart[d, z]
        for e in range(7):
            s = s + lrecv[e, d]
        own.append(s)
    own = dot(jnp.concatenate(own, axis=1), perm[...], 1, 0, HIGHEST)
    left[z] = own

    def ring(step):
        up, down = pc.dev(z=pc.zs(1)), pc.dev(z=pc.zs(7))
        a, b = left.at[pc.zs(9 - step)], left.at[pc.zs(step - 1)]
        if step == 4:
            a, b = a.at[pl.ds(0, 32)], b.at[pl.ds(32, 32)]
        return [pc.copy(a, a, up), pc.copy(b, b, down)]

    blocks = []
    for i in range(4):
        row = dot(own[:, 128 * i:128 * i + 128], own[:, :128 * i + 128], 0, 0, HIGHEST)
        blocks += [row[:, 128 * j:128 * j + 128] for j in range(i + 1)]
    gbuf[...] = jnp.concatenate(blocks, axis=0).reshape(4, 4, 2, 40, 128)
    gscatter = Scatter(pc, gbuf, gr1, gacc, gr2)
    gscatter.first()
    lefts = ring(1)
    gscatter.second()
    received(lefts)
    lefts = ring(2)
    own0, own1 = gscatter.finish()
    zbuf[z, 0] = own0
    zbuf[z, 1] = own1
    zs = []
    for d in (4, 3, 5, 2, 6, 1, 7):
        zs.append(pc.copy(zbuf.at[z], zbuf.at[z], pc.dev(z=pc.zs(d))))
    received(lefts)
    lefts = ring(3)
    received(zs)
    total = zbuf[0]
    for d in range(1, 8):
        total = total + zbuf[d]
    gfull[y, x] = total
    ggather = Gather(pc, gfull)
    ggather.first()
    received(lefts)
    lefts = ring(4)
    ggather.second()
    received(lefts)
    for i in range(4):
        lt = left[:, :, 128 * i:128 * i + 128].reshape(RANK, 128)
        part = dot(lt, blend[...].reshape(512, 1024), 0, 0, HIGH)
        wbuf[i] = part.reshape(4, 2, 16, 1024)
    wscatter = Scatter(pc, wbuf, wr1, wacc, wr2)
    wscatter.first()
    left_all[c] = left[pl.ds(4 * c, 4)]
    left_swap = pc.copy(left.at[pl.ds(4 * (1 - c), 4)], left_all.at[c], pc.partner())
    ggather.finish()

    wgather = Gather(pc, wall.at[c])
    w_swaps = []

    def w_second():
        wscatter.second()

    def w_gather():
        o0, o1 = wscatter.finish()
        wall[c, y, x, 0] = o0
        wall[c, y, x, 1] = o1
        wgather.first()

    def w_gather_second():
        wgather.second()
        for a in (wall.at[c, y, :, 0], wall.at[c, :, x, 1]):
            w_swaps.append(pc.copy(a, a, pc.partner()))

    def w_last():
        for d in (1, 3, 2):
            received(wgather.two[d])
            for a in (wall.at[c, pc.ys(4 - d), :, 0], wall.at[c, :, pc.xs(4 - d), 1]):
                w_swaps.append(pc.copy(a, a, pc.partner()))

    events = {(1, 24): w_second, (2, 12): w_gather, (2, 30): w_gather_second}
    flat = gfull[...].reshape(1280, 128)
    for b in range(10):
        work[b] = flat[128 * b:128 * b + 128]
    at = lambda i, j: i * (i + 1) // 2 + j
    yat = lambda i, j: i * (i - 1) // 2 + j
    rowi = lax.broadcasted_iota(jnp.int32, (128, 128), 0)
    coli = lax.broadcasted_iota(jnp.int32, (128, 128), 1)
    tri_swaps = []
    pending = []

    def tri_row(k, inv):
        for j in range(4):
            cols = pl.ds(128 * j, 128)
            if j < k:
                tri[c, pl.ds(128 * k, 128), cols] = dot(inv, ybuf[yat(k, j)], 1, 0, HIGHEST)
            elif j == k:
                tri[c, pl.ds(128 * k, 128), cols] = inv
            else:
                tri[c, pl.ds(128 * k, 128), cols] = jnp.zeros((128, 128), F32)
        a = tri.at[c, pl.ds(128 * k, 128)]
        tri_swaps.append(pc.copy(a, a, pc.partner()))

    def later(k, inv):
        def solve(i):
            work[at(i, k)] = dot(work[at(i, k)], inv, 1, 1, HIGHEST)

        def trail(i, j):
            work[at(i, j)] = work[at(i, j)] - dot(work[at(i, k)], work[at(j, k)], 1, 1, HIGHEST)

        def inverse(i, j):
            new = dot(work[at(i, k)], tri[c, pl.ds(128 * k, 128), pl.ds(128 * j, 128)], 1, 0, HIGHEST)
            ybuf[yat(i, j)] = -new if j == k else ybuf[yat(i, j)] - new

        jobs = [lambda: tri_row(k, inv)]
        for i in range(k + 2, 4):
            jobs.append(lambda i=i: solve(i))
        for i in range(k + 2, 4):
            for j in range(k + 1, i + 1):
                jobs.append(lambda i=i, j=j: trail(i, j))
        for i in range(k + 1, 4):
            for j in range(k + 1):
                jobs.append(lambda i=i, j=j: inverse(i, j))
        return jobs

    for k in range(4):

        def tick(q, k=k):
            if (k, q) in events:
                events[k, q]()
            if pending and q >= 1:
                pending.pop(0)()

        rows = factor_block(lambda r: work[at(k, k), 8 * r:8 * r + 8, :], tick)
        while pending:
            pending.pop(0)()
        inv = jnp.where(rowi >= coli, jnp.concatenate(rows, axis=0), 0.0)
        if k < 3:
            below = dot(work[at(k + 1, k)], inv, 1, 1, HIGHEST)
            work[at(k + 1, k)] = below
            work[at(k + 1, k + 1)] = work[at(k + 1, k + 1)] - dot(below, below, 1, 1, HIGHEST)
            pending = later(k, inv)
        else:
            tri_row(k, inv)
    w_last()

    def raw(m):
        def part(j, carry):
            cols = pl.ds(pl.multiple_of(j * 256, 256), 256)
            wj = wall[m, :, :, :, :, cols].reshape(RANK, 256)
            for i in range(4):
                n = 128 * (i + 1)
                t = tri[m, pl.ds(128 * i, 128), pl.ds(0, n)]
                right[m, pl.ds(128 * i, 128), cols] = dot(t, wj[:n], 1, 0, HIGH)
            return carry

        lax.fori_loop(0, 4, part, 0)
        fold = right[m, :, 0:128] * right[m, :, 0:128]
        for j in range(1, 8):
            fold = fold + right[m, :, 128 * j:128 * j + 128] * right[m, :, 128 * j:128 * j + 128]
        sums[m] = dot(jnp.ones((8, 128), F32), fold, 1, 1, HIGHEST)

    raw(c)
    received(w_swaps)
    received(tri_swaps)
    raw(1 - c)
    left_swap.wait_recv()
    pieces = [sums[m, 0:1, 128 * j:128 * j + 128] for m in range(2) for j in range(4)]
    squares[z] = jnp.concatenate(pieces, axis=0)
    zs = []
    for d in (4, 3, 5, 2, 6, 1, 7):
        zs.append(pc.copy(squares.at[z], squares.at[z], pc.dev(z=pc.zs(d))))
    for m in range(2):
        orth[m] = dot(left_all[m].reshape(256, RANK), tri[m], 1, 1, HIGH)

        def feed(j, carry, m=m):
            cols = pl.ds(pl.multiple_of(j * 256, 256), 256)
            back = dot(orth[m], right[m, :, cols], 1, 0, HIGH)
            blended = mom[m, :, cols] + grad[m, :, cols].astype(F32)
            momentum_next[m, :, cols] = blended - (1.0 - momentum_decay) * back
            return carry

        lax.fori_loop(0, 4, feed, 0)
    received(zs)
    total = squares[0]
    for d in range(1, 8):
        total = total + squares[d]
    inverse = lax.rsqrt(total / D + epsilon_sq)
    lane = lax.broadcasted_iota(jnp.int32, (16, RANK), 1)
    sub = lax.broadcasted_iota(jnp.int32, (16, RANK), 0)
    for m in range(2):
        inv = jnp.concatenate([inverse[4 * m + j:4 * m + j + 1] for j in range(4)], axis=1)
        orth[m] = orth[m] * inv
        pick = jnp.sum(jnp.where(lane == pc.f * 16 + sub, inv, 0.0), axis=1, keepdims=True)
        basis_next[m] = right[m, pl.ds(pl.multiple_of(pc.f * 16, 16), 16), :] * pick

        def direction(j, carry, m=m):
            cols = pl.ds(pl.multiple_of(j * 256, 256), 256)
            rj = right[m, :, cols]
            out = math.sqrt(D / RANK) * dot(orth[m], rj, 1, 0, HIGH)
            update[m, :, cols] = out.astype(jnp.bfloat16)
            return carry

        lax.fori_loop(0, 4, direction, 0)
    pc.drain()


def place_kernel(update, momentum_next, basis_next, update_out, momentum_out, basis_out, sem):
    pairs = [(basis_next.at[m], basis_out.at[m]) for m in range(2)]
    for m in range(2):
        for i in range(2):
            rows = pl.ds(128 * i, 128)
            pairs.append((momentum_next.at[m, rows], momentum_out.at[m, rows]))
            pairs.append((update.at[m, rows], update_out.at[m, rows]))
    copies = [pltpu.make_async_copy(a, b, sem.at[i]) for i, (a, b) in enumerate(pairs)]
    for cp in copies:
        cp.start()
    for cp in copies:
        cp.wait()


def shards(gradient, momentum, right_basis):
    vmem = pl.BlockSpec(memory_space=pltpu.VMEM)
    shape = lambda s: jax.ShapeDtypeStruct(s, F32)
    buf = lambda *s: pltpu.VMEM(s, F32)
    n = 126
    results = pl.pallas_call(
        kernel,
        out_shape=(
            jax.ShapeDtypeStruct((2, 256, 1024), jnp.bfloat16), shape((2, 256, 1024)), shape((2, 16, 1024))
        ),
        in_specs=[vmem] * 3,
        out_specs=[vmem] * 3,
        scratch_shapes=[
            buf(2, 256, 1024), buf(256, 1024), buf(4, 4, 2, 16, 1024),
            buf(4, 8, 64, 128), buf(7, 4, 64, 128), buf(8, 64, RANK), buf(RANK, RANK),
            buf(4, 4, 2, 40, 128), buf(2, 3, 4, 40, 128), buf(2, 4, 40, 128), buf(2, 3, 40, 128),
            buf(8, 2, 40, 128), buf(4, 4, 2, 40, 128),
            buf(4, 4, 2, 16, 1024), buf(2, 3, 4, 16, 1024), buf(2, 4, 16, 1024), buf(2, 3, 16, 1024),
            buf(2, 4, 4, 2, 16, 1024), buf(2, 4, 64, RANK),
            buf(10, 128, 128), buf(6, 128, 128), buf(2, RANK, RANK),
            buf(2, RANK, 1024), buf(2, 256, RANK), buf(2, 8, RANK), buf(8, 8, 128),
            pltpu.SemaphoreType.DMA((n,)), pltpu.SemaphoreType.DMA((n,)),
        ],
        compiler_params=pltpu.CompilerParams(
            collective_id=0, has_side_effects=True, vmem_limit_bytes=VMEM_BYTES
        ),
        name="dion",
    )(gradient, momentum, right_basis)
    anywhere = pl.BlockSpec(memory_space=pl.ANY)
    return pl.pallas_call(
        place_kernel,
        out_shape=tuple(jax.ShapeDtypeStruct(r.shape, r.dtype) for r in results),
        in_specs=[anywhere] * 3,
        out_specs=[anywhere] * 3,
        scratch_shapes=[pltpu.SemaphoreType.DMA((10,))],
        compiler_params=pltpu.CompilerParams(has_side_effects=True),
        name="place",
    )(*results)


def solution(mesh):
    placed = (P(None, "fsdp", "tp"), P(None, "fsdp", "tp"), P(None, "fsdp", "tp"))
    return jax.shard_map(
        shards,
        mesh=mesh,
        in_specs=placed,
        out_specs=placed,
        check_vma=False,
    )
```

```python
import math

import jax
import jax.numpy as jnp
from jax import lax
from jax.experimental import pallas as pl
from jax.experimental.pallas import tpu as pltpu
from jax.sharding import PartitionSpec as P

D = 8192
RANK = 512
momentum_decay = 0.8
epsilon_sq = 1e-06
MESH = pl.DeviceIdType.MESH
F32 = jnp.float32
HIGH = lax.Precision.HIGH
HIGHEST = lax.Precision.HIGHEST
VMEM_BYTES = 56 * 1024 * 1024


def dot(a, b, ca, cb, precision):
    return lax.dot_general(
        a, b, (((ca,), (cb,)), ((), ())), precision=precision, preferred_element_type=F32
    )


class Place:
    def __init__(self, send_sem, recv_sem):
        f = lax.axis_index("fsdp")
        self.f = f
        self.z = lax.axis_index("tp")
        self.c = lax.rem(f, 2)
        self.x = lax.rem(f // 2, 4)
        self.y = f // 8
        self.send_sem, self.recv_sem = send_sem, recv_sem
        self.count = 0
        self.open = []

    def dev(self, y=None, x=None, z=None, c=None):
        y = self.y if y is None else y
        x = self.x if x is None else x
        c = self.c if c is None else c
        z = self.z if z is None else z
        return ((y * 4 + x) * 2 + c, z)

    def partner(self):
        return self.dev(c=1 - self.c)

    def xs(self, d):
        return lax.rem(self.x + d, 4)

    def ys(self, d):
        return lax.rem(self.y + d, 4)

    def zs(self, d):
        return lax.rem(self.z + d, 8)

    def reserve(self, n):
        i = self.count
        self.count += n
        assert self.count <= self.send_sem.shape[0]
        return i

    def copy(self, src, dst, to, recv=None):
        i = self.reserve(1)
        cp = pltpu.make_async_remote_copy(
            src_ref=src,
            dst_ref=dst,
            send_sem=self.send_sem.at[i],
            recv_sem=self.recv_sem.at[i if recv is None else recv],
            device_id=to,
            device_id_type=MESH,
        )
        cp.start()
        self.open.append(cp)
        return cp

    def barrier(self, peers):
        sem = pltpu.get_barrier_semaphore()
        for p in peers:
            pl.semaphore_signal(sem, inc=1, device_id=p, device_id_type=MESH)
        pl.semaphore_wait(sem, len(peers))

    def drain(self):
        for cp in self.open:
            cp.wait_send()
        self.open = []


def received(copies):
    for cp in copies:
        cp.wait_recv()


class Gather:
    def __init__(self, pc, buf):
        self.pc, self.buf = pc, buf

    def first(self):
        pc, buf = self.pc, self.buf
        self.one = []
        for d in (1, 3, 2):
            a, b = buf.at[pc.y, pc.x, 0], buf.at[pc.y, pc.x, 1]
            self.one.append(pc.copy(a, a, pc.dev(x=pc.xs(d))))
            self.one.append(pc.copy(b, b, pc.dev(y=pc.ys(d))))

    def second(self):
        pc, buf = self.pc, self.buf
        received(self.one)
        self.two = {}
        for d in (1, 3, 2):
            a, b = buf.at[pc.y, :, 0], buf.at[:, pc.x, 1]
            self.two[d] = (pc.copy(a, a, pc.dev(y=pc.ys(d))), pc.copy(b, b, pc.dev(x=pc.xs(d))))

    def finish(self):
        for d in (1, 3, 2):
            received(self.two[d])


class Scatter:
    def __init__(self, pc, buf, r1, acc, r2):
        self.pc, self.buf, self.r1, self.acc, self.r2 = pc, buf, r1, acc, r2

    def first(self):
        pc, buf = self.pc, self.buf
        self.one = []
        for d in (1, 3, 2):
            self.one.append(pc.copy(buf.at[pc.ys(d), :, 0], self.r1.at[0, d - 1], pc.dev(y=pc.ys(d))))
            self.one.append(pc.copy(buf.at[:, pc.xs(d), 1], self.r1.at[1, d - 1], pc.dev(x=pc.xs(d))))

    def second(self):
        pc, buf, r1, acc = self.pc, self.buf, self.r1, self.acc
        received(self.one)
        acc[0] = buf[pc.y, :, 0] + r1[0, 0] + r1[0, 1] + r1[0, 2]
        acc[1] = buf[:, pc.x, 1] + r1[1, 0] + r1[1, 1] + r1[1, 2]
        self.two = []
        for d in (1, 3, 2):
            self.two.append(pc.copy(acc.at[0, pc.xs(d)], self.r2.at[0, d - 1], pc.dev(x=pc.xs(d))))
            self.two.append(pc.copy(acc.at[1, pc.ys(d)], self.r2.at[1, d - 1], pc.dev(y=pc.ys(d))))

    def finish(self):
        pc, acc, r2 = self.pc, self.acc, self.r2
        received(self.two)
        own0 = acc[0, pc.x] + r2[0, 0] + r2[0, 1] + r2[0, 2]
        own1 = acc[1, pc.y] + r2[1, 0] + r2[1, 1] + r2[1, 2]
        return own0, own1


def factor_block(load, tick):
    groups = 16
    a = [load(r) for r in range(groups)]
    lane = lax.broadcasted_iota(jnp.int32, (8, 128), 1)
    sub = lax.broadcasted_iota(jnp.int32, (8, 128), 0)
    out = [None] * groups

    def column(v, j):
        return jnp.broadcast_to(v[:, j:j + 1], (8, 128))

    def recip(v):
        return pl.reciprocal(v, approx=True)

    for q in range(32):
        r0, s0, j0 = q // 2, 4 * (q % 2), 4 * q
        rows = [jnp.broadcast_to(a[r0][s0 + s:s0 + s + 1, :], (8, 128)) for s in range(4)]
        p = {(s, t): column(rows[s], j0 + t) for s in range(4) for t in range(s, 4)}
        inside = (lane >= j0) & (lane < j0 + 4)
        sc = [lax.rsqrt(p[s, s]) for s in range(4)]
        v = [jnp.where(inside, jnp.where(lane == j0 + s, 1.0, 0.0), rows[s]) * sc[s] for s in range(4)]
        r = {(s, t): p[s, t] * (sc[s] * sc[t]) for s in range(4) for t in range(s + 1, 4)}
        l10, l20, l30 = r[0, 1], r[0, 2], r[0, 3]
        u11, u22, u33 = 1.0 - l10 * l10, 1.0 - l20 * l20, 1.0 - l30 * l30
        u12, u13, u23 = r[1, 2] - l10 * l20, r[1, 3] - l10 * l30, r[2, 3] - l20 * l30
        v22, v23, v33 = u11 * u22 - u12 * u12, u11 * u23 - u12 * u13, u11 * u33 - u13 * u13
        w33 = v22 * v33 - v23 * v23
        i1, i2, i3 = recip(u11), recip(v22), recip(w33)
        l21, l31, l32 = u12 * i1, u13 * i1, v23 * i2
        d1, d2, d3 = i1, u11 * i2, (u11 * v22) * i3
        n10, n21, n32 = -l10, -l21, -l32
        n20 = l21 * l10 - l20
        n31 = l32 * l21 - l31
        n30 = l31 * l10 - l30 - l32 * n20
        n = [[None] * 4, [n10], [n20, n21], [n30, n31, n32]]
        m = {}
        e1 = d1 * n10
        e20, e21 = d2 * n20, d2 * n21
        m[0, 0] = (1.0 + e1 * n10 + e20 * n20) + d3 * (n30 * n30)
        m[0, 1] = (e1 + e20 * n21) + d3 * (n30 * n31)
        m[0, 2] = e20 + d3 * (n30 * n32)
        m[0, 3] = d3 * n30
        m[1, 1] = (d1 + e21 * n21) + d3 * (n31 * n31)
        m[1, 2] = e21 + d3 * (n31 * n32)
        m[1, 3] = d3 * n31
        m[2, 2] = d2 + d3 * (n32 * n32)
        m[2, 3] = d3 * n32
        m[3, 3] = d3
        w = []
        for s in range(4):
            t = [m[min(s, t), max(s, t)] * v[t] for t in range(4)]
            w.append(((t[0] + t[1]) + (t[2] + t[3])) * sc[s])
        f = [None, d1 * lax.rsqrt(d1), d2 * lax.rsqrt(d2), d3 * lax.rsqrt(d3)]
        done = [v[0]]
        for s in range(1, 4):
            t = v[s]
            for k in range(s):
                t = t + n[s][k] * v[k]
            done.append(f[s] * t)
        o = done[0]
        for s in range(1, 4):
            o = jnp.where(sub == s0 + s, done[s], o)
        out[r0] = o if s0 == 0 else jnp.where(sub < 4, out[r0], o)
        for g in range(r0 if s0 == 0 else r0 + 1, groups):
            t = [column(a[g], j0 + t) * w[t] for t in range(4)]
            a[g] = jnp.where(inside, 0.0, a[g]) - ((t[0] + t[1]) + (t[2] + t[3]))
        tick(q)
    return out


def kernel(
    grad, mom, rb, update, momentum_next, basis_next,
    gv, mv, upd, bnext, blend, blend_send, basis, lpart, lrecv, left, perm,
    gbuf, gr1, gacc, gr2, zsrc, zpart, zfull, gfull,
    wbuf, wr1, wacc, wr2, wall, left_all,
    work, ybuf, tri, right, orth, sums, squares,
    send_sem, recv_sem, local_sem,
):
    pc = Place(send_sem, recv_sem)
    c, x, y, z = pc.c, pc.x, pc.y, pc.z
    loads = []
    for i, m in enumerate((1 - c, c)):
        loads.append(
            (
                pltpu.make_async_copy(mom.at[m], mv.at[m], local_sem.at[2 * i]),
                pltpu.make_async_copy(grad.at[m], gv.at[m], local_sem.at[2 * i + 1]),
            )
        )
        for cp in loads[i]:
            cp.start()
    peers = [pc.partner()]
    peers += [pc.dev(x=pc.xs(d), c=m) for d in (1, 2, 3) for m in (0, 1)]
    peers += [pc.dev(y=pc.ys(d), c=m) for d in (1, 2, 3) for m in (0, 1)]
    peers += [pc.dev(z=pc.zs(d)) for d in range(1, 8)]
    pc.barrier(peers)

    first = pc.reserve(6)
    slot = lambda d, h: first + 2 * (d - 1) + h
    for d in (1, 3, 2):
        to_y, to_x = lax.rem(y + d * c, 4), lax.rem(x + d * (1 - c), 4)
        for m in range(2):
            pc.copy(rb.at[m], basis.at[y, x, c], pc.dev(y=to_y, x=to_x, c=m), recv=slot(d, c))
    basis_swap = pc.copy(rb.at[1 - c], basis.at[y, x, c], pc.partner())
    basis[y, x, c] = rb[c]
    for cp in loads[0]:
        cp.wait()
    blend_send[...] = mv[1 - c] + gv[1 - c].astype(F32)
    blend_swap = pc.copy(blend_send, blend.at[c], pc.partner())
    for cp in loads[1]:
        cp.wait()
    blend[c] = mv[c] + gv[c].astype(F32)
    basis_swap.wait_recv()
    for d in (1, 3, 2):
        for h in range(2):
            pltpu.make_async_remote_copy(
                src_ref=rb.at[0],
                dst_ref=basis.at[y, x, h],
                send_sem=send_sem.at[slot(d, h)],
                recv_sem=recv_sem.at[slot(d, h)],
                device_id=pc.partner(),
                device_id_type=MESH,
            ).wait_recv()
    gather = Gather(pc, basis)
    gather.one = []
    gather.second()
    at = lax.broadcasted_iota(jnp.int32, (RANK, RANK), 0)
    group, half = at // 128, (at // 64) % 2
    index, low = (at // 16) % 4, at % 16
    py = jnp.where(half == 0, (y + group) % 4, index)
    px = jnp.where(half == 0, index, (x + group) % 4)
    rank = ((py * 4 + px) * 2 + half) * 16 + low
    perm[...] = jnp.where(lax.broadcasted_iota(jnp.int32, (RANK, RANK), 1) == rank, 1.0, 0.0)
    blend_swap.wait_recv()
    sums_in = []
    for d in (0, 3, 1, 2):
        if d:
            received(gather.two[4 - d])
        rows = jnp.concatenate(
            [basis[pc.ys(d), :, 0].reshape(64, 1024), basis[:, pc.xs(d), 1].reshape(64, 1024)], axis=0
        )
        part = dot(blend[...].reshape(512, 1024), rows, 1, 1, HIGH)
        lpart[d] = part.reshape(8, 64, 128)
        for e in (4, 3, 5, 2, 6, 1, 7):
            sums_in.append(pc.copy(lpart.at[d, pc.zs(e)], lrecv.at[e - 1, d], pc.dev(z=pc.zs(e))))
    received(sums_in)
    own = []
    for d in range(4):
        s = lpart[d, z]
        for e in range(7):
            s = s + lrecv[e, d]
        own.append(s)
    own = dot(jnp.concatenate(own, axis=1), perm[...], 1, 0, HIGHEST)
    for q in range(2):
        left[q, z] = own[:, 256 * q:256 * q + 256]

    def ring(step):
        up, down = pc.dev(z=pc.zs(1)), pc.dev(z=pc.zs(7))
        copies = []
        for q in range(2):
            a, b = left.at[q, pc.zs(9 - step)], left.at[q, pc.zs(step - 1)]
            if step == 4:
                a, b = a.at[pl.ds(0, 32)], b.at[pl.ds(32, 32)]
            copies += [pc.copy(a, a, up), pc.copy(b, b, down)]
        return copies

    blocks = []
    for i in range(4):
        row = dot(own[:, 128 * i:128 * i + 128], own[:, :128 * i + 128], 0, 0, HIGHEST)
        blocks += [row[:, 128 * j:128 * j + 128] for j in range(i + 1)]
    gbuf[...] = jnp.concatenate(blocks, axis=0).reshape(4, 4, 2, 40, 128)
    gscatter = Scatter(pc, gbuf, gr1, gacc, gr2)
    gscatter.first()
    lefts = ring(1)
    gscatter.second()
    received(lefts)
    lefts = ring(2)
    own0, own1 = gscatter.finish()
    zsrc[0:5] = jnp.concatenate([own0, own1], axis=0).reshape(5, 16, 128)
    zsrc[5:8] = jnp.zeros((3, 16, 128), F32)
    zs = []
    for d in (4, 3, 5, 2, 6, 1, 7):
        zs.append(pc.copy(zsrc.at[pc.zs(d)], zpart.at[d - 1], pc.dev(z=pc.zs(d))))
    received(lefts)
    lefts = ring(3)
    received(zs)
    total = zsrc[z]
    for d in range(7):
        total = total + zpart[d]
    zfull[z] = total
    zs = []
    for d in (4, 3, 5, 2, 6, 1, 7):
        zs.append(pc.copy(zfull.at[z], zfull.at[z], pc.dev(z=pc.zs(d))))
    received(lefts)
    lefts = ring(4)
    received(zs)
    gfull[y, x] = zfull[0:5].reshape(2, 40, 128)
    ggather = Gather(pc, gfull)
    ggather.first()
    received(lefts)
    ggather.second()
    wscatter, wgather = [], []
    for q in range(2):
        for i in range(2):
            lt = left[q, :, :, 128 * i:128 * i + 128].reshape(RANK, 128)
            part = dot(lt, blend[...].reshape(512, 1024), 0, 0, HIGH)
            wbuf[q, 2 * i:2 * i + 2] = part.reshape(2, 4, 2, 8, 1024)
        wscatter.append(Scatter(pc, wbuf.at[q], wr1.at[q], wacc.at[q], wr2.at[q]))
        wscatter[q].first()
        wgather.append(Gather(pc, wall.at[c, q]))
    left_all[c] = left[:, pl.ds(4 * c, 4)]
    left_swap = pc.copy(left.at[:, pl.ds(4 * (1 - c), 4)], left_all.at[c], pc.partner())
    ggather.finish()

    w_swaps = ([], [])

    def w_gather(q):
        o0, o1 = wscatter[q].finish()
        wall[c, q, y, x, 0] = o0
        wall[c, q, y, x, 1] = o1
        wgather[q].first()

    def w_gather_second(q):
        wgather[q].second()
        for a in (wall.at[c, q, y, :, 0], wall.at[c, q, :, x, 1]):
            w_swaps[q].append(pc.copy(a, a, pc.partner()))

    def w_last(q):
        for d in (1, 3, 2):
            received(wgather[q].two[d])
            for a in (wall.at[c, q, pc.ys(4 - d), :, 0], wall.at[c, q, :, pc.xs(4 - d), 1]):
                w_swaps[q].append(pc.copy(a, a, pc.partner()))

    def w_step1():
        wscatter[0].second()

    def w_step2():
        wscatter[1].second()
        w_gather(0)

    def w_step3():
        w_gather(1)
        w_gather_second(0)

    def w_step4():
        w_gather_second(1)

    events = {(1, 2): w_step1, (1, 28): w_step2, (2, 10): w_step3, (2, 26): w_step4}
    flat = gfull[...].reshape(1280, 128)
    for b in range(10):
        work[b] = flat[128 * b:128 * b + 128]
    at = lambda i, j: i * (i + 1) // 2 + j
    yat = lambda i, j: i * (i - 1) // 2 + j
    rowi = lax.broadcasted_iota(jnp.int32, (128, 128), 0)
    coli = lax.broadcasted_iota(jnp.int32, (128, 128), 1)
    tri_swaps = []
    pending = []

    def tri_row(k, inv):
        for j in range(4):
            cols = pl.ds(128 * j, 128)
            if j < k:
                tri[c, pl.ds(128 * k, 128), cols] = dot(inv, ybuf[yat(k, j)], 1, 0, HIGHEST)
            elif j == k:
                tri[c, pl.ds(128 * k, 128), cols] = inv
            else:
                tri[c, pl.ds(128 * k, 128), cols] = jnp.zeros((128, 128), F32)
        a = tri.at[c, pl.ds(128 * k, 128)]
        tri_swaps.append(pc.copy(a, a, pc.partner()))

    def later(k, inv):
        def solve(i):
            work[at(i, k)] = dot(work[at(i, k)], inv, 1, 1, HIGHEST)

        def trail(i, j):
            work[at(i, j)] = work[at(i, j)] - dot(work[at(i, k)], work[at(j, k)], 1, 1, HIGHEST)

        def inverse(i, j):
            new = dot(work[at(i, k)], tri[c, pl.ds(128 * k, 128), pl.ds(128 * j, 128)], 1, 0, HIGHEST)
            ybuf[yat(i, j)] = -new if j == k else ybuf[yat(i, j)] - new

        jobs = [lambda: tri_row(k, inv)]
        for i in range(k + 2, 4):
            jobs.append(lambda i=i: solve(i))
        for i in range(k + 2, 4):
            for j in range(k + 1, i + 1):
                jobs.append(lambda i=i, j=j: trail(i, j))
        for i in range(k + 1, 4):
            for j in range(k + 1):
                jobs.append(lambda i=i, j=j: inverse(i, j))
        return jobs

    for k in range(4):

        def tick(q, k=k):
            if (k, q) in events:
                events[k, q]()
            if pending and q >= 1:
                pending.pop(0)()

        rows = factor_block(lambda r: work[at(k, k), 8 * r:8 * r + 8, :], tick)
        while pending:
            pending.pop(0)()
        inv = jnp.where(rowi >= coli, jnp.concatenate(rows, axis=0), 0.0)
        if k < 3:
            below = dot(work[at(k + 1, k)], inv, 1, 1, HIGHEST)
            work[at(k + 1, k)] = below
            work[at(k + 1, k + 1)] = work[at(k + 1, k + 1)] - dot(below, below, 1, 1, HIGHEST)
            pending = later(k, inv)
        else:
            tri_row(k, inv)

    def raw(m, q):
        def part(j, carry):
            cols = pl.ds(pl.multiple_of(j * 256, 256), 256)
            wj = wall[m, q, :, :, :, :, cols].reshape(256, 256)
            t = tri[m, pl.ds(256 * q, 512 - 256 * q), pl.ds(256 * q, 256)]
            new = dot(t, wj, 1, 0, HIGH)
            if q == 0:
                right[m, :, cols] = new
            else:
                right[m, 256:, cols] = right[m, 256:, cols] + new
            return carry

        lax.fori_loop(0, 4, part, 0)

    def squares_of(m):
        fold = right[m, :, 0:128] * right[m, :, 0:128]
        for j in range(1, 8):
            fold = fold + right[m, :, 128 * j:128 * j + 128] * right[m, :, 128 * j:128 * j + 128]
        sums[m] = dot(jnp.ones((8, 128), F32), fold, 1, 1, HIGHEST)

    w_last(0)
    raw(c, 0)
    w_last(1)
    raw(c, 1)
    squares_of(c)
    received(tri_swaps)
    received(w_swaps[0])
    raw(1 - c, 0)
    received(w_swaps[1])
    raw(1 - c, 1)
    squares_of(1 - c)
    left_swap.wait_recv()
    pieces = [sums[m, 0:1, 128 * j:128 * j + 128] for m in range(2) for j in range(4)]
    squares[z] = jnp.concatenate(pieces, axis=0)
    zs = []
    for d in (4, 3, 5, 2, 6, 1, 7):
        zs.append(pc.copy(squares.at[z], squares.at[z], pc.dev(z=pc.zs(d))))
    stores = []

    def store(src, dst):
        cp = pltpu.make_async_copy(src, dst, local_sem.at[4 + len(stores)])
        cp.start()
        stores.append(cp)

    for m in range(2):
        rows = jnp.concatenate([left_all[m, q].reshape(256, 256) for q in range(2)], axis=1)
        orth[m] = dot(rows, tri[m], 1, 1, HIGH)

        def feed(j, carry, m=m):
            cols = pl.ds(pl.multiple_of(j * 256, 256), 256)
            back = dot(orth[m], right[m, :, cols], 1, 0, HIGH)
            blended = mv[m, :, cols] + gv[m, :, cols].astype(F32)
            mv[m, :, cols] = blended - (1.0 - momentum_decay) * back
            return carry

        lax.fori_loop(0, 4, feed, 0)
        store(mv.at[m], momentum_next.at[m])
    received(zs)
    total = squares[0]
    for d in range(1, 8):
        total = total + squares[d]
    inverse = lax.rsqrt(total / D + epsilon_sq)
    lane = lax.broadcasted_iota(jnp.int32, (16, RANK), 1)
    sub = lax.broadcasted_iota(jnp.int32, (16, RANK), 0)
    for m in range(2):
        inv = jnp.concatenate([inverse[4 * m + j:4 * m + j + 1] for j in range(4)], axis=1)
        orth[m] = orth[m] * inv
        pick = jnp.sum(jnp.where(lane == pc.f * 16 + sub, inv, 0.0), axis=1, keepdims=True)
        bnext[m] = right[m, pl.ds(pl.multiple_of(pc.f * 16, 16), 16), :] * pick
        store(bnext.at[m], basis_next.at[m])

        def direction(j, carry, m=m):
            cols = pl.ds(pl.multiple_of(j * 256, 256), 256)
            out = math.sqrt(D / RANK) * dot(orth[m], right[m, :, cols], 1, 0, HIGH)
            upd[m, :, cols] = out.astype(jnp.bfloat16)
            return carry

        lax.fori_loop(0, 4, direction, 0)
        store(upd.at[m], update.at[m])
    for cp in stores:
        cp.wait()
    pc.drain()


def place_kernel(update, momentum_next, basis_next, update_out, momentum_out, basis_out, uv, mv, bv, sem):
    parts = [(basis_next, bv, basis_out, pl.ds(0, 16))]
    for i in range(2):
        parts.append((momentum_next, mv, momentum_out, pl.ds(128 * i, 128)))
        parts.append((update, uv, update_out, pl.ds(128 * i, 128)))
    loads, stores = [], []
    for m in range(2):
        for src, held, dst, rows in parts:
            i = len(loads)
            loads.append(pltpu.make_async_copy(src.at[m, rows], held.at[m, rows], sem.at[2 * i]))
            stores.append(pltpu.make_async_copy(held.at[m, rows], dst.at[m, rows], sem.at[2 * i + 1]))
    for cp in loads:
        cp.start()
    for a, b in zip(loads, stores):
        a.wait()
        b.start()
    for cp in stores:
        cp.wait()


def shards(gradient, momentum, right_basis):
    vmem = pl.BlockSpec(memory_space=pltpu.VMEM)
    anywhere = pl.BlockSpec(memory_space=pl.ANY)
    shape = lambda s: jax.ShapeDtypeStruct(s, F32)
    buf = lambda *s: pltpu.VMEM(s, F32)
    half = pltpu.VMEM((2, 256, 1024), jnp.bfloat16)
    out_shape = (jax.ShapeDtypeStruct((2, 256, 1024), jnp.bfloat16), shape((2, 256, 1024)), shape((2, 16, 1024)))
    n = 200
    results = pl.pallas_call(
        kernel,
        out_shape=out_shape,
        in_specs=[anywhere, anywhere, vmem],
        out_specs=[anywhere] * 3,
        scratch_shapes=[
            half, buf(2, 256, 1024), half, buf(2, 16, 1024),
            buf(2, 256, 1024), buf(256, 1024), buf(4, 4, 2, 16, 1024),
            buf(4, 8, 64, 128), buf(7, 4, 64, 128), buf(2, 8, 64, 256), buf(RANK, RANK),
            buf(4, 4, 2, 40, 128), buf(2, 3, 4, 40, 128), buf(2, 4, 40, 128), buf(2, 3, 40, 128),
            buf(8, 16, 128), buf(7, 16, 128), buf(8, 16, 128), buf(4, 4, 2, 40, 128),
            buf(2, 4, 4, 2, 8, 1024), buf(2, 2, 3, 4, 8, 1024), buf(2, 2, 4, 8, 1024), buf(2, 2, 3, 8, 1024),
            buf(2, 2, 4, 4, 2, 8, 1024), buf(2, 2, 4, 64, 256),
            buf(10, 128, 128), buf(6, 128, 128), buf(2, RANK, RANK),
            buf(2, RANK, 1024), buf(2, 256, RANK), buf(2, 8, RANK), buf(8, 8, 128),
            pltpu.SemaphoreType.DMA((n,)), pltpu.SemaphoreType.DMA((n,)), pltpu.SemaphoreType.DMA((10,)),
        ],
        compiler_params=pltpu.CompilerParams(
            collective_id=0, has_side_effects=True, vmem_limit_bytes=VMEM_BYTES
        ),
        name="dion",
    )(gradient, momentum, right_basis)
    return pl.pallas_call(
        place_kernel,
        out_shape=out_shape,
        in_specs=[anywhere] * 3,
        out_specs=[anywhere] * 3,
        scratch_shapes=[half, buf(2, 256, 1024), buf(2, 16, 1024), pltpu.SemaphoreType.DMA((20,))],
        compiler_params=pltpu.CompilerParams(vmem_limit_bytes=VMEM_BYTES),
        name="place",
    )(*results)


def solution(mesh):
    placed = (P(None, "fsdp", "tp"), P(None, "fsdp", "tp"), P(None, "fsdp", "tp"))
    return jax.shard_map(
        shards,
        mesh=mesh,
        in_specs=placed,
        out_specs=placed,
        check_vma=False,
    )
```

```python
import math

import jax
import jax.numpy as jnp
from jax import lax
from jax.experimental import pallas as pl
from jax.experimental.pallas import tpu as pltpu
from jax.sharding import PartitionSpec as P

D = 8192
RANK = 512
momentum_decay = 0.8
epsilon_sq = 1e-06
MESH = pl.DeviceIdType.MESH
F32 = jnp.float32
HIGH = lax.Precision.HIGH
HIGHEST = lax.Precision.HIGHEST
VMEM_BYTES = 56 * 1024 * 1024


def dot(a, b, ca, cb, precision):
    return lax.dot_general(
        a, b, (((ca,), (cb,)), ((), ())), precision=precision, preferred_element_type=F32
    )


class Place:
    def __init__(self, send_sem, recv_sem):
        f = lax.axis_index("fsdp")
        self.f = f
        self.z = lax.axis_index("tp")
        self.c = lax.rem(f, 2)
        self.x = lax.rem(f // 2, 4)
        self.y = f // 8
        self.send_sem, self.recv_sem = send_sem, recv_sem
        self.count = 0
        self.open = []

    def dev(self, y=None, x=None, z=None, c=None):
        y = self.y if y is None else y
        x = self.x if x is None else x
        c = self.c if c is None else c
        z = self.z if z is None else z
        return ((y * 4 + x) * 2 + c, z)

    def partner(self):
        return self.dev(c=1 - self.c)

    def xs(self, d):
        return lax.rem(self.x + d, 4)

    def ys(self, d):
        return lax.rem(self.y + d, 4)

    def zs(self, d):
        return lax.rem(self.z + d, 8)

    def reserve(self, n):
        i = self.count
        self.count += n
        assert self.count <= self.send_sem.shape[0]
        return i

    def copy(self, src, dst, to, recv=None):
        i = self.reserve(1)
        cp = pltpu.make_async_remote_copy(
            src_ref=src,
            dst_ref=dst,
            send_sem=self.send_sem.at[i],
            recv_sem=self.recv_sem.at[i if recv is None else recv],
            device_id=to,
            device_id_type=MESH,
        )
        cp.start()
        self.open.append(cp)
        return cp

    def barrier(self, peers):
        sem = pltpu.get_barrier_semaphore()
        for p in peers:
            pl.semaphore_signal(sem, inc=1, device_id=p, device_id_type=MESH)
        pl.semaphore_wait(sem, len(peers))

    def drain(self):
        for cp in self.open:
            cp.wait_send()
        self.open = []


def received(copies):
    for cp in copies:
        cp.wait_recv()


class Gather:
    def __init__(self, pc, buf):
        self.pc, self.buf = pc, buf

    def first(self):
        pc, buf = self.pc, self.buf
        self.one = []
        for d in (2, 1, 3):
            a, b = buf.at[pc.y, pc.x, 0], buf.at[pc.y, pc.x, 1]
            self.one.append(pc.copy(a, a, pc.dev(x=pc.xs(d))))
            self.one.append(pc.copy(b, b, pc.dev(y=pc.ys(d))))

    def second(self):
        pc, buf = self.pc, self.buf
        received(self.one)
        self.two, self.passed = {}, []
        for d in (1, 3):
            a, b = buf.at[pc.y, :, 0], buf.at[:, pc.x, 1]
            self.two[d] = (pc.copy(a, a, pc.dev(y=pc.ys(d))), pc.copy(b, b, pc.dev(x=pc.xs(d))))

    def relay(self, d):
        pc, buf = self.pc, self.buf
        received(self.two[d])
        half = pl.ds(0, 2) if d == 1 else pl.ds(2, 2)
        a, b = buf.at[pc.ys(4 - d), half, 0], buf.at[half, pc.xs(4 - d), 1]
        self.passed.append(pc.copy(a, a, pc.dev(y=pc.ys(d))))
        self.passed.append(pc.copy(b, b, pc.dev(x=pc.xs(d))))

    def finish(self):
        received(self.passed)


class Scatter:
    def __init__(self, pc, buf, rel, r1, acc, r2):
        self.pc, self.buf, self.rel, self.r1, self.acc, self.r2 = pc, buf, rel, r1, acc, r2

    def first(self):
        pc, buf, rel = self.pc, self.buf, self.rel
        self.halves = []
        for i, d in enumerate((1, 3)):
            half = pl.ds(2 * i, 2)
            self.halves.append(pc.copy(buf.at[pc.ys(2), half, 0], rel.at[0, i], pc.dev(y=pc.ys(d))))
            self.halves.append(pc.copy(buf.at[half, pc.xs(2), 1], rel.at[1, i], pc.dev(x=pc.xs(d))))

    def middle(self):
        pc, buf, rel, r1 = self.pc, self.buf, self.rel, self.r1
        received(self.halves)
        self.one = []
        for i, d in enumerate((1, 3)):
            half = pl.ds(2 * i, 2)
            buf[pc.ys(d), half, 0] = buf[pc.ys(d), half, 0] + rel[0, i]
            self.one.append(pc.copy(buf.at[pc.ys(d), :, 0], r1.at[0, i], pc.dev(y=pc.ys(d))))
            buf[half, pc.xs(d), 1] = buf[half, pc.xs(d), 1] + rel[1, i]
            self.one.append(pc.copy(buf.at[:, pc.xs(d), 1], r1.at[1, i], pc.dev(x=pc.xs(d))))

    def second(self):
        pc, buf, r1, acc = self.pc, self.buf, self.r1, self.acc
        received(self.one)
        acc[0] = buf[pc.y, :, 0] + r1[0, 0] + r1[0, 1]
        acc[1] = buf[:, pc.x, 1] + r1[1, 0] + r1[1, 1]
        self.two = []
        for d in (2, 1, 3):
            self.two.append(pc.copy(acc.at[0, pc.xs(d)], self.r2.at[0, d - 1], pc.dev(x=pc.xs(d))))
            self.two.append(pc.copy(acc.at[1, pc.ys(d)], self.r2.at[1, d - 1], pc.dev(y=pc.ys(d))))

    def finish(self):
        pc, acc, r2 = self.pc, self.acc, self.r2
        received(self.two)
        own0 = acc[0, pc.x] + r2[0, 0] + r2[0, 1] + r2[0, 2]
        own1 = acc[1, pc.y] + r2[1, 0] + r2[1, 1] + r2[1, 2]
        return own0, own1


def factor_block(load, tick):
    groups = 16
    a = [load(r) for r in range(groups)]
    lane = lax.broadcasted_iota(jnp.int32, (8, 128), 1)
    sub = lax.broadcasted_iota(jnp.int32, (8, 128), 0)
    out = [None] * groups

    def column(v, j):
        return jnp.broadcast_to(v[:, j:j + 1], (8, 128))

    def recip(v):
        return pl.reciprocal(v, approx=True)

    for q in range(32):
        r0, s0, j0 = q // 2, 4 * (q % 2), 4 * q
        rows = [jnp.broadcast_to(a[r0][s0 + s:s0 + s + 1, :], (8, 128)) for s in range(4)]
        p = {(s, t): column(rows[s], j0 + t) for s in range(4) for t in range(s, 4)}
        inside = (lane >= j0) & (lane < j0 + 4)
        sc = [lax.rsqrt(p[s, s]) for s in range(4)]
        v = [jnp.where(inside, jnp.where(lane == j0 + s, 1.0, 0.0), rows[s]) * sc[s] for s in range(4)]
        r = {(s, t): p[s, t] * (sc[s] * sc[t]) for s in range(4) for t in range(s + 1, 4)}
        l10, l20, l30 = r[0, 1], r[0, 2], r[0, 3]
        u11, u22, u33 = 1.0 - l10 * l10, 1.0 - l20 * l20, 1.0 - l30 * l30
        u12, u13, u23 = r[1, 2] - l10 * l20, r[1, 3] - l10 * l30, r[2, 3] - l20 * l30
        v22, v23, v33 = u11 * u22 - u12 * u12, u11 * u23 - u12 * u13, u11 * u33 - u13 * u13
        w33 = v22 * v33 - v23 * v23
        i1, i2, i3 = recip(u11), recip(v22), recip(w33)
        l21, l31, l32 = u12 * i1, u13 * i1, v23 * i2
        d1, d2, d3 = i1, u11 * i2, (u11 * v22) * i3
        n10, n21, n32 = -l10, -l21, -l32
        n20 = l21 * l10 - l20
        n31 = l32 * l21 - l31
        n30 = l31 * l10 - l30 - l32 * n20
        n = [[None] * 4, [n10], [n20, n21], [n30, n31, n32]]
        m = {}
        e1 = d1 * n10
        e20, e21 = d2 * n20, d2 * n21
        m[0, 0] = (1.0 + e1 * n10 + e20 * n20) + d3 * (n30 * n30)
        m[0, 1] = (e1 + e20 * n21) + d3 * (n30 * n31)
        m[0, 2] = e20 + d3 * (n30 * n32)
        m[0, 3] = d3 * n30
        m[1, 1] = (d1 + e21 * n21) + d3 * (n31 * n31)
        m[1, 2] = e21 + d3 * (n31 * n32)
        m[1, 3] = d3 * n31
        m[2, 2] = d2 + d3 * (n32 * n32)
        m[2, 3] = d3 * n32
        m[3, 3] = d3
        w = []
        for s in range(4):
            t = [m[min(s, t), max(s, t)] * v[t] for t in range(4)]
            w.append(((t[0] + t[1]) + (t[2] + t[3])) * sc[s])
        f = [None, d1 * lax.rsqrt(d1), d2 * lax.rsqrt(d2), d3 * lax.rsqrt(d3)]
        done = [v[0]]
        for s in range(1, 4):
            t = v[s]
            for k in range(s):
                t = t + n[s][k] * v[k]
            done.append(f[s] * t)
        o = done[0]
        for s in range(1, 4):
            o = jnp.where(sub == s0 + s, done[s], o)
        out[r0] = o if s0 == 0 else jnp.where(sub < 4, out[r0], o)
        for g in range(r0 if s0 == 0 else r0 + 1, groups):
            t = [column(a[g], j0 + t) * w[t] for t in range(4)]
            a[g] = jnp.where(inside, 0.0, a[g]) - ((t[0] + t[1]) + (t[2] + t[3]))
        tick(q)
    return out


def kernel(
    grad, mom, rb, update, momentum_next, basis_next,
    gv, mv, upd, bnext, blend, blend_send, basis, lpart, lrel, lrecv, left, perm,
    gbuf, grel, gr1, gacc, gr2, zsrc, zpart, zfull, gfull,
    wbuf, wrel, wr1, wacc, wr2, wall, left_all,
    work, ybuf, tri, right, orth, sums, squares,
    send_sem, recv_sem, local_sem,
):
    pc = Place(send_sem, recv_sem)
    c, x, y, z = pc.c, pc.x, pc.y, pc.z
    loads = []
    for i, m in enumerate((1 - c, c)):
        loads.append(
            (
                pltpu.make_async_copy(mom.at[m], mv.at[m], local_sem.at[2 * i]),
                pltpu.make_async_copy(grad.at[m], gv.at[m], local_sem.at[2 * i + 1]),
            )
        )
        for cp in loads[i]:
            cp.start()
    peers = [pc.partner()]
    peers += [pc.dev(x=pc.xs(d), c=m) for d in (1, 2, 3) for m in (0, 1)]
    peers += [pc.dev(y=pc.ys(d), c=m) for d in (1, 2, 3) for m in (0, 1)]
    peers += [pc.dev(z=pc.zs(d)) for d in range(1, 8)]
    pc.barrier(peers)

    first = pc.reserve(6)
    slot = lambda d, h: first + 2 * (d - 1) + h
    for d in (1, 3, 2):
        to_y, to_x = lax.rem(y + d * c, 4), lax.rem(x + d * (1 - c), 4)
        for m in range(2):
            pc.copy(rb.at[m], basis.at[y, x, c], pc.dev(y=to_y, x=to_x, c=m), recv=slot(d, c))
    basis_swap = pc.copy(rb.at[1 - c], basis.at[y, x, c], pc.partner())
    basis[y, x, c] = rb[c]
    for cp in loads[0]:
        cp.wait()
    blend_send[...] = mv[1 - c] + gv[1 - c].astype(F32)
    blend_swap = pc.copy(blend_send, blend.at[c], pc.partner())
    for cp in loads[1]:
        cp.wait()
    blend[c] = mv[c] + gv[c].astype(F32)
    basis_swap.wait_recv()
    for d in (1, 3, 2):
        for h in range(2):
            pltpu.make_async_remote_copy(
                src_ref=rb.at[0],
                dst_ref=basis.at[y, x, h],
                send_sem=send_sem.at[slot(d, h)],
                recv_sem=recv_sem.at[slot(d, h)],
                device_id=pc.partner(),
                device_id_type=MESH,
            ).wait_recv()
    gather = Gather(pc, basis)
    gather.one = []
    gather.second()
    at = lax.broadcasted_iota(jnp.int32, (RANK, RANK), 0)
    group, half = at // 128, (at // 64) % 2
    index, low = (at // 16) % 4, at % 16
    py = jnp.where(half == 0, (y + group) % 4, index)
    px = jnp.where(half == 0, index, (x + group) % 4)
    rank = ((py * 4 + px) * 2 + half) * 16 + low
    perm[...] = jnp.where(lax.broadcasted_iota(jnp.int32, (RANK, RANK), 1) == rank, 1.0, 0.0)
    blend_swap.wait_recv()
    sums_in, opposite = [], {}

    def to_z(d, e):
        i = e - 1 if e < 4 else e - 2
        sums_in.append(pc.copy(lpart.at[d, pc.zs(e)], lrecv.at[i, d], pc.dev(z=pc.zs(e))))

    def to_z_far(d):
        received(opposite[d])
        for i, e in enumerate((3, 5)):
            rows = pl.ds(32 * i, 32)
            lpart[d, pc.zs(e), rows] = lpart[d, pc.zs(e), rows] + lrel[i, d]
            to_z(d, e)

    before = None
    for d in (0, 3, 1, 2):
        if d == 2:
            gather.finish()
        elif d:
            gather.relay(4 - d)
        rows = jnp.concatenate(
            [basis[pc.ys(d), :, 0].reshape(64, 1024), basis[:, pc.xs(d), 1].reshape(64, 1024)], axis=0
        )
        part = dot(blend[...].reshape(512, 1024), rows, 1, 1, HIGH)
        lpart[d] = part.reshape(8, 64, 128)
        opposite[d] = []
        for i, e in enumerate((1, 7)):
            src = lpart.at[d, pc.zs(4), pl.ds(32 * i, 32)]
            opposite[d].append(pc.copy(src, lrel.at[i, d], pc.dev(z=pc.zs(e))))
        if before is not None:
            to_z_far(before)
        for e in (2, 6, 1, 7):
            to_z(d, e)
        before = d
    to_z_far(before)
    received(sums_in)
    own = []
    for d in range(4):
        s = lpart[d, z]
        for e in range(6):
            s = s + lrecv[e, d]
        own.append(s)
    own = dot(jnp.concatenate(own, axis=1), perm[...], 1, 0, HIGHEST)
    for q in range(2):
        left[q, z] = own[:, 256 * q:256 * q + 256]

    def ring(step):
        up, down = pc.dev(z=pc.zs(1)), pc.dev(z=pc.zs(7))
        copies = []
        for q in range(2):
            a, b = left.at[q, pc.zs(9 - step)], left.at[q, pc.zs(step - 1)]
            if step == 4:
                a, b = a.at[pl.ds(0, 32)], b.at[pl.ds(32, 32)]
            copies += [pc.copy(a, a, up), pc.copy(b, b, down)]
        return copies

    blocks = []
    for i in range(4):
        row = dot(own[:, 128 * i:128 * i + 128], own[:, :128 * i + 128], 0, 0, HIGHEST)
        blocks += [row[:, 128 * j:128 * j + 128] for j in range(i + 1)]
    gbuf[...] = jnp.concatenate(blocks, axis=0).reshape(4, 4, 2, 40, 128)
    gscatter = Scatter(pc, gbuf, grel, gr1, gacc, gr2)
    gscatter.first()
    lefts = ring(1)
    gscatter.middle()
    gscatter.second()
    received(lefts)
    lefts = ring(2)
    own0, own1 = gscatter.finish()
    zsrc[0:5] = jnp.concatenate([own0, own1], axis=0).reshape(5, 16, 128)
    zsrc[5:8] = jnp.zeros((3, 16, 128), F32)
    zs = []
    for d in (4, 3, 5, 2, 6, 1, 7):
        zs.append(pc.copy(zsrc.at[pc.zs(d)], zpart.at[d - 1], pc.dev(z=pc.zs(d))))
    received(lefts)
    lefts = ring(3)
    received(zs)
    total = zsrc[z]
    for d in range(7):
        total = total + zpart[d]
    zfull[z] = total
    zs = []
    for d in (4, 3, 5, 2, 6, 1, 7):
        zs.append(pc.copy(zfull.at[z], zfull.at[z], pc.dev(z=pc.zs(d))))
    received(lefts)
    lefts = ring(4)
    received(zs)
    gfull[y, x] = zfull[0:5].reshape(2, 40, 128)
    ggather = Gather(pc, gfull)
    ggather.first()
    received(lefts)
    ggather.second()
    wscatter, wgather = [], []
    for q in range(2):
        for i in range(2):
            lt = left[q, :, :, 128 * i:128 * i + 128].reshape(RANK, 128)
            part = dot(lt, blend[...].reshape(512, 1024), 0, 0, HIGH)
            wbuf[q, 2 * i:2 * i + 2] = part.reshape(2, 4, 2, 8, 1024)
        wscatter.append(Scatter(pc, wbuf.at[q], wrel.at[q], wr1.at[q], wacc.at[q], wr2.at[q]))
        wscatter[q].first()
        if q == 0:
            ggather.relay(1)
            ggather.relay(3)
        wgather.append(Gather(pc, wall.at[c, q]))
    left_all[c] = left[:, pl.ds(4 * c, 4)]
    left_swap = pc.copy(left.at[:, pl.ds(4 * (1 - c), 4)], left_all.at[c], pc.partner())
    ggather.finish()

    w_swaps = ([], [])

    def w_gather(q):
        o0, o1 = wscatter[q].finish()
        wall[c, q, y, x, 0] = o0
        wall[c, q, y, x, 1] = o1
        wgather[q].first()

    def w_gather_second(q):
        wgather[q].second()
        for a in (wall.at[c, q, y, :, 0], wall.at[c, q, :, x, 1]):
            w_swaps[q].append(pc.copy(a, a, pc.partner()))

    def w_swap(q, parts):
        for a in parts:
            w_swaps[q].append(pc.copy(a, a, pc.partner()))

    def w_relay(q):
        for d in (1, 3):
            wgather[q].relay(d)
            w_swap(q, (wall.at[c, q, pc.ys(4 - d), :, 0], wall.at[c, q, :, pc.xs(4 - d), 1]))

    def w_last(q):
        wgather[q].finish()
        w_swap(q, (wall.at[c, q, pc.ys(2), :, 0], wall.at[c, q, :, pc.xs(2), 1]))

    def w_step1():
        wscatter[0].middle()
        wscatter[1].middle()

    def w_step2():
        wscatter[0].second()

    def w_step3():
        wscatter[1].second()
        w_gather(0)

    def w_step4():
        w_gather(1)
        w_gather_second(0)

    def w_step5():
        w_gather_second(1)
        w_relay(0)

    def w_step6():
        w_relay(1)

    def w_step7():
        w_last(0)

    def w_step8():
        w_last(1)

    def raw_job(m, i, j):
        def job():
            cols = pl.ds(256 * j, 256)
            n = 128 * (i + 1)
            wj = [wall[m, q, :, :, :, :, cols].reshape(256, 256) for q in range(2 if i > 1 else 1)]
            wj = jnp.concatenate(wj, axis=0)[:n]
            t = tri[m, pl.ds(128 * i, 128), pl.ds(0, n)]
            right[m, pl.ds(128 * i, 128), cols] = dot(t, wj, 1, 0, HIGH)

        return job

    def raw_own():
        pending.extend(raw_job(c, i, j) for j in range(4) for i in range(3))

    def raw_other():
        received(tri_swaps)
        received(w_swaps[0] + w_swaps[1])
        tri_swaps.clear()
        pending.extend(raw_job(1 - c, i, j) for j in range(4) for i in range(3))

    events = {
        (0, 8): w_step1, (0, 28): w_step2, (1, 6): w_step3, (1, 20): w_step4, (2, 4): w_step5, (2, 16): w_step6,
        (2, 24): w_step7, (3, 0): w_step8, (3, 4): raw_own, (3, 17): raw_other,
    }
    flat = gfull[...].reshape(1280, 128)
    for b in range(10):
        work[b] = flat[128 * b:128 * b + 128]
    at = lambda i, j: i * (i + 1) // 2 + j
    yat = lambda i, j: i * (i - 1) // 2 + j
    rowi = lax.broadcasted_iota(jnp.int32, (128, 128), 0)
    coli = lax.broadcasted_iota(jnp.int32, (128, 128), 1)
    tri_swaps = []
    pending = []

    def tri_row(k, inv):
        for j in range(4):
            cols = pl.ds(128 * j, 128)
            if j < k:
                tri[c, pl.ds(128 * k, 128), cols] = dot(inv, ybuf[yat(k, j)], 1, 0, HIGHEST)
            elif j == k:
                tri[c, pl.ds(128 * k, 128), cols] = inv
            else:
                tri[c, pl.ds(128 * k, 128), cols] = jnp.zeros((128, 128), F32)
        a = tri.at[c, pl.ds(128 * k, 128)]
        tri_swaps.append(pc.copy(a, a, pc.partner()))

    def later(k, inv):
        def solve(i):
            work[at(i, k)] = dot(work[at(i, k)], inv, 1, 1, HIGHEST)

        def trail(i, j):
            work[at(i, j)] = work[at(i, j)] - dot(work[at(i, k)], work[at(j, k)], 1, 1, HIGHEST)

        def inverse(i, j):
            new = dot(work[at(i, k)], tri[c, pl.ds(128 * k, 128), pl.ds(128 * j, 128)], 1, 0, HIGHEST)
            ybuf[yat(i, j)] = -new if j == k else ybuf[yat(i, j)] - new

        jobs = [lambda: tri_row(k, inv)]
        for i in range(k + 2, 4):
            jobs.append(lambda i=i: solve(i))
        for i in range(k + 2, 4):
            for j in range(k + 1, i + 1):
                jobs.append(lambda i=i, j=j: trail(i, j))
        for i in range(k + 1, 4):
            for j in range(k + 1):
                jobs.append(lambda i=i, j=j: inverse(i, j))
        return jobs

    for k in range(4):

        def tick(q, k=k):
            if (k, q) in events:
                events[k, q]()
            if pending and q >= 1:
                pending.pop(0)()

        rows = factor_block(lambda r: work[at(k, k), 8 * r:8 * r + 8, :], tick)
        while pending:
            pending.pop(0)()
        inv = jnp.where(rowi >= coli, jnp.concatenate(rows, axis=0), 0.0)
        if k < 3:
            below = dot(work[at(k + 1, k)], inv, 1, 1, HIGHEST)
            work[at(k + 1, k)] = below
            work[at(k + 1, k + 1)] = work[at(k + 1, k + 1)] - dot(below, below, 1, 1, HIGHEST)
            pending = later(k, inv)
        else:
            tri_row(k, inv)

    def raw_end(m):
        def part(j, carry):
            cols = pl.ds(pl.multiple_of(j * 256, 256), 256)
            wj = wall[m, :, :, :, :, :, cols].reshape(RANK, 256)
            right[m, 384:, cols] = dot(tri[m, 384:, :], wj, 1, 0, HIGH)
            return carry

        lax.fori_loop(0, 4, part, 0)

    def squares_of(m):
        fold = right[m, :, 0:128] * right[m, :, 0:128]
        for j in range(1, 8):
            fold = fold + right[m, :, 128 * j:128 * j + 128] * right[m, :, 128 * j:128 * j + 128]
        sums[m] = dot(jnp.ones((8, 128), F32), fold, 1, 1, HIGHEST)

    raw_end(c)
    squares_of(c)
    received(tri_swaps)
    raw_end(1 - c)
    squares_of(1 - c)
    left_swap.wait_recv()
    pieces = [sums[m, 0:1, 128 * j:128 * j + 128] for m in range(2) for j in range(4)]
    squares[z] = jnp.concatenate(pieces, axis=0)
    zs = []
    for d in (4, 3, 5, 2, 6, 1, 7):
        zs.append(pc.copy(squares.at[z], squares.at[z], pc.dev(z=pc.zs(d))))
    stores = []

    def store(src, dst):
        cp = pltpu.make_async_copy(src, dst, local_sem.at[4 + len(stores)])
        cp.start()
        stores.append(cp)

    for m in range(2):
        rows = jnp.concatenate([left_all[m, q].reshape(256, 256) for q in range(2)], axis=1)
        orth[m] = dot(rows, tri[m], 1, 1, HIGH)

        def feed(j, carry, m=m):
            cols = pl.ds(pl.multiple_of(j * 256, 256), 256)
            back = dot(orth[m], right[m, :, cols], 1, 0, HIGH)
            blended = mv[m, :, cols] + gv[m, :, cols].astype(F32)
            mv[m, :, cols] = blended - (1.0 - momentum_decay) * back
            return carry

        lax.fori_loop(0, 4, feed, 0)
        store(mv.at[m], momentum_next.at[m])
    received(zs)
    total = squares[0]
    for d in range(1, 8):
        total = total + squares[d]
    inverse = lax.rsqrt(total / D + epsilon_sq)
    lane = lax.broadcasted_iota(jnp.int32, (16, RANK), 1)
    sub = lax.broadcasted_iota(jnp.int32, (16, RANK), 0)
    for m in range(2):
        inv = jnp.concatenate([inverse[4 * m + j:4 * m + j + 1] for j in range(4)], axis=1)
        orth[m] = orth[m] * inv
        pick = jnp.sum(jnp.where(lane == pc.f * 16 + sub, inv, 0.0), axis=1, keepdims=True)
        bnext[m] = right[m, pl.ds(pl.multiple_of(pc.f * 16, 16), 16), :] * pick
        store(bnext.at[m], basis_next.at[m])

        def direction(j, carry, m=m):
            cols = pl.ds(pl.multiple_of(j * 256, 256), 256)
            out = math.sqrt(D / RANK) * dot(orth[m], right[m, :, cols], 1, 0, HIGH)
            upd[m, :, cols] = out.astype(jnp.bfloat16)
            return carry

        lax.fori_loop(0, 4, direction, 0)
        store(upd.at[m], update.at[m])
    for cp in stores:
        cp.wait()
    pc.drain()


def place_kernel(update, momentum_next, basis_next, update_out, momentum_out, basis_out, uv, mv, bv, sem):
    parts = [(basis_next, bv, basis_out, pl.ds(0, 16))]
    for i in range(2):
        parts.append((momentum_next, mv, momentum_out, pl.ds(128 * i, 128)))
        parts.append((update, uv, update_out, pl.ds(128 * i, 128)))
    loads, stores = [], []
    for m in range(2):
        for src, held, dst, rows in parts:
            i = len(loads)
            loads.append(pltpu.make_async_copy(src.at[m, rows], held.at[m, rows], sem.at[2 * i]))
            stores.append(pltpu.make_async_copy(held.at[m, rows], dst.at[m, rows], sem.at[2 * i + 1]))
    for cp in loads:
        cp.start()
    for a, b in zip(loads, stores):
        a.wait()
        b.start()
    for cp in stores:
        cp.wait()


def shards(gradient, momentum, right_basis):
    vmem = pl.BlockSpec(memory_space=pltpu.VMEM)
    anywhere = pl.BlockSpec(memory_space=pl.ANY)
    shape = lambda s: jax.ShapeDtypeStruct(s, F32)
    buf = lambda *s: pltpu.VMEM(s, F32)
    half = pltpu.VMEM((2, 256, 1024), jnp.bfloat16)
    out_shape = (jax.ShapeDtypeStruct((2, 256, 1024), jnp.bfloat16), shape((2, 256, 1024)), shape((2, 16, 1024)))
    n = 208
    results = pl.pallas_call(
        kernel,
        out_shape=out_shape,
        in_specs=[anywhere, anywhere, vmem],
        out_specs=[anywhere] * 3,
        scratch_shapes=[
            half, buf(2, 256, 1024), half, buf(2, 16, 1024),
            buf(2, 256, 1024), buf(256, 1024), buf(4, 4, 2, 16, 1024),
            buf(4, 8, 64, 128), buf(2, 4, 32, 128), buf(6, 4, 64, 128), buf(2, 8, 64, 256), buf(RANK, RANK),
            buf(4, 4, 2, 40, 128), buf(2, 2, 2, 40, 128), buf(2, 2, 4, 40, 128), buf(2, 4, 40, 128), buf(2, 3, 40, 128),
            buf(8, 16, 128), buf(7, 16, 128), buf(8, 16, 128), buf(4, 4, 2, 40, 128),
            buf(2, 4, 4, 2, 8, 1024), buf(2, 2, 2, 2, 8, 1024), buf(2, 2, 2, 4, 8, 1024), buf(2, 2, 4, 8, 1024), buf(2, 2, 3, 8, 1024),
            buf(2, 2, 4, 4, 2, 8, 1024), buf(2, 2, 4, 64, 256),
            buf(10, 128, 128), buf(6, 128, 128), buf(2, RANK, RANK),
            buf(2, RANK, 1024), buf(2, 256, RANK), buf(2, 8, RANK), buf(8, 8, 128),
            pltpu.SemaphoreType.DMA((n,)), pltpu.SemaphoreType.DMA((n,)), pltpu.SemaphoreType.DMA((10,)),
        ],
        compiler_params=pltpu.CompilerParams(
            collective_id=0, has_side_effects=True, vmem_limit_bytes=VMEM_BYTES
        ),
        name="dion",
    )(gradient, momentum, right_basis)
    return pl.pallas_call(
        place_kernel,
        out_shape=out_shape,
        in_specs=[anywhere] * 3,
        out_specs=[anywhere] * 3,
        scratch_shapes=[half, buf(2, 256, 1024), buf(2, 16, 1024), pltpu.SemaphoreType.DMA((20,))],
        compiler_params=pltpu.CompilerParams(vmem_limit_bytes=VMEM_BYTES),
        name="place",
    )(*results)


def solution(mesh):
    placed = (P(None, "fsdp", "tp"), P(None, "fsdp", "tp"), P(None, "fsdp", "tp"))
    return jax.shard_map(
        shards,
        mesh=mesh,
        in_specs=placed,
        out_specs=placed,
        check_vma=False,
    )
```

```python
import math

import jax
import jax.numpy as jnp
from jax import lax
from jax.experimental import pallas as pl
from jax.experimental.pallas import tpu as pltpu
from jax.sharding import PartitionSpec as P

D = 8192
RANK = 512
momentum_decay = 0.8
epsilon_sq = 1e-06
MESH = pl.DeviceIdType.MESH
F32 = jnp.float32
HIGH = lax.Precision.HIGH
HIGHEST = lax.Precision.HIGHEST
VMEM_BYTES = 56 * 1024 * 1024


def dot(a, b, ca, cb, precision):
    return lax.dot_general(
        a, b, (((ca,), (cb,)), ((), ())), precision=precision, preferred_element_type=F32
    )


class Place:
    def __init__(self, send_sem, recv_sem):
        f = lax.axis_index("fsdp")
        self.f = f
        self.z = lax.axis_index("tp")
        self.c = lax.rem(f, 2)
        self.x = lax.rem(f // 2, 4)
        self.y = f // 8
        self.send_sem, self.recv_sem = send_sem, recv_sem
        self.count = 0
        self.open = []

    def dev(self, y=None, x=None, z=None, c=None):
        y = self.y if y is None else y
        x = self.x if x is None else x
        c = self.c if c is None else c
        z = self.z if z is None else z
        return ((y * 4 + x) * 2 + c, z)

    def partner(self):
        return self.dev(c=1 - self.c)

    def xs(self, d):
        return lax.rem(self.x + d, 4)

    def ys(self, d):
        return lax.rem(self.y + d, 4)

    def zs(self, d):
        return lax.rem(self.z + d, 8)

    def reserve(self, n):
        i = self.count
        self.count += n
        assert self.count <= self.send_sem.shape[0]
        return i

    def copy(self, src, dst, to, recv=None):
        i = self.reserve(1)
        cp = pltpu.make_async_remote_copy(
            src_ref=src,
            dst_ref=dst,
            send_sem=self.send_sem.at[i],
            recv_sem=self.recv_sem.at[i if recv is None else recv],
            device_id=to,
            device_id_type=MESH,
        )
        cp.start()
        self.open.append(cp)
        return cp

    def barrier(self, peers):
        sem = pltpu.get_barrier_semaphore()
        for p in peers:
            pl.semaphore_signal(sem, inc=1, device_id=p, device_id_type=MESH)
        pl.semaphore_wait(sem, len(peers))

    def drain(self):
        for cp in self.open:
            cp.wait_send()
        self.open = []


def received(copies):
    for cp in copies:
        cp.wait_recv()


class Gather:
    def __init__(self, pc, buf):
        self.pc, self.buf = pc, buf

    def first(self):
        pc, buf = self.pc, self.buf
        self.one = []
        for d in (2, 1, 3):
            a, b = buf.at[pc.y, pc.x, 0], buf.at[pc.y, pc.x, 1]
            self.one.append(pc.copy(a, a, pc.dev(x=pc.xs(d))))
            self.one.append(pc.copy(b, b, pc.dev(y=pc.ys(d))))

    def second(self):
        pc, buf = self.pc, self.buf
        received(self.one)
        self.two, self.passed = {}, []
        for d in (1, 3):
            a, b = buf.at[pc.y, :, 0], buf.at[:, pc.x, 1]
            self.two[d] = (pc.copy(a, a, pc.dev(y=pc.ys(d))), pc.copy(b, b, pc.dev(x=pc.xs(d))))

    def relay(self, d):
        pc, buf = self.pc, self.buf
        received(self.two[d])
        half = pl.ds(0, 2) if d == 1 else pl.ds(2, 2)
        a, b = buf.at[pc.ys(4 - d), half, 0], buf.at[half, pc.xs(4 - d), 1]
        self.passed.append(pc.copy(a, a, pc.dev(y=pc.ys(d))))
        self.passed.append(pc.copy(b, b, pc.dev(x=pc.xs(d))))

    def finish(self):
        received(self.passed)


class Scatter:
    def __init__(self, pc, buf, rel, r1, acc, r2):
        self.pc, self.buf, self.rel, self.r1, self.acc, self.r2 = pc, buf, rel, r1, acc, r2

    def first(self):
        pc, buf, rel = self.pc, self.buf, self.rel
        self.halves = []
        for i, d in enumerate((1, 3)):
            half = pl.ds(2 * i, 2)
            self.halves.append(pc.copy(buf.at[pc.ys(2), half, 0], rel.at[0, i], pc.dev(y=pc.ys(d))))
            self.halves.append(pc.copy(buf.at[half, pc.xs(2), 1], rel.at[1, i], pc.dev(x=pc.xs(d))))

    def middle(self):
        pc, buf, rel, r1 = self.pc, self.buf, self.rel, self.r1
        received(self.halves)
        self.one = []
        for i, d in enumerate((1, 3)):
            half = pl.ds(2 * i, 2)
            buf[pc.ys(d), half, 0] = buf[pc.ys(d), half, 0] + rel[0, i]
            self.one.append(pc.copy(buf.at[pc.ys(d), :, 0], r1.at[0, i], pc.dev(y=pc.ys(d))))
            buf[half, pc.xs(d), 1] = buf[half, pc.xs(d), 1] + rel[1, i]
            self.one.append(pc.copy(buf.at[:, pc.xs(d), 1], r1.at[1, i], pc.dev(x=pc.xs(d))))

    def second(self):
        pc, buf, r1, acc = self.pc, self.buf, self.r1, self.acc
        received(self.one)
        acc[0] = buf[pc.y, :, 0] + r1[0, 0] + r1[0, 1]
        acc[1] = buf[:, pc.x, 1] + r1[1, 0] + r1[1, 1]
        self.two = []
        for d in (2, 1, 3):
            self.two.append(pc.copy(acc.at[0, pc.xs(d)], self.r2.at[0, d - 1], pc.dev(x=pc.xs(d))))
            self.two.append(pc.copy(acc.at[1, pc.ys(d)], self.r2.at[1, d - 1], pc.dev(y=pc.ys(d))))

    def finish(self):
        pc, acc, r2 = self.pc, self.acc, self.r2
        received(self.two)
        own0 = acc[0, pc.x] + r2[0, 0] + r2[0, 1] + r2[0, 2]
        own1 = acc[1, pc.y] + r2[1, 0] + r2[1, 1] + r2[1, 2]
        return own0, own1


def factor_block(load, tick):
    groups = 16
    a = [load(r) for r in range(groups)]
    lane = lax.broadcasted_iota(jnp.int32, (8, 128), 1)
    sub = lax.broadcasted_iota(jnp.int32, (8, 128), 0)
    out = [None] * groups

    def column(v, j):
        return jnp.broadcast_to(v[:, j:j + 1], (8, 128))

    def spread(v, i):
        return jnp.broadcast_to(v[i:i + 1, :], (8, 128))

    def recip(v):
        return pl.reciprocal(v, approx=True)

    for q in range(32):
        r0, s0, j0 = q // 2, 4 * (q % 2), 4 * q
        end = 4 * (r0 // 4) + 4
        rows = [spread(a[r0], s0 + s) for s in range(4)]
        cols = [column(a[r0], j0 + t) for t in range(4)]
        p = {(s, t): spread(cols[t], s0 + s) for s in range(4) for t in range(s, 4)}
        inside = (lane >= j0) & (lane < j0 + 4)
        sc = [lax.rsqrt(p[s, s]) for s in range(4)]
        v = [jnp.where(inside, jnp.where(lane == j0 + s, 1.0, 0.0), rows[s]) * sc[s] for s in range(4)]
        r = {(s, t): p[s, t] * (sc[s] * sc[t]) for s in range(4) for t in range(s + 1, 4)}
        l10, l20, l30 = r[0, 1], r[0, 2], r[0, 3]
        u11, u22, u33 = 1.0 - l10 * l10, 1.0 - l20 * l20, 1.0 - l30 * l30
        u12, u13, u23 = r[1, 2] - l10 * l20, r[1, 3] - l10 * l30, r[2, 3] - l20 * l30
        v22, v23, v33 = u11 * u22 - u12 * u12, u11 * u23 - u12 * u13, u11 * u33 - u13 * u13
        w33 = v22 * v33 - v23 * v23
        i1, i2, i3 = recip(u11), recip(v22), recip(w33)
        l21, l31, l32 = u12 * i1, u13 * i1, v23 * i2
        d1, d2, d3 = i1, u11 * i2, (u11 * v22) * i3
        n10, n21, n32 = -l10, -l21, -l32
        n20 = l21 * l10 - l20
        n31 = l32 * l21 - l31
        n30 = l31 * l10 - l30 - l32 * n20
        n = [[None] * 4, [n10], [n20, n21], [n30, n31, n32]]
        m = {}
        e1 = d1 * n10
        e20, e21 = d2 * n20, d2 * n21
        m[0, 0] = (1.0 + e1 * n10 + e20 * n20) + d3 * (n30 * n30)
        m[0, 1] = (e1 + e20 * n21) + d3 * (n30 * n31)
        m[0, 2] = e20 + d3 * (n30 * n32)
        m[0, 3] = d3 * n30
        m[1, 1] = (d1 + e21 * n21) + d3 * (n31 * n31)
        m[1, 2] = e21 + d3 * (n31 * n32)
        m[1, 3] = d3 * n31
        m[2, 2] = d2 + d3 * (n32 * n32)
        m[2, 3] = d3 * n32
        m[3, 3] = d3
        w = []
        for s in range(4):
            t = [m[min(s, t), max(s, t)] * v[t] for t in range(4)]
            w.append(((t[0] + t[1]) + (t[2] + t[3])) * sc[s])
        f = [None, d1 * lax.rsqrt(d1), d2 * lax.rsqrt(d2), d3 * lax.rsqrt(d3)]
        done = [v[0]]
        for s in range(1, 4):
            t = v[s]
            for k in range(s):
                t = t + n[s][k] * v[k]
            done.append(f[s] * t)
        o = done[0]
        for s in range(1, 4):
            o = jnp.where(sub == s0 + s, done[s], o)
        out[r0] = o if s0 == 0 else jnp.where(sub < 4, out[r0], o)
        for g in range(r0 if s0 == 0 else r0 + 1, end):
            if g > r0:
                cols = [column(a[g], j0 + t) for t in range(4)]
            t = [cols[t] * w[t] for t in range(4)]
            a[g] = jnp.where(inside, 0.0, a[g]) - ((t[0] + t[1]) + (t[2] + t[3]))
        if q % 8 == 7 and end < groups:
            new = jnp.concatenate(out[end - 4:end], axis=0)
            lanes = lax.broadcasted_iota(jnp.int32, (32, 128), 1)
            over = lanes > 8 * end - 32 + lax.broadcasted_iota(jnp.int32, (32, 128), 0)
            right = jnp.where(lanes >= 8 * end, new, 0.0)
            step = dot(right, jnp.where(over, right, new), 0, 0, HIGHEST)
            done_lanes = (lane >= 8 * end - 32) & (lane < 8 * end)
            for g in range(end, groups):
                a[g] = jnp.where(done_lanes, 0.0, a[g]) - step[8 * g:8 * g + 8]
        tick(q)
    return out


def kernel(
    grad, mom, rb, update, momentum_next, basis_next,
    gv, mv, upd, bnext, blend, blend_send, basis, lpart, lrel, lrecv, left, perm,
    gbuf, grel, gr1, gacc, gr2, zsrc, zpart, zfull, gfull,
    wbuf, wrel, wr1, wacc, wr2, wall, left_all,
    work, ybuf, tri, right, orth, sums, squares,
    send_sem, recv_sem, local_sem,
):
    pc = Place(send_sem, recv_sem)
    c, x, y, z = pc.c, pc.x, pc.y, pc.z
    loads = []
    for i, m in enumerate((1 - c, c)):
        loads.append(
            (
                pltpu.make_async_copy(mom.at[m], mv.at[m], local_sem.at[2 * i]),
                pltpu.make_async_copy(grad.at[m], gv.at[m], local_sem.at[2 * i + 1]),
            )
        )
        for cp in loads[i]:
            cp.start()
    peers = [pc.partner()]
    peers += [pc.dev(x=pc.xs(d), c=m) for d in (1, 2, 3) for m in (0, 1)]
    peers += [pc.dev(y=pc.ys(d), c=m) for d in (1, 2, 3) for m in (0, 1)]
    peers += [pc.dev(z=pc.zs(d)) for d in range(1, 8)]
    pc.barrier(peers)

    first = pc.reserve(6)
    slot = lambda d, h: first + 2 * (d - 1) + h
    for d in (1, 3, 2):
        to_y, to_x = lax.rem(y + d * c, 4), lax.rem(x + d * (1 - c), 4)
        for m in range(2):
            pc.copy(rb.at[m], basis.at[y, x, c], pc.dev(y=to_y, x=to_x, c=m), recv=slot(d, c))
    basis_swap = pc.copy(rb.at[1 - c], basis.at[y, x, c], pc.partner())
    basis[y, x, c] = rb[c]
    for cp in loads[0]:
        cp.wait()
    blend_send[...] = mv[1 - c] + gv[1 - c].astype(F32)
    blend_swap = pc.copy(blend_send, blend.at[c], pc.partner())
    for cp in loads[1]:
        cp.wait()
    blend[c] = mv[c] + gv[c].astype(F32)
    basis_swap.wait_recv()
    for d in (1, 3, 2):
        for h in range(2):
            pltpu.make_async_remote_copy(
                src_ref=rb.at[0],
                dst_ref=basis.at[y, x, h],
                send_sem=send_sem.at[slot(d, h)],
                recv_sem=recv_sem.at[slot(d, h)],
                device_id=pc.partner(),
                device_id_type=MESH,
            ).wait_recv()
    gather = Gather(pc, basis)
    gather.one = []
    gather.second()
    at = lax.broadcasted_iota(jnp.int32, (RANK, RANK), 0)
    group, half = at // 128, (at // 64) % 2
    index, low = (at // 16) % 4, at % 16
    py = jnp.where(half == 0, (y + group) % 4, index)
    px = jnp.where(half == 0, index, (x + group) % 4)
    rank = ((py * 4 + px) * 2 + half) * 16 + low
    perm[...] = jnp.where(lax.broadcasted_iota(jnp.int32, (RANK, RANK), 1) == rank, 1.0, 0.0)
    blend_swap.wait_recv()
    sums_in, opposite = [], {}

    def to_z(d, e):
        i = e - 1 if e < 4 else e - 2
        sums_in.append(pc.copy(lpart.at[d, pc.zs(e)], lrecv.at[i, d], pc.dev(z=pc.zs(e))))

    def to_z_far(d):
        received(opposite[d])
        for i, e in enumerate((3, 5)):
            rows = pl.ds(32 * i, 32)
            lpart[d, pc.zs(e), rows] = lpart[d, pc.zs(e), rows] + lrel[i, d]
            to_z(d, e)

    before = None
    for d in (0, 3, 1, 2):
        if d == 2:
            gather.finish()
        elif d:
            gather.relay(4 - d)
        rows = jnp.concatenate(
            [basis[pc.ys(d), :, 0].reshape(64, 1024), basis[:, pc.xs(d), 1].reshape(64, 1024)], axis=0
        )
        part = dot(blend[...].reshape(512, 1024), rows, 1, 1, HIGH)
        lpart[d] = part.reshape(8, 64, 128)
        opposite[d] = []
        for i, e in enumerate((1, 7)):
            src = lpart.at[d, pc.zs(4), pl.ds(32 * i, 32)]
            opposite[d].append(pc.copy(src, lrel.at[i, d], pc.dev(z=pc.zs(e))))
        if before is not None:
            to_z_far(before)
        for e in (2, 6, 1, 7):
            to_z(d, e)
        before = d
    to_z_far(before)
    received(sums_in)
    own = []
    for d in range(4):
        s = lpart[d, z]
        for e in range(6):
            s = s + lrecv[e, d]
        own.append(s)
    own = dot(jnp.concatenate(own, axis=1), perm[...], 1, 0, HIGHEST)
    for q in range(2):
        left[q, z] = own[:, 256 * q:256 * q + 256]

    def ring(step):
        up, down = pc.dev(z=pc.zs(1)), pc.dev(z=pc.zs(7))
        copies = []
        for q in range(2):
            a, b = left.at[q, pc.zs(9 - step)], left.at[q, pc.zs(step - 1)]
            if step == 4:
                a, b = a.at[pl.ds(0, 32)], b.at[pl.ds(32, 32)]
            copies += [pc.copy(a, a, up), pc.copy(b, b, down)]
        return copies

    blocks = []
    for i in range(4):
        row = dot(own[:, 128 * i:128 * i + 128], own[:, :128 * i + 128], 0, 0, HIGHEST)
        blocks += [row[:, 128 * j:128 * j + 128] for j in range(i + 1)]
    gbuf[...] = jnp.concatenate(blocks, axis=0).reshape(4, 4, 2, 40, 128)
    gscatter = Scatter(pc, gbuf, grel, gr1, gacc, gr2)
    gscatter.first()
    lefts = ring(1)
    gscatter.middle()
    gscatter.second()
    received(lefts)
    lefts = ring(2)
    own0, own1 = gscatter.finish()
    zsrc[0:5] = jnp.concatenate([own0, own1], axis=0).reshape(5, 16, 128)
    zsrc[5:8] = jnp.zeros((3, 16, 128), F32)
    zs = []
    for d in (4, 3, 5, 2, 6, 1, 7):
        zs.append(pc.copy(zsrc.at[pc.zs(d)], zpart.at[d - 1], pc.dev(z=pc.zs(d))))
    received(lefts)
    lefts = ring(3)
    received(zs)
    total = zsrc[z]
    for d in range(7):
        total = total + zpart[d]
    zfull[z] = total
    zs = []
    for d in (4, 3, 5, 2, 6, 1, 7):
        zs.append(pc.copy(zfull.at[z], zfull.at[z], pc.dev(z=pc.zs(d))))
    received(lefts)
    lefts = ring(4)
    received(zs)
    gfull[y, x] = zfull[0:5].reshape(2, 40, 128)
    ggather = Gather(pc, gfull)
    ggather.first()
    received(lefts)
    ggather.second()
    wscatter, wgather = [], []
    for q in range(2):
        for i in range(2):
            lt = left[q, :, :, 128 * i:128 * i + 128].reshape(RANK, 128)
            part = dot(lt, blend[...].reshape(512, 1024), 0, 0, HIGH)
            wbuf[q, 2 * i:2 * i + 2] = part.reshape(2, 4, 2, 8, 1024)
        wscatter.append(Scatter(pc, wbuf.at[q], wrel.at[q], wr1.at[q], wacc.at[q], wr2.at[q]))
        wscatter[q].first()
        if q == 0:
            ggather.relay(1)
            ggather.relay(3)
        wgather.append(Gather(pc, wall.at[c, q]))
    left_all[c] = left[:, pl.ds(4 * c, 4)]
    left_swap = pc.copy(left.at[:, pl.ds(4 * (1 - c), 4)], left_all.at[c], pc.partner())
    ggather.finish()

    w_swaps = ([], [])

    def w_gather(q):
        o0, o1 = wscatter[q].finish()
        wall[c, q, y, x, 0] = o0
        wall[c, q, y, x, 1] = o1
        wgather[q].first()

    def w_gather_second(q):
        wgather[q].second()
        for a in (wall.at[c, q, y, :, 0], wall.at[c, q, :, x, 1]):
            w_swaps[q].append(pc.copy(a, a, pc.partner()))

    def w_swap(q, parts):
        for a in parts:
            w_swaps[q].append(pc.copy(a, a, pc.partner()))

    def w_relay(q):
        for d in (1, 3):
            wgather[q].relay(d)
            w_swap(q, (wall.at[c, q, pc.ys(4 - d), :, 0], wall.at[c, q, :, pc.xs(4 - d), 1]))

    def w_last(q):
        wgather[q].finish()
        w_swap(q, (wall.at[c, q, pc.ys(2), :, 0], wall.at[c, q, :, pc.xs(2), 1]))

    def w_step1():
        wscatter[0].middle()
        wscatter[1].middle()

    def w_step2():
        wscatter[0].second()

    def w_step3():
        wscatter[1].second()
        w_gather(0)

    def w_step4():
        w_gather(1)
        w_gather_second(0)

    def w_step5():
        w_gather_second(1)
        w_relay(0)

    def w_step6():
        w_relay(1)

    def w_step7():
        w_last(0)

    def w_step8():
        w_last(1)

    def raw_job(m, i, j):
        def job():
            cols = pl.ds(256 * j, 256)
            n = 128 * (i + 1)
            wj = [wall[m, q, :, :, :, :, cols].reshape(256, 256) for q in range(2 if i > 1 else 1)]
            wj = jnp.concatenate(wj, axis=0)[:n]
            t = tri[m, pl.ds(128 * i, 128), pl.ds(0, n)]
            right[m, pl.ds(128 * i, 128), cols] = dot(t, wj, 1, 0, HIGH)

        return job

    def raw_own():
        pending.extend(raw_job(c, i, j) for j in range(4) for i in range(3))

    def raw_other():
        received(tri_swaps)
        received(w_swaps[0] + w_swaps[1])
        tri_swaps.clear()
        pending.extend(raw_job(1 - c, i, j) for j in range(4) for i in range(3))

    events = {
        (0, 8): w_step1, (0, 28): w_step2, (1, 6): w_step3, (1, 20): w_step4, (2, 4): w_step5, (2, 16): w_step6,
        (2, 24): w_step7, (3, 0): w_step8, (3, 4): raw_own, (3, 17): raw_other,
    }
    flat = gfull[...].reshape(1280, 128)
    for b in range(10):
        work[b] = flat[128 * b:128 * b + 128]
    at = lambda i, j: i * (i + 1) // 2 + j
    yat = lambda i, j: i * (i - 1) // 2 + j
    rowi = lax.broadcasted_iota(jnp.int32, (128, 128), 0)
    coli = lax.broadcasted_iota(jnp.int32, (128, 128), 1)
    tri_swaps = []
    pending = []

    def tri_row(k, inv):
        for j in range(4):
            cols = pl.ds(128 * j, 128)
            if j < k:
                tri[c, pl.ds(128 * k, 128), cols] = dot(inv, ybuf[yat(k, j)], 1, 0, HIGHEST)
            elif j == k:
                tri[c, pl.ds(128 * k, 128), cols] = inv
            else:
                tri[c, pl.ds(128 * k, 128), cols] = jnp.zeros((128, 128), F32)
        a = tri.at[c, pl.ds(128 * k, 128)]
        tri_swaps.append(pc.copy(a, a, pc.partner()))

    def later(k, inv):
        def solve(i):
            work[at(i, k)] = dot(work[at(i, k)], inv, 1, 1, HIGHEST)

        def trail(i, j):
            work[at(i, j)] = work[at(i, j)] - dot(work[at(i, k)], work[at(j, k)], 1, 1, HIGHEST)

        def inverse(i, j):
            new = dot(work[at(i, k)], tri[c, pl.ds(128 * k, 128), pl.ds(128 * j, 128)], 1, 0, HIGHEST)
            ybuf[yat(i, j)] = -new if j == k else ybuf[yat(i, j)] - new

        jobs = [lambda: tri_row(k, inv)]
        for i in range(k + 2, 4):
            jobs.append(lambda i=i: solve(i))
        for i in range(k + 2, 4):
            for j in range(k + 1, i + 1):
                jobs.append(lambda i=i, j=j: trail(i, j))
        for i in range(k + 1, 4):
            for j in range(k + 1):
                jobs.append(lambda i=i, j=j: inverse(i, j))
        return jobs

    for k in range(4):

        def tick(q, k=k):
            if (k, q) in events:
                events[k, q]()
            if pending and q >= 1:
                pending.pop(0)()

        rows = factor_block(lambda r: work[at(k, k), 8 * r:8 * r + 8, :], tick)
        while pending:
            pending.pop(0)()
        inv = jnp.where(rowi >= coli, jnp.concatenate(rows, axis=0), 0.0)
        if k < 3:
            below = dot(work[at(k + 1, k)], inv, 1, 1, HIGHEST)
            work[at(k + 1, k)] = below
            work[at(k + 1, k + 1)] = work[at(k + 1, k + 1)] - dot(below, below, 1, 1, HIGHEST)
            pending = later(k, inv)
        else:
            tri_row(k, inv)

    def raw_end(m):
        def part(j, carry):
            cols = pl.ds(pl.multiple_of(j * 256, 256), 256)
            wj = wall[m, :, :, :, :, :, cols].reshape(RANK, 256)
            right[m, 384:, cols] = dot(tri[m, 384:, :], wj, 1, 0, HIGH)
            return carry

        lax.fori_loop(0, 4, part, 0)

    def squares_of(m):
        fold = right[m, :, 0:128] * right[m, :, 0:128]
        for j in range(1, 8):
            fold = fold + right[m, :, 128 * j:128 * j + 128] * right[m, :, 128 * j:128 * j + 128]
        sums[m] = dot(jnp.ones((8, 128), F32), fold, 1, 1, HIGHEST)

    raw_end(c)
    squares_of(c)
    received(tri_swaps)
    raw_end(1 - c)
    squares_of(1 - c)
    left_swap.wait_recv()
    pieces = [sums[m, 0:1, 128 * j:128 * j + 128] for m in range(2) for j in range(4)]
    squares[z] = jnp.concatenate(pieces, axis=0)
    zs = []
    for d in (4, 3, 5, 2, 6, 1, 7):
        zs.append(pc.copy(squares.at[z], squares.at[z], pc.dev(z=pc.zs(d))))
    stores = []

    def store(src, dst):
        cp = pltpu.make_async_copy(src, dst, local_sem.at[4 + len(stores)])
        cp.start()
        stores.append(cp)

    for m in range(2):
        rows = jnp.concatenate([left_all[m, q].reshape(256, 256) for q in range(2)], axis=1)
        orth[m] = dot(rows, tri[m], 1, 1, HIGH)

        def feed(j, carry, m=m):
            cols = pl.ds(pl.multiple_of(j * 256, 256), 256)
            back = dot(orth[m], right[m, :, cols], 1, 0, HIGH)
            blended = mv[m, :, cols] + gv[m, :, cols].astype(F32)
            mv[m, :, cols] = blended - (1.0 - momentum_decay) * back
            return carry

        lax.fori_loop(0, 4, feed, 0)
        store(mv.at[m], momentum_next.at[m])
    received(zs)
    total = squares[0]
    for d in range(1, 8):
        total = total + squares[d]
    inverse = lax.rsqrt(total / D + epsilon_sq)
    lane = lax.broadcasted_iota(jnp.int32, (16, RANK), 1)
    sub = lax.broadcasted_iota(jnp.int32, (16, RANK), 0)
    for m in range(2):
        inv = jnp.concatenate([inverse[4 * m + j:4 * m + j + 1] for j in range(4)], axis=1)
        orth[m] = orth[m] * inv
        pick = jnp.sum(jnp.where(lane == pc.f * 16 + sub, inv, 0.0), axis=1, keepdims=True)
        bnext[m] = right[m, pl.ds(pl.multiple_of(pc.f * 16, 16), 16), :] * pick
        store(bnext.at[m], basis_next.at[m])

        def direction(j, carry, m=m):
            cols = pl.ds(pl.multiple_of(j * 256, 256), 256)
            out = math.sqrt(D / RANK) * dot(orth[m], right[m, :, cols], 1, 0, HIGH)
            upd[m, :, cols] = out.astype(jnp.bfloat16)
            return carry

        lax.fori_loop(0, 4, direction, 0)
        store(upd.at[m], update.at[m])
    for cp in stores:
        cp.wait()
    pc.drain()


def place_kernel(update, momentum_next, basis_next, update_out, momentum_out, basis_out, uv, mv, bv, sem):
    parts = [(basis_next, bv, basis_out, pl.ds(0, 16))]
    for i in range(2):
        parts.append((momentum_next, mv, momentum_out, pl.ds(128 * i, 128)))
        parts.append((update, uv, update_out, pl.ds(128 * i, 128)))
    loads, stores = [], []
    for m in range(2):
        for src, held, dst, rows in parts:
            i = len(loads)
            loads.append(pltpu.make_async_copy(src.at[m, rows], held.at[m, rows], sem.at[2 * i]))
            stores.append(pltpu.make_async_copy(held.at[m, rows], dst.at[m, rows], sem.at[2 * i + 1]))
    for cp in loads:
        cp.start()
    for a, b in zip(loads, stores):
        a.wait()
        b.start()
    for cp in stores:
        cp.wait()


def shards(gradient, momentum, right_basis):
    vmem = pl.BlockSpec(memory_space=pltpu.VMEM)
    anywhere = pl.BlockSpec(memory_space=pl.ANY)
    shape = lambda s: jax.ShapeDtypeStruct(s, F32)
    buf = lambda *s: pltpu.VMEM(s, F32)
    half = pltpu.VMEM((2, 256, 1024), jnp.bfloat16)
    out_shape = (jax.ShapeDtypeStruct((2, 256, 1024), jnp.bfloat16), shape((2, 256, 1024)), shape((2, 16, 1024)))
    n = 208
    results = pl.pallas_call(
        kernel,
        out_shape=out_shape,
        in_specs=[anywhere, anywhere, vmem],
        out_specs=[anywhere] * 3,
        scratch_shapes=[
            half, buf(2, 256, 1024), half, buf(2, 16, 1024),
            buf(2, 256, 1024), buf(256, 1024), buf(4, 4, 2, 16, 1024),
            buf(4, 8, 64, 128), buf(2, 4, 32, 128), buf(6, 4, 64, 128), buf(2, 8, 64, 256), buf(RANK, RANK),
            buf(4, 4, 2, 40, 128), buf(2, 2, 2, 40, 128), buf(2, 2, 4, 40, 128), buf(2, 4, 40, 128), buf(2, 3, 40, 128),
            buf(8, 16, 128), buf(7, 16, 128), buf(8, 16, 128), buf(4, 4, 2, 40, 128),
            buf(2, 4, 4, 2, 8, 1024), buf(2, 2, 2, 2, 8, 1024), buf(2, 2, 2, 4, 8, 1024), buf(2, 2, 4, 8, 1024), buf(2, 2, 3, 8, 1024),
            buf(2, 2, 4, 4, 2, 8, 1024), buf(2, 2, 4, 64, 256),
            buf(10, 128, 128), buf(6, 128, 128), buf(2, RANK, RANK),
            buf(2, RANK, 1024), buf(2, 256, RANK), buf(2, 8, RANK), buf(8, 8, 128),
            pltpu.SemaphoreType.DMA((n,)), pltpu.SemaphoreType.DMA((n,)), pltpu.SemaphoreType.DMA((10,)),
        ],
        compiler_params=pltpu.CompilerParams(
            collective_id=0, has_side_effects=True, vmem_limit_bytes=VMEM_BYTES
        ),
        name="dion",
    )(gradient, momentum, right_basis)
    return pl.pallas_call(
        place_kernel,
        out_shape=out_shape,
        in_specs=[anywhere] * 3,
        out_specs=[anywhere] * 3,
        scratch_shapes=[half, buf(2, 256, 1024), buf(2, 16, 1024), pltpu.SemaphoreType.DMA((20,))],
        compiler_params=pltpu.CompilerParams(vmem_limit_bytes=VMEM_BYTES),
        name="place",
    )(*results)


def solution(mesh):
    placed = (P(None, "fsdp", "tp"), P(None, "fsdp", "tp"), P(None, "fsdp", "tp"))
    return jax.shard_map(
        shards,
        mesh=mesh,
        in_specs=placed,
        out_specs=placed,
        check_vma=False,
    )
```

```python
import math

import jax
import jax.numpy as jnp
from jax import lax
from jax.experimental import pallas as pl
from jax.experimental.pallas import tpu as pltpu
from jax.sharding import PartitionSpec as P

D = 8192
RANK = 512
momentum_decay = 0.8
epsilon_sq = 1e-06
MESH = pl.DeviceIdType.MESH
F32 = jnp.float32
HIGH = lax.Precision.HIGH
HIGHEST = lax.Precision.HIGHEST
VMEM_BYTES = 56 * 1024 * 1024


def dot(a, b, ca, cb, precision):
    return lax.dot_general(
        a, b, (((ca,), (cb,)), ((), ())), precision=precision, preferred_element_type=F32
    )


class Place:
    def __init__(self, send_sem, recv_sem):
        f = lax.axis_index("fsdp")
        self.f = f
        self.z = lax.axis_index("tp")
        self.c = lax.rem(f, 2)
        self.x = lax.rem(f // 2, 4)
        self.y = f // 8
        self.send_sem, self.recv_sem = send_sem, recv_sem
        self.count = 0
        self.open = []

    def dev(self, y=None, x=None, z=None, c=None):
        y = self.y if y is None else y
        x = self.x if x is None else x
        c = self.c if c is None else c
        z = self.z if z is None else z
        return ((y * 4 + x) * 2 + c, z)

    def partner(self):
        return self.dev(c=1 - self.c)

    def xs(self, d):
        return lax.rem(self.x + d, 4)

    def ys(self, d):
        return lax.rem(self.y + d, 4)

    def zs(self, d):
        return lax.rem(self.z + d, 8)

    def reserve(self, n):
        i = self.count
        self.count += n
        assert self.count <= self.send_sem.shape[0]
        return i

    def copy(self, src, dst, to, recv=None):
        i = self.reserve(1)
        cp = pltpu.make_async_remote_copy(
            src_ref=src,
            dst_ref=dst,
            send_sem=self.send_sem.at[i],
            recv_sem=self.recv_sem.at[i if recv is None else recv],
            device_id=to,
            device_id_type=MESH,
        )
        cp.start()
        self.open.append(cp)
        return cp

    def barrier(self, peers):
        sem = pltpu.get_barrier_semaphore()
        for p in peers:
            pl.semaphore_signal(sem, inc=1, device_id=p, device_id_type=MESH)
        pl.semaphore_wait(sem, len(peers))

    def drain(self, keep=0):
        n = len(self.open) - keep
        for cp in self.open[:n]:
            cp.wait_send()
        self.open = self.open[n:]


def received(copies):
    for cp in copies:
        cp.wait_recv()


class Gather:
    def __init__(self, pc, buf):
        self.pc, self.buf = pc, buf

    def first(self):
        pc, buf = self.pc, self.buf
        self.one = []
        for d in (2, 1, 3):
            a, b = buf.at[pc.y, pc.x, 0], buf.at[pc.y, pc.x, 1]
            self.one.append(pc.copy(a, a, pc.dev(x=pc.xs(d))))
            self.one.append(pc.copy(b, b, pc.dev(y=pc.ys(d))))

    def second(self):
        pc, buf = self.pc, self.buf
        received(self.one)
        self.two, self.passed = {}, []
        for d in (1, 3):
            a, b = buf.at[pc.y, :, 0], buf.at[:, pc.x, 1]
            self.two[d] = (pc.copy(a, a, pc.dev(y=pc.ys(d))), pc.copy(b, b, pc.dev(x=pc.xs(d))))

    def relay(self, d):
        pc, buf = self.pc, self.buf
        received(self.two[d])
        half = pl.ds(0, 2) if d == 1 else pl.ds(2, 2)
        a, b = buf.at[pc.ys(4 - d), half, 0], buf.at[half, pc.xs(4 - d), 1]
        self.passed.append(pc.copy(a, a, pc.dev(y=pc.ys(d))))
        self.passed.append(pc.copy(b, b, pc.dev(x=pc.xs(d))))

    def finish(self):
        received(self.passed)


class Scatter:
    def __init__(self, pc, buf, rel, r1, acc, r2):
        self.pc, self.buf, self.rel, self.r1, self.acc, self.r2 = pc, buf, rel, r1, acc, r2

    def first(self):
        pc, buf, rel = self.pc, self.buf, self.rel
        self.halves = []
        for i, d in enumerate((1, 3)):
            half = pl.ds(2 * i, 2)
            self.halves.append(pc.copy(buf.at[pc.ys(2), half, 0], rel.at[0, i], pc.dev(y=pc.ys(d))))
            self.halves.append(pc.copy(buf.at[half, pc.xs(2), 1], rel.at[1, i], pc.dev(x=pc.xs(d))))

    def middle(self):
        pc, buf, rel, r1 = self.pc, self.buf, self.rel, self.r1
        received(self.halves)
        self.one = []
        for i, d in enumerate((1, 3)):
            half = pl.ds(2 * i, 2)
            buf[pc.ys(d), half, 0] = buf[pc.ys(d), half, 0] + rel[0, i]
            self.one.append(pc.copy(buf.at[pc.ys(d), :, 0], r1.at[0, i], pc.dev(y=pc.ys(d))))
            buf[half, pc.xs(d), 1] = buf[half, pc.xs(d), 1] + rel[1, i]
            self.one.append(pc.copy(buf.at[:, pc.xs(d), 1], r1.at[1, i], pc.dev(x=pc.xs(d))))

    def second(self):
        pc, buf, r1, acc = self.pc, self.buf, self.r1, self.acc
        received(self.one)
        acc[0] = buf[pc.y, :, 0] + r1[0, 0] + r1[0, 1]
        acc[1] = buf[:, pc.x, 1] + r1[1, 0] + r1[1, 1]
        self.two = []
        for d in (2, 1, 3):
            self.two.append(pc.copy(acc.at[0, pc.xs(d)], self.r2.at[0, d - 1], pc.dev(x=pc.xs(d))))
            self.two.append(pc.copy(acc.at[1, pc.ys(d)], self.r2.at[1, d - 1], pc.dev(y=pc.ys(d))))

    def finish(self):
        pc, acc, r2 = self.pc, self.acc, self.r2
        received(self.two)
        own0 = acc[0, pc.x] + r2[0, 0] + r2[0, 1] + r2[0, 2]
        own1 = acc[1, pc.y] + r2[1, 0] + r2[1, 1] + r2[1, 2]
        return own0, own1


def factor_block(load, tick):
    groups = 16
    a = [load(r) for r in range(groups)]
    lane = lax.broadcasted_iota(jnp.int32, (8, 128), 1)
    sub = lax.broadcasted_iota(jnp.int32, (8, 128), 0)
    out = [None] * groups

    def column(v, j):
        return jnp.broadcast_to(v[:, j:j + 1], (8, 128))

    def spread(v, i):
        return jnp.broadcast_to(v[i:i + 1, :], (8, 128))

    def recip(v):
        return pl.reciprocal(v, approx=True)

    for q in range(32):
        r0, s0, j0 = q // 2, 4 * (q % 2), 4 * q
        end = 4 * (r0 // 4) + 4
        rows = [spread(a[r0], s0 + s) for s in range(4)]
        cols = [column(a[r0], j0 + t) for t in range(4)]
        p = {(s, t): spread(cols[t], s0 + s) for s in range(4) for t in range(s, 4)}
        inside = (lane >= j0) & (lane < j0 + 4)
        sc = [lax.rsqrt(p[s, s]) for s in range(4)]
        v = [jnp.where(inside, jnp.where(lane == j0 + s, 1.0, 0.0), rows[s]) * sc[s] for s in range(4)]
        r = {(s, t): p[s, t] * (sc[s] * sc[t]) for s in range(4) for t in range(s + 1, 4)}
        l10, l20, l30 = r[0, 1], r[0, 2], r[0, 3]
        u11, u22, u33 = 1.0 - l10 * l10, 1.0 - l20 * l20, 1.0 - l30 * l30
        u12, u13, u23 = r[1, 2] - l10 * l20, r[1, 3] - l10 * l30, r[2, 3] - l20 * l30
        v22, v23, v33 = u11 * u22 - u12 * u12, u11 * u23 - u12 * u13, u11 * u33 - u13 * u13
        w33 = v22 * v33 - v23 * v23
        i1, i2, i3 = recip(u11), recip(v22), recip(w33)
        l21, l31, l32 = u12 * i1, u13 * i1, v23 * i2
        d1, d2, d3 = i1, u11 * i2, (u11 * v22) * i3
        n10, n21, n32 = -l10, -l21, -l32
        n20 = l21 * l10 - l20
        n31 = l32 * l21 - l31
        n30 = l31 * l10 - l30 - l32 * n20
        n = [[None] * 4, [n10], [n20, n21], [n30, n31, n32]]
        m = {}
        e1 = d1 * n10
        e20, e21 = d2 * n20, d2 * n21
        m[0, 0] = (1.0 + e1 * n10 + e20 * n20) + d3 * (n30 * n30)
        m[0, 1] = (e1 + e20 * n21) + d3 * (n30 * n31)
        m[0, 2] = e20 + d3 * (n30 * n32)
        m[0, 3] = d3 * n30
        m[1, 1] = (d1 + e21 * n21) + d3 * (n31 * n31)
        m[1, 2] = e21 + d3 * (n31 * n32)
        m[1, 3] = d3 * n31
        m[2, 2] = d2 + d3 * (n32 * n32)
        m[2, 3] = d3 * n32
        m[3, 3] = d3
        w = []
        for s in range(4):
            t = [m[min(s, t), max(s, t)] * v[t] for t in range(4)]
            w.append(((t[0] + t[1]) + (t[2] + t[3])) * sc[s])
        f = [None, d1 * lax.rsqrt(d1), d2 * lax.rsqrt(d2), d3 * lax.rsqrt(d3)]
        done = [v[0]]
        for s in range(1, 4):
            t = v[s]
            for k in range(s):
                t = t + n[s][k] * v[k]
            done.append(f[s] * t)
        o = done[0]
        for s in range(1, 4):
            o = jnp.where(sub == s0 + s, done[s], o)
        out[r0] = o if s0 == 0 else jnp.where(sub < 4, out[r0], o)
        for g in range(r0 if s0 == 0 else r0 + 1, end):
            if g > r0:
                cols = [column(a[g], j0 + t) for t in range(4)]
            t = [cols[t] * w[t] for t in range(4)]
            a[g] = jnp.where(inside, 0.0, a[g]) - ((t[0] + t[1]) + (t[2] + t[3]))
        if q % 8 == 7 and end < groups:
            new = jnp.concatenate(out[end - 4:end], axis=0)
            lanes = lax.broadcasted_iota(jnp.int32, (32, 128), 1)
            over = lanes > 8 * end - 32 + lax.broadcasted_iota(jnp.int32, (32, 128), 0)
            right = jnp.where(lanes >= 8 * end, new, 0.0)
            step = dot(right, jnp.where(over, right, new), 0, 0, HIGHEST)
            done_lanes = (lane >= 8 * end - 32) & (lane < 8 * end)
            for g in range(end, groups):
                a[g] = jnp.where(done_lanes, 0.0, a[g]) - step[8 * g:8 * g + 8]
        tick(q)
    return out


def kernel(
    grad, mom, rb, update, momentum_next, basis_next,
    gv, mv, upd, usend, urecv, mrecv, bown, bsend, brecv, blend, blend_send, basis, lpart, lrel, lrecv, left, perm,
    gbuf, grel, gr1, gacc, gr2, zsrc, zpart, zfull, gfull,
    wbuf, wrel, wr1, wacc, wr2, wall,
    work, ybuf, tri, right, orth, squares,
    send_sem, recv_sem, local_sem,
):
    pc = Place(send_sem, recv_sem)
    c, x, y, z = pc.c, pc.x, pc.y, pc.z
    loads = []
    for i, m in enumerate((1 - c, c)):
        loads.append(
            (
                pltpu.make_async_copy(mom.at[m], mv.at[m], local_sem.at[2 * i]),
                pltpu.make_async_copy(grad.at[m], gv.at[m], local_sem.at[2 * i + 1]),
            )
        )
        for cp in loads[i]:
            cp.start()
    peers = [pc.partner()]
    peers += [pc.dev(x=pc.xs(d), c=m) for d in (1, 2, 3) for m in (0, 1)]
    peers += [pc.dev(y=pc.ys(d), c=m) for d in (1, 2, 3) for m in (0, 1)]
    peers += [pc.dev(z=pc.zs(d)) for d in range(1, 8)]
    pc.barrier(peers)

    first = pc.reserve(6)
    slot = lambda d, h: first + 2 * (d - 1) + h
    for d in (1, 3, 2):
        to_y, to_x = lax.rem(y + d * c, 4), lax.rem(x + d * (1 - c), 4)
        for m in range(2):
            pc.copy(rb.at[m], basis.at[y, x, c], pc.dev(y=to_y, x=to_x, c=m), recv=slot(d, c))
    basis_swap = pc.copy(rb.at[1 - c], basis.at[y, x, c], pc.partner())
    basis[y, x, c] = rb[c]
    for cp in loads[0]:
        cp.wait()
    blend_send[...] = mv[1 - c] + gv[1 - c].astype(F32)
    blend_swap = pc.copy(blend_send, blend.at[c], pc.partner())
    for cp in loads[1]:
        cp.wait()
    blend[c] = mv[c] + gv[c].astype(F32)
    basis_swap.wait_recv()
    for d in (1, 3, 2):
        for h in range(2):
            pltpu.make_async_remote_copy(
                src_ref=rb.at[0],
                dst_ref=basis.at[y, x, h],
                send_sem=send_sem.at[slot(d, h)],
                recv_sem=recv_sem.at[slot(d, h)],
                device_id=pc.partner(),
                device_id_type=MESH,
            ).wait_recv()
    gather = Gather(pc, basis)
    gather.one = []
    gather.second()
    at = lax.broadcasted_iota(jnp.int32, (RANK, RANK), 0)
    group, half = at // 128, (at // 64) % 2
    index, low = (at // 16) % 4, at % 16
    py = jnp.where(half == 0, (y + group) % 4, index)
    px = jnp.where(half == 0, index, (x + group) % 4)
    rank = ((py * 4 + px) * 2 + half) * 16 + low
    perm[...] = jnp.where(lax.broadcasted_iota(jnp.int32, (RANK, RANK), 1) == rank, 1.0, 0.0)
    blend_swap.wait_recv()
    sums_in, opposite = [], {}

    def to_z(d, e):
        i = e - 1 if e < 4 else e - 2
        sums_in.append(pc.copy(lpart.at[d, pc.zs(e)], lrecv.at[i, d], pc.dev(z=pc.zs(e))))

    def to_z_far(d):
        received(opposite[d])
        for i, e in enumerate((3, 5)):
            rows = pl.ds(32 * i, 32)
            lpart[d, pc.zs(e), rows] = lpart[d, pc.zs(e), rows] + lrel[i, d]
            to_z(d, e)

    before = None
    for d in (0, 3, 1, 2):
        if d == 2:
            gather.finish()
        elif d:
            gather.relay(4 - d)
        rows = jnp.concatenate(
            [basis[pc.ys(d), :, 0].reshape(64, 1024), basis[:, pc.xs(d), 1].reshape(64, 1024)], axis=0
        )
        part = dot(blend[...].reshape(512, 1024), rows, 1, 1, HIGH)
        lpart[d] = part.reshape(8, 64, 128)
        opposite[d] = []
        for i, e in enumerate((1, 7)):
            src = lpart.at[d, pc.zs(4), pl.ds(32 * i, 32)]
            opposite[d].append(pc.copy(src, lrel.at[i, d], pc.dev(z=pc.zs(e))))
        if before is not None:
            to_z_far(before)
        for e in (2, 6, 1, 7):
            to_z(d, e)
        before = d
    to_z_far(before)
    received(sums_in)
    own = []
    for d in range(4):
        s = lpart[d, z]
        for e in range(6):
            s = s + lrecv[e, d]
        own.append(s)
    own = dot(jnp.concatenate(own, axis=1), perm[...], 1, 0, HIGHEST)
    for q in range(2):
        left[q, z] = own[:, 256 * q:256 * q + 256]

    def ring(step):
        up, down = pc.dev(z=pc.zs(1)), pc.dev(z=pc.zs(7))
        copies = []
        for q in range(2):
            a, b = left.at[q, pc.zs(9 - step)], left.at[q, pc.zs(step - 1)]
            if step == 4:
                a, b = a.at[pl.ds(0, 32)], b.at[pl.ds(32, 32)]
            copies += [pc.copy(a, a, up), pc.copy(b, b, down)]
        return copies

    blocks = []
    for i in range(4):
        row = dot(own[:, 128 * i:128 * i + 128], own[:, :128 * i + 128], 0, 0, HIGHEST)
        blocks += [row[:, 128 * j:128 * j + 128] for j in range(i + 1)]
    gbuf[...] = jnp.concatenate(blocks, axis=0).reshape(4, 4, 2, 40, 128)
    gscatter = Scatter(pc, gbuf, grel, gr1, gacc, gr2)
    gscatter.first()
    lefts = ring(1)
    gscatter.middle()
    gscatter.second()
    received(lefts)
    lefts = ring(2)
    own0, own1 = gscatter.finish()
    zsrc[0:5] = jnp.concatenate([own0, own1], axis=0).reshape(5, 16, 128)
    zsrc[5:8] = jnp.zeros((3, 16, 128), F32)
    zs = []
    for d in (4, 3, 5, 2, 6, 1, 7):
        zs.append(pc.copy(zsrc.at[pc.zs(d)], zpart.at[d - 1], pc.dev(z=pc.zs(d))))
    received(lefts)
    lefts = ring(3)
    received(zs)
    total = zsrc[z]
    for d in range(7):
        total = total + zpart[d]
    zfull[z] = total
    zs = []
    for d in (4, 3, 5, 2, 6, 1, 7):
        zs.append(pc.copy(zfull.at[z], zfull.at[z], pc.dev(z=pc.zs(d))))
    received(lefts)
    lefts = ring(4)
    received(zs)
    gfull[y, x] = zfull[0:5].reshape(2, 40, 128)
    ggather = Gather(pc, gfull)
    ggather.first()
    received(lefts)
    ggather.second()
    wscatter, wgather = [], []
    for q in range(2):
        for i in range(2):
            lt = left[q, :, :, 128 * i:128 * i + 128].reshape(RANK, 128)
            part = dot(lt, blend[...].reshape(512, 1024), 0, 0, HIGH)
            wbuf[q, 2 * i:2 * i + 2] = part.reshape(2, 4, 2, 8, 1024)
        wscatter.append(Scatter(pc, wbuf.at[q], wrel.at[q], wr1.at[q], wacc.at[q], wr2.at[q]))
        wscatter[q].first()
        if q == 0:
            ggather.relay(1)
            ggather.relay(3)
        wgather.append(Gather(pc, wall.at[q]))
    pc.drain(keep=16)
    ggather.finish()

    def w_gather(q):
        o0, o1 = wscatter[q].finish()
        wall[q, y, x, 0] = o0
        wall[q, y, x, 1] = o1
        wgather[q].first()

    def w_relay(q):
        wgather[q].relay(1)
        wgather[q].relay(3)

    def w_step1():
        wscatter[0].middle()
        wscatter[1].middle()

    def w_step2():
        wscatter[0].second()

    def w_step3():
        wscatter[1].second()
        w_gather(0)

    def w_step4():
        w_gather(1)
        wgather[0].second()

    def w_step5():
        wgather[1].second()
        w_relay(0)

    def w_step6():
        w_relay(1)

    def w_step7():
        wgather[0].finish()
        wgather[1].finish()
        pending.extend(raw_job(i, j) for j in range(4) for i in range(3))
        pending.extend(feed_job(h, j) for j in range(4) for h in range(2))

    def w_part(q, cols):
        return wall[q, :, :, :, :, cols].reshape(256, 256)

    def raw_job(i, j):
        def job():
            cols = pl.ds(256 * j, 256)
            n = 128 * (i + 1)
            wj = jnp.concatenate([w_part(q, cols) for q in range(2 if i > 1 else 1)], axis=0)[:n]
            right[128 * i:128 * i + 128, cols] = dot(tri[128 * i:128 * i + 128, 0:n], wj, 1, 0, HIGH)

        return job

    def feed_job(h, j):
        def job():
            cols = pl.ds(256 * j, 256)
            back = dot(orth[h, :, 0:384], right[0:384, cols], 1, 0, HIGH)
            blend[h, :, cols] = blend[h, :, cols] - (1.0 - momentum_decay) * back

        return job

    def orth_job(k, h):
        def job():
            n = 128 * (k + 1)
            rows = jnp.concatenate([left[q, 4 * h:4 * h + 4].reshape(256, 256) for q in range(2)], axis=1)[:, :n]
            orth[h, :, 128 * k:n] = dot(rows, tri[128 * k:n, 0:n], 1, 1, HIGH)

        return job

    events = {
        (0, 8): w_step1, (0, 28): w_step2, (1, 6): w_step3, (1, 20): w_step4, (2, 4): w_step5, (2, 16): w_step6,
        (3, 12): w_step7,
    }
    flat = gfull[...].reshape(1280, 128)
    for b in range(10):
        work[b] = flat[128 * b:128 * b + 128]
    at = lambda i, j: i * (i + 1) // 2 + j
    yat = lambda i, j: i * (i - 1) // 2 + j
    rowi = lax.broadcasted_iota(jnp.int32, (128, 128), 0)
    coli = lax.broadcasted_iota(jnp.int32, (128, 128), 1)
    pending = []

    def tri_row(k, inv):
        for j in range(k):
            tri[128 * k:128 * k + 128, 128 * j:128 * j + 128] = dot(inv, ybuf[yat(k, j)], 1, 0, HIGHEST)
        tri[128 * k:128 * k + 128, 128 * k:128 * k + 128] = inv

    def later(k, inv):
        def solve(i):
            work[at(i, k)] = dot(work[at(i, k)], inv, 1, 1, HIGHEST)

        def trail(i, j):
            work[at(i, j)] = work[at(i, j)] - dot(work[at(i, k)], work[at(j, k)], 1, 1, HIGHEST)

        def inverse(i, j):
            new = dot(work[at(i, k)], tri[128 * k:128 * k + 128, 128 * j:128 * j + 128], 1, 0, HIGHEST)
            ybuf[yat(i, j)] = -new if j == k else ybuf[yat(i, j)] - new

        jobs = [lambda: tri_row(k, inv)]
        for i in range(k + 2, 4):
            jobs.append(lambda i=i: solve(i))
        for i in range(k + 2, 4):
            for j in range(k + 1, i + 1):
                jobs.append(lambda i=i, j=j: trail(i, j))
        for i in range(k + 1, 4):
            for j in range(k + 1):
                jobs.append(lambda i=i, j=j: inverse(i, j))
        return jobs + [orth_job(k, h) for h in range(2)]

    for k in range(4):

        def tick(q, k=k):
            if (k, q) in events:
                events[k, q]()
            if pending and q >= 1:
                pending.pop(0)()

        rows = factor_block(lambda r: work[at(k, k), 8 * r:8 * r + 8, :], tick)
        while pending:
            pending.pop(0)()
        inv = jnp.where(rowi >= coli, jnp.concatenate(rows, axis=0), 0.0)
        if k < 3:
            below = dot(work[at(k + 1, k)], inv, 1, 1, HIGHEST)
            work[at(k + 1, k)] = below
            work[at(k + 1, k + 1)] = work[at(k + 1, k + 1)] - dot(below, below, 1, 1, HIGHEST)
            pending = later(k, inv)
        else:
            tri_row(k, inv)


    def columns(body):
        def step(j, carry):
            body(pl.ds(pl.multiple_of(j * 256, 256), 256))
            return carry

        lax.fori_loop(0, 4, step, 0)

    def raw_end(cols):
        wj = jnp.concatenate([w_part(q, cols) for q in range(2)], axis=0)
        new = dot(tri[384:, :], wj, 1, 0, HIGH)
        right[384:, cols] = new

    columns(raw_end)
    fold = right[:, 0:128] * right[:, 0:128]
    for j in range(1, 8):
        fold = fold + right[:, 128 * j:128 * j + 128] * right[:, 128 * j:128 * j + 128]
    sums = dot(jnp.ones((8, 128), F32), fold, 1, 1, HIGHEST)
    squares[z] = jnp.concatenate([sums[0:1, 128 * j:128 * j + 128] for j in range(4)] * 2, axis=0)
    zs = []
    for d in (4, 3, 5, 2, 6, 1, 7):
        zs.append(pc.copy(squares.at[z], squares.at[z], pc.dev(z=pc.zs(d))))
    stores = []

    def store(src, dst):
        cp = pltpu.make_async_copy(src, dst, local_sem.at[4 + len(stores)])
        cp.start()
        stores.append(cp)

    for h in range(2):
        orth_job(3, h)()

    def feed(h):
        def part(cols):
            back = dot(orth[h, :, 384:], right[384:, cols], 1, 0, HIGH)
            blend[h, :, cols] = blend[h, :, cols] - (1.0 - momentum_decay) * back

        columns(part)

    feed(1 - c)
    momentum_swap = pc.copy(blend.at[1 - c], mrecv, pc.partner())
    feed(c)
    store(blend.at[c], momentum_next.at[c])
    pc.drain(keep=8)
    received(zs)
    total = squares[0]
    for d in range(1, 8):
        total = total + squares[d]
    inverse = lax.rsqrt(total / D + epsilon_sq)
    inv = jnp.concatenate([inverse[j:j + 1] for j in range(4)], axis=1)
    lane = lax.broadcasted_iota(jnp.int32, (16, RANK), 1)
    sub = lax.broadcasted_iota(jnp.int32, (16, RANK), 0)

    def basis_rows(f):
        pick = jnp.sum(jnp.where(lane == f * 16 + sub, inv, 0.0), axis=1, keepdims=True)
        return right[pl.ds(pl.multiple_of(f * 16, 16), 16), :] * pick

    other = pc.f + 1 - 2 * c
    bsend[...] = basis_rows(other)
    basis_out_swap = pc.copy(bsend, brecv, pc.partner())
    bown[...] = basis_rows(pc.f)
    store(bown, basis_next.at[c])
    for h in range(2):
        orth[h] = orth[h] * (math.sqrt(D / RANK) * inv)
    update_swaps = []
    for i in range(2):
        for j in range(2):
            cols = pl.ds(512 * i + 256 * j, 256)
            usend[i, :, 256 * j:256 * j + 256] = dot(orth[1 - c], right[:, cols], 1, 0, HIGH)
        update_swaps.append(pc.copy(usend.at[i], urecv.at[i], pc.partner()))
    momentum_swap.wait_recv()
    store(mrecv, momentum_next.at[1 - c])

    def direction(cols):
        upd[c, :, cols] = dot(orth[c], right[:, cols], 1, 0, HIGH).astype(jnp.bfloat16)

    columns(direction)
    store(upd.at[c], update.at[c])
    basis_out_swap.wait_recv()
    store(brecv, basis_next.at[1 - c])
    for i in range(2):
        update_swaps[i].wait_recv()
        upd[1 - c, :, 512 * i:512 * i + 512] = urecv[i].astype(jnp.bfloat16)
    store(upd.at[1 - c], update.at[1 - c])
    for cp in stores:
        cp.wait()
    pc.drain()


def place_kernel(update, momentum_next, basis_next, update_out, momentum_out, basis_out, uv, mv, bv, sem):
    parts = [(basis_next, bv, basis_out, pl.ds(0, 16))]
    for i in range(2):
        parts.append((momentum_next, mv, momentum_out, pl.ds(128 * i, 128)))
        parts.append((update, uv, update_out, pl.ds(128 * i, 128)))
    loads, stores = [], []
    for m in range(2):
        for src, held, dst, rows in parts:
            i = len(loads)
            loads.append(pltpu.make_async_copy(src.at[m, rows], held.at[m, rows], sem.at[2 * i]))
            stores.append(pltpu.make_async_copy(held.at[m, rows], dst.at[m, rows], sem.at[2 * i + 1]))
    for cp in loads:
        cp.start()
    for a, b in zip(loads, stores):
        a.wait()
        b.start()
    for cp in stores:
        cp.wait()


def shards(gradient, momentum, right_basis):
    vmem = pl.BlockSpec(memory_space=pltpu.VMEM)
    anywhere = pl.BlockSpec(memory_space=pl.ANY)
    shape = lambda s: jax.ShapeDtypeStruct(s, F32)
    buf = lambda *s: pltpu.VMEM(s, F32)
    half = pltpu.VMEM((2, 256, 1024), jnp.bfloat16)
    out_shape = (jax.ShapeDtypeStruct((2, 256, 1024), jnp.bfloat16), shape((2, 256, 1024)), shape((2, 16, 1024)))
    n = 208
    results = pl.pallas_call(
        kernel,
        out_shape=out_shape,
        in_specs=[anywhere, anywhere, vmem],
        out_specs=[anywhere] * 3,
        scratch_shapes=[
            half, buf(2, 256, 1024), half, buf(2, 256, 512), buf(2, 256, 512), buf(256, 1024),
            buf(16, 1024), buf(16, 1024), buf(16, 1024),
            buf(2, 256, 1024), buf(256, 1024), buf(4, 4, 2, 16, 1024),
            buf(4, 8, 64, 128), buf(2, 4, 32, 128), buf(6, 4, 64, 128), buf(2, 8, 64, 256), buf(RANK, RANK),
            buf(4, 4, 2, 40, 128), buf(2, 2, 2, 40, 128), buf(2, 2, 4, 40, 128), buf(2, 4, 40, 128), buf(2, 3, 40, 128),
            buf(8, 16, 128), buf(7, 16, 128), buf(8, 16, 128), buf(4, 4, 2, 40, 128),
            buf(2, 4, 4, 2, 8, 1024), buf(2, 2, 2, 2, 8, 1024), buf(2, 2, 2, 4, 8, 1024), buf(2, 2, 4, 8, 1024), buf(2, 2, 3, 8, 1024),
            buf(2, 4, 4, 2, 8, 1024),
            buf(10, 128, 128), buf(6, 128, 128), buf(RANK, RANK),
            buf(RANK, 1024), buf(2, 256, RANK), buf(8, 8, 128),
            pltpu.SemaphoreType.DMA((n,)), pltpu.SemaphoreType.DMA((n,)), pltpu.SemaphoreType.DMA((10,)),
        ],
        compiler_params=pltpu.CompilerParams(
            collective_id=0, has_side_effects=True, vmem_limit_bytes=VMEM_BYTES
        ),
        name="dion",
    )(gradient, momentum, right_basis)
    return pl.pallas_call(
        place_kernel,
        out_shape=out_shape,
        in_specs=[anywhere] * 3,
        out_specs=[anywhere] * 3,
        scratch_shapes=[half, buf(2, 256, 1024), buf(2, 16, 1024), pltpu.SemaphoreType.DMA((20,))],
        compiler_params=pltpu.CompilerParams(vmem_limit_bytes=VMEM_BYTES),
        name="place",
    )(*results)


def solution(mesh):
    placed = (P(None, "fsdp", "tp"), P(None, "fsdp", "tp"), P(None, "fsdp", "tp"))
    return jax.shard_map(
        shards,
        mesh=mesh,
        in_specs=placed,
        out_specs=placed,
        check_vma=False,
    )
```

```python
import math

import jax
import jax.numpy as jnp
from jax import lax
from jax.experimental import pallas as pl
from jax.experimental.pallas import tpu as pltpu
from jax.sharding import PartitionSpec as P

D = 8192
RANK = 512
momentum_decay = 0.8
epsilon_sq = 1e-06
MESH = pl.DeviceIdType.MESH
ALL = slice(None)
F32 = jnp.float32
HIGH = lax.Precision.HIGH
HIGHEST = lax.Precision.HIGHEST
VMEM_BYTES = 56 * 1024 * 1024


def dot(a, b, ca, cb, precision):
    return lax.dot_general(
        a, b, (((ca,), (cb,)), ((), ())), precision=precision, preferred_element_type=F32
    )


class Loc:
    def __init__(self, ref, *index):
        self.ref, self.index = ref, index

    def __call__(self):
        return self.ref.at[self.index]


class Copy:
    def __init__(self, place, src, dst, send, recv, to):
        self.place, self.src, self.dst, self.send, self.recv, self.to = place, src, dst, send, recv, to

    def make(self):
        src = self.src() if isinstance(self.src, Loc) else self.src
        dst = self.dst() if isinstance(self.dst, Loc) else self.dst
        return pltpu.make_async_remote_copy(
            src_ref=src,
            dst_ref=dst,
            send_sem=self.place.send_sem.at[self.send],
            recv_sem=self.place.recv_sem.at[self.recv],
            device_id=self.to,
            device_id_type=MESH,
        )

    def wait_send(self):
        self.make().wait_send()

    def wait_recv(self):
        self.make().wait_recv()


class Place:
    def __init__(self, send_sem, recv_sem):
        f = lax.axis_index("fsdp")
        self.f = f
        self.z = lax.axis_index("tp")
        self.c = lax.rem(f, 2)
        self.x = lax.rem(f // 2, 4)
        self.y = f // 8
        self.at_x = [lax.rem(self.x + d, 4) for d in range(4)]
        self.at_y = [lax.rem(self.y + d, 4) for d in range(4)]
        self.at_z = [lax.rem(self.z + d, 8) for d in range(8)]
        self.to_x = [self.dev(x=v) for v in self.at_x]
        self.to_y = [self.dev(y=v) for v in self.at_y]
        self.to_z = [self.dev(z=v) for v in self.at_z]
        self.send_sem, self.recv_sem = send_sem, recv_sem
        self.count = 0
        self.open = []

    def dev(self, y=None, x=None, z=None, c=None):
        y = self.y if y is None else y
        x = self.x if x is None else x
        c = self.c if c is None else c
        z = self.z if z is None else z
        return ((y * 4 + x) * 2 + c, z)

    def partner(self):
        return self.dev(c=1 - self.c)

    def xs(self, d):
        return self.at_x[d]

    def ys(self, d):
        return self.at_y[d]

    def zs(self, d):
        return self.at_z[d % 8]

    def reserve(self, n):
        i = self.count
        self.count += n
        assert self.count <= self.send_sem.shape[0]
        return i

    def copy(self, src, dst, to, recv=None):
        i = self.reserve(1)
        cp = Copy(self, src, dst, i, i if recv is None else recv, to)
        cp.make().start()
        self.open.append(cp)
        return cp

    def barrier(self, peers):
        sem = pltpu.get_barrier_semaphore()
        for p in peers:
            pl.semaphore_signal(sem, inc=1, device_id=p, device_id_type=MESH)
        pl.semaphore_wait(sem, len(peers))

    def drain(self, keep=0):
        n = len(self.open) - keep
        for cp in self.open[:n]:
            cp.wait_send()
        self.open = self.open[n:]


def received(copies):
    for cp in copies:
        cp.wait_recv()


class Gather:
    def __init__(self, pc, buf):
        self.pc, self.buf = pc, buf

    def first(self):
        pc, buf = self.pc, self.buf
        self.one = []
        for d in (2, 1, 3):
            a, b = Loc(buf, pc.y, pc.x, 0), Loc(buf, pc.y, pc.x, 1)
            self.one.append(pc.copy(a, a, pc.to_x[d]))
            self.one.append(pc.copy(b, b, pc.to_y[d]))

    def second(self):
        pc, buf = self.pc, self.buf
        received(self.one)
        self.two, self.passed = {}, []
        for d in (1, 3):
            a, b = Loc(buf, pc.y, ALL, 0), Loc(buf, ALL, pc.x, 1)
            self.two[d] = (pc.copy(a, a, pc.to_y[d]), pc.copy(b, b, pc.to_x[d]))

    def relay(self, d):
        pc, buf = self.pc, self.buf
        received(self.two[d])
        half = pl.ds(0, 2) if d == 1 else pl.ds(2, 2)
        a, b = Loc(buf, pc.ys(4 - d), half, 0), Loc(buf, half, pc.xs(4 - d), 1)
        self.passed.append(pc.copy(a, a, pc.to_y[d]))
        self.passed.append(pc.copy(b, b, pc.to_x[d]))

    def finish(self):
        received(self.passed)


class Scatter:
    def __init__(self, pc, buf, rel, r1, acc, r2):
        self.pc, self.buf, self.rel, self.r1, self.acc, self.r2 = pc, buf, rel, r1, acc, r2

    def first(self):
        pc, buf, rel = self.pc, self.buf, self.rel
        self.halves = []
        for i, d in enumerate((1, 3)):
            half = pl.ds(2 * i, 2)
            self.halves.append(pc.copy(Loc(buf, pc.ys(2), half, 0), Loc(rel, 0, i), pc.to_y[d]))
            self.halves.append(pc.copy(Loc(buf, half, pc.xs(2), 1), Loc(rel, 1, i), pc.to_x[d]))

    def middle(self):
        pc, buf, rel, r1 = self.pc, self.buf, self.rel, self.r1
        received(self.halves)
        self.one = []
        for i, d in enumerate((1, 3)):
            half = pl.ds(2 * i, 2)
            buf[pc.ys(d), half, 0] = buf[pc.ys(d), half, 0] + rel[0, i]
            self.one.append(pc.copy(Loc(buf, pc.ys(d), ALL, 0), Loc(r1, 0, i), pc.to_y[d]))
            buf[half, pc.xs(d), 1] = buf[half, pc.xs(d), 1] + rel[1, i]
            self.one.append(pc.copy(Loc(buf, ALL, pc.xs(d), 1), Loc(r1, 1, i), pc.to_x[d]))

    def second(self):
        pc, buf, r1, acc = self.pc, self.buf, self.r1, self.acc
        received(self.one)
        acc[0] = buf[pc.y, :, 0] + r1[0, 0] + r1[0, 1]
        acc[1] = buf[:, pc.x, 1] + r1[1, 0] + r1[1, 1]
        self.two = []
        for d in (2, 1, 3):
            self.two.append(pc.copy(Loc(acc, 0, pc.xs(d)), Loc(self.r2, 0, d - 1), pc.to_x[d]))
            self.two.append(pc.copy(Loc(acc, 1, pc.ys(d)), Loc(self.r2, 1, d - 1), pc.to_y[d]))

    def finish(self):
        pc, acc, r2 = self.pc, self.acc, self.r2
        received(self.two)
        own0 = acc[0, pc.x] + r2[0, 0] + r2[0, 1] + r2[0, 2]
        own1 = acc[1, pc.y] + r2[1, 0] + r2[1, 1] + r2[1, 2]
        return own0, own1


def factor_part(blk, b):
    a = [blk[8 * g:8 * g + 8, :] for g in range(4)]
    lane = lax.broadcasted_iota(jnp.int32, (8, 128), 1)
    sub = lax.broadcasted_iota(jnp.int32, (8, 128), 0)
    out = [None] * 4

    def column(v, j):
        return jnp.broadcast_to(v[:, j:j + 1], (8, 128))

    def spread(v, i):
        return jnp.broadcast_to(v[i:i + 1, :], (8, 128))

    def recip(v):
        return pl.reciprocal(v, approx=True)

    for q in range(8):
        r0, s0, j0 = q // 2, 4 * (q % 2), 4 * q
        rows = [spread(a[r0], s0 + s) for s in range(4)]
        cols = [column(a[r0], j0 + t) for t in range(4)]
        p = {(s, t): spread(cols[t], s0 + s) for s in range(4) for t in range(s, 4)}
        inside = (lane >= j0) & (lane < j0 + 4)
        sc = [lax.rsqrt(p[s, s]) for s in range(4)]
        v = [jnp.where(inside, jnp.where(lane == j0 + s, 1.0, 0.0), rows[s]) * sc[s] for s in range(4)]
        r = {(s, t): p[s, t] * (sc[s] * sc[t]) for s in range(4) for t in range(s + 1, 4)}
        l10, l20, l30 = r[0, 1], r[0, 2], r[0, 3]
        u11, u22, u33 = 1.0 - l10 * l10, 1.0 - l20 * l20, 1.0 - l30 * l30
        u12, u13, u23 = r[1, 2] - l10 * l20, r[1, 3] - l10 * l30, r[2, 3] - l20 * l30
        v22, v23, v33 = u11 * u22 - u12 * u12, u11 * u23 - u12 * u13, u11 * u33 - u13 * u13
        w33 = v22 * v33 - v23 * v23
        i1, i2, i3 = recip(u11), recip(v22), recip(w33)
        l21, l31, l32 = u12 * i1, u13 * i1, v23 * i2
        d1, d2, d3 = i1, u11 * i2, (u11 * v22) * i3
        n10, n21, n32 = -l10, -l21, -l32
        n20 = l21 * l10 - l20
        n31 = l32 * l21 - l31
        n30 = l31 * l10 - l30 - l32 * n20
        n = [[None] * 4, [n10], [n20, n21], [n30, n31, n32]]
        m = {}
        e1 = d1 * n10
        e20, e21 = d2 * n20, d2 * n21
        m[0, 0] = (1.0 + e1 * n10 + e20 * n20) + d3 * (n30 * n30)
        m[0, 1] = (e1 + e20 * n21) + d3 * (n30 * n31)
        m[0, 2] = e20 + d3 * (n30 * n32)
        m[0, 3] = d3 * n30
        m[1, 1] = (d1 + e21 * n21) + d3 * (n31 * n31)
        m[1, 2] = e21 + d3 * (n31 * n32)
        m[1, 3] = d3 * n31
        m[2, 2] = d2 + d3 * (n32 * n32)
        m[2, 3] = d3 * n32
        m[3, 3] = d3
        w = []
        for s in range(4):
            t = [m[min(s, t), max(s, t)] * v[t] for t in range(4)]
            w.append(((t[0] + t[1]) + (t[2] + t[3])) * sc[s])
        f = [None, d1 * lax.rsqrt(d1), d2 * lax.rsqrt(d2), d3 * lax.rsqrt(d3)]
        done = [v[0]]
        for s in range(1, 4):
            t = v[s]
            for k in range(s):
                t = t + n[s][k] * v[k]
            done.append(f[s] * t)
        o = done[0]
        for s in range(1, 4):
            o = jnp.where(sub == s0 + s, done[s], o)
        out[r0] = o if s0 == 0 else jnp.where(sub < 4, out[r0], o)
        for g in range(r0 if s0 == 0 else r0 + 1, 4):
            if g > r0:
                cols = [column(a[g], j0 + t) for t in range(4)]
            t = [cols[t] * w[t] for t in range(4)]
            a[g] = jnp.where(inside, 0.0, a[g]) - ((t[0] + t[1]) + (t[2] + t[3]))
    new = jnp.concatenate(out, axis=0)
    lanes = lax.broadcasted_iota(jnp.int32, (128, 128), 1)
    rows = lax.broadcasted_iota(jnp.int32, (128, 128), 0)
    live = 128 - 32 * b
    below = jnp.where((lanes[:32] >= 32) & (lanes[:32] < live), new, 0.0)
    step = dot(below, jnp.where((lanes[:32] > rows[:32]) & (lanes[:32] < live), below, new), 0, 0, HIGHEST)
    rest = jnp.where((lanes[32:] < 32) & (rows[32:] < live), 0.0, blk[32:, :]) - step[32:]
    blk[0:96, :] = pltpu.roll(rest, 96, 1)
    blk[96:128, :] = pltpu.roll(new, 96, 1)


def kernel(
    grad, mom, rb, update, momentum_next, basis_next,
    gv, mv, upd, usend, urecv, mrecv, bown, bsend, brecv, blend, blend_send, basis, lpart, lrel, lrecv, left, leftt, ownp, perm,
    gbuf, grel, gr1, gacc, gr2, zsrc, zpart, zfull, gfull,
    wbuf, wrel, wr1, wacc, wr2, wall,
    work, ybuf, blk, tri, right, orth, squares,
    send_sem, recv_sem, local_sem,
):
    pc = Place(send_sem, recv_sem)
    c, x, y, z = pc.c, pc.x, pc.y, pc.z
    loads = []
    for i, m in enumerate((1 - c, c)):
        loads.append(
            (
                pltpu.make_async_copy(mom.at[m], mv.at[m], local_sem.at[2 * i]),
                pltpu.make_async_copy(grad.at[m], gv.at[m], local_sem.at[2 * i + 1]),
            )
        )
        for cp in loads[i]:
            cp.start()
    peers = [pc.partner()]
    peers += [pc.dev(x=pc.xs(d), c=m) for d in (1, 2, 3) for m in (0, 1)]
    peers += [pc.dev(y=pc.ys(d), c=m) for d in (1, 2, 3) for m in (0, 1)]
    peers += [pc.to_z[d] for d in range(1, 8)]
    pc.barrier(peers)

    first = pc.reserve(6)
    slot = lambda d, h: first + 2 * (d - 1) + h
    for d in (1, 3, 2):
        to_y, to_x = lax.rem(y + d * c, 4), lax.rem(x + d * (1 - c), 4)
        for m in range(2):
            pc.copy(rb.at[m], basis.at[y, x, c], pc.dev(y=to_y, x=to_x, c=m), recv=slot(d, c))
    basis_swap = pc.copy(rb.at[1 - c], basis.at[y, x, c], pc.partner())
    basis[y, x, c] = rb[c]
    for cp in loads[0]:
        cp.wait()
    blend_send[...] = mv[1 - c] + gv[1 - c].astype(F32)
    blend_swap = pc.copy(blend_send, blend.at[c], pc.partner())
    for cp in loads[1]:
        cp.wait()
    blend[c] = mv[c] + gv[c].astype(F32)
    basis_swap.wait_recv()
    for d in (1, 3, 2):
        for h in range(2):
            pltpu.make_async_remote_copy(
                src_ref=rb.at[0],
                dst_ref=basis.at[y, x, h],
                send_sem=send_sem.at[slot(d, h)],
                recv_sem=recv_sem.at[slot(d, h)],
                device_id=pc.partner(),
                device_id_type=MESH,
            ).wait_recv()
    gather = Gather(pc, basis)
    gather.one = []
    gather.second()

    def perm_part(i, carry):
        at = lax.broadcasted_iota(jnp.int32, (64, RANK), 0)
        group, half = i // 2, i % 2
        index, low = at // 16, at % 16
        py = (1 - half) * lax.rem(y + group, 4) + half * index
        px = (1 - half) * index + half * lax.rem(x + group, 4)
        rank = ((py * 4 + px) * 2 + half) * 16 + low
        hit = lax.broadcasted_iota(jnp.int32, (64, RANK), 1) == rank
        perm[pl.ds(pl.multiple_of(64 * i, 64), 64), :] = jnp.where(hit, 1.0, 0.0)
        return carry

    lax.fori_loop(0, 8, perm_part, 0)
    blend_swap.wait_recv()
    sums_in, opposite = [], {}

    def to_z(d, e):
        i = e - 1 if e < 4 else e - 2
        sums_in.append(pc.copy(lpart.at[d, pc.zs(e)], lrecv.at[i, d], pc.to_z[e]))

    def to_z_far(d):
        received(opposite[d])
        for i, e in enumerate((3, 5)):
            rows = pl.ds(32 * i, 32)
            lpart[d, pc.zs(e), rows] = lpart[d, pc.zs(e), rows] + lrel[i, d]
            to_z(d, e)

    before = None
    for d in (0, 3, 1, 2):
        if d == 2:
            gather.finish()
        elif d:
            gather.relay(4 - d)

        def left_part(h, carry, d=d):
            rows = jnp.concatenate(
                [basis[pc.ys(d), :, 0].reshape(64, 1024), basis[:, pc.xs(d), 1].reshape(64, 1024)], axis=0
            )
            lpart[d, pl.ds(4 * h, 4)] = dot(blend[h], rows, 1, 1, HIGH).reshape(4, 64, 128)
            return carry

        lax.fori_loop(0, 2, left_part, 0)
        opposite[d] = []
        for i, e in enumerate((1, 7)):
            src = lpart.at[d, pc.zs(4), pl.ds(32 * i, 32)]
            opposite[d].append(pc.copy(src, lrel.at[i, d], pc.to_z[e]))
        if before is not None:
            to_z_far(before)
        for e in (2, 6, 1, 7):
            to_z(d, e)
        before = d
    to_z_far(before)
    received(sums_in)
    own = []
    for d in range(4):
        s = lpart[d, z]
        for e in range(6):
            s = s + lrecv[e, d]
        own.append(s)
    ownp[...] = jnp.concatenate(own, axis=1)

    def order(j, carry):
        cols = pl.ds(pl.multiple_of(128 * j, 128), 128)
        own = dot(ownp[...], perm[:, cols], 1, 0, HIGHEST)
        left[j // 2, z, :, pl.ds(pl.multiple_of(128 * (j % 2), 128), 128)] = own
        return carry

    lax.fori_loop(0, 4, order, 0)
    own = jnp.concatenate([left[q, z] for q in range(2)], axis=1)

    def ring(step):
        up, down = pc.to_z[1], pc.to_z[7]
        copies = []
        for q in range(2):
            a, b = left.at[q, pc.zs(9 - step)], left.at[q, pc.zs(step - 1)]
            if step == 4:
                a, b = a.at[pl.ds(0, 32)], b.at[pl.ds(32, 32)]
            copies += [pc.copy(a, a, up), pc.copy(b, b, down)]
        return copies

    blocks = []
    for i in range(4):
        row = dot(own[:, 128 * i:128 * i + 128], own[:, :128 * i + 128], 0, 0, HIGHEST)
        blocks += [row[:, 128 * j:128 * j + 128] for j in range(i + 1)]
    gbuf[...] = jnp.concatenate(blocks, axis=0).reshape(4, 4, 2, 40, 128)
    gscatter = Scatter(pc, gbuf, grel, gr1, gacc, gr2)
    gscatter.first()
    lefts = ring(1)
    gscatter.middle()
    gscatter.second()
    received(lefts)
    lefts = ring(2)
    own0, own1 = gscatter.finish()
    zsrc[0:5] = jnp.concatenate([own0, own1], axis=0).reshape(5, 16, 128)
    zsrc[5:8] = jnp.zeros((3, 16, 128), F32)
    zs = []
    for d in (4, 3, 5, 2, 6, 1, 7):
        zs.append(pc.copy(zsrc.at[pc.zs(d)], zpart.at[d - 1], pc.to_z[d]))
    received(lefts)
    lefts = ring(3)
    received(zs)
    total = zsrc[z]
    for d in range(7):
        total = total + zpart[d]
    zfull[z] = total
    zs = []
    for d in (4, 3, 5, 2, 6, 1, 7):
        zs.append(pc.copy(zfull.at[z], zfull.at[z], pc.to_z[d]))
    received(lefts)
    lefts = ring(4)
    received(zs)
    gfull[y, x] = zfull[0:5].reshape(2, 40, 128)
    ggather = Gather(pc, gfull)
    ggather.first()
    received(lefts)
    ggather.second()
    wscatter, wgather = [], []
    for q in range(2):
        for i in range(2):
            leftt[256 * q + 128 * i:256 * q + 128 * i + 128, :] = left[q, :, :, 128 * i:128 * i + 128].reshape(RANK, 128).T

        def w_product(j, carry, q=q):
            cols = pl.ds(pl.multiple_of(256 * j, 256), 256)
            part = dot(leftt[256 * q:256 * q + 256, :], blend[:, :, cols].reshape(512, 256), 1, 0, HIGH)
            wbuf[q, :, :, :, :, cols] = part.reshape(4, 4, 2, 8, 256)
            return carry

        lax.fori_loop(0, 4, w_product, 0)
        wscatter.append(Scatter(pc, wbuf.at[q], wrel.at[q], wr1.at[q], wacc.at[q], wr2.at[q]))
        wscatter[q].first()
        if q == 0:
            ggather.relay(1)
            ggather.relay(3)
        wgather.append(Gather(pc, wall.at[q]))
    pc.drain(keep=16)
    ggather.finish()

    def w_gather(q):
        o0, o1 = wscatter[q].finish()
        wall[q, y, x, 0] = o0
        wall[q, y, x, 1] = o1
        wgather[q].first()

    def w_relay(q):
        wgather[q].relay(1)
        wgather[q].relay(3)

    def w_step1():
        wscatter[0].middle()
        wscatter[1].middle()

    def w_step2():
        wscatter[0].second()

    def w_step3():
        wscatter[1].second()
        w_gather(0)

    def w_step4():
        w_gather(1)
        wgather[0].second()

    def w_step5():
        wgather[1].second()
        w_relay(0)

    def w_step6():
        w_relay(1)

    def w_part(q, cols):
        return wall[q, :, :, :, :, cols].reshape(256, 256)

    events = {1: w_step1, 3: w_step2, 5: w_step3, 7: w_step4, 9: w_step5, 11: w_step6}
    flat = gfull[...].reshape(1280, 128)
    for b in range(10):
        work[b] = flat[128 * b:128 * b + 128]
    at = lambda i, j: i * (i + 1) // 2 + j
    yat = lambda i, j: i * (i - 1) // 2 + j
    rowi = lax.broadcasted_iota(jnp.int32, (128, 128), 0)
    coli = lax.broadcasted_iota(jnp.int32, (128, 128), 1)
    tri[...] = jnp.zeros((RANK, RANK), F32)

    def panel_end(k):
        inv = jnp.where(rowi >= coli, blk[...], 0.0)
        tri[128 * k:128 * k + 128, 128 * k:128 * k + 128] = inv
        for i in range(k + 1, 4):
            work[at(i, k)] = dot(work[at(i, k)], inv, 1, 1, HIGHEST)
        for i in range(k + 1, 4):
            for j in range(k + 1, i + 1):
                new = work[at(i, j)] - dot(work[at(i, k)], work[at(j, k)], 1, 1, HIGHEST)
                work[at(i, j)] = new
                if i == k + 1:
                    blk[...] = new
        for j in range(k):
            tri[128 * k:128 * k + 128, 128 * j:128 * j + 128] = dot(inv, ybuf[yat(k, j)], 1, 0, HIGHEST)
        for i in range(k + 1, 4):
            for j in range(k + 1):
                new = dot(work[at(i, k)], tri[128 * k:128 * k + 128, 128 * j:128 * j + 128], 1, 0, HIGHEST)
                ybuf[yat(i, j)] = -new if j == k else ybuf[yat(i, j)] - new

    blk[...] = work[0]

    def pivots(i, carry):
        for n, event in events.items():
            pl.when(i == n)(event)
        factor_part(blk, lax.rem(i, 4))
        for k in range(3):
            pl.when(i == 4 * k + 3)(lambda k=k: panel_end(k))
        return carry

    lax.fori_loop(0, 16, pivots, 0)
    panel_end(3)
    wgather[0].finish()
    wgather[1].finish()

    def columns(body):
        def step(j, carry):
            body(pl.ds(pl.multiple_of(j * 256, 256), 256))
            return carry

        lax.fori_loop(0, 4, step, 0)

    def raw_end(cols):
        wj = jnp.concatenate([w_part(q, cols) for q in range(2)], axis=0)
        right[:, cols] = dot(tri[...], wj, 1, 0, HIGH)

    columns(raw_end)
    fold = right[:, 0:128] * right[:, 0:128]
    for j in range(1, 8):
        fold = fold + right[:, 128 * j:128 * j + 128] * right[:, 128 * j:128 * j + 128]
    sums = dot(jnp.ones((8, 128), F32), fold, 1, 1, HIGHEST)
    squares[z] = jnp.concatenate([sums[0:1, 128 * j:128 * j + 128] for j in range(4)] * 2, axis=0)
    zs = []
    for d in (4, 3, 5, 2, 6, 1, 7):
        zs.append(pc.copy(squares.at[z], squares.at[z], pc.to_z[d]))
    stores = []

    def store(src, dst):
        cp = pltpu.make_async_copy(src, dst, local_sem.at[4 + len(stores)])
        cp.start()
        stores.append(cp)

    def orth_part(h, carry):
        rows = jnp.concatenate([left[q, pl.ds(4 * h, 4)].reshape(256, 256) for q in range(2)], axis=1)
        orth[h] = dot(rows, tri[...], 1, 1, HIGH)
        return carry

    lax.fori_loop(0, 2, orth_part, 0)

    def feed(h):
        def part(cols):
            back = dot(orth[h], right[:, cols], 1, 0, HIGH)
            blend[h, :, cols] = blend[h, :, cols] - (1.0 - momentum_decay) * back

        columns(part)

    feed(1 - c)
    momentum_swap = pc.copy(blend.at[1 - c], mrecv, pc.partner())
    feed(c)
    store(blend.at[c], momentum_next.at[c])
    pc.drain(keep=8)
    received(zs)
    total = squares[0]
    for d in range(1, 8):
        total = total + squares[d]
    inverse = lax.rsqrt(total / D + epsilon_sq)
    inv = jnp.concatenate([inverse[j:j + 1] for j in range(4)], axis=1)
    lane = lax.broadcasted_iota(jnp.int32, (16, RANK), 1)
    sub = lax.broadcasted_iota(jnp.int32, (16, RANK), 0)

    def basis_rows(f):
        pick = jnp.sum(jnp.where(lane == f * 16 + sub, inv, 0.0), axis=1, keepdims=True)
        return right[pl.ds(pl.multiple_of(f * 16, 16), 16), :] * pick

    other = pc.f + 1 - 2 * c
    bsend[...] = basis_rows(other)
    basis_out_swap = pc.copy(bsend, brecv, pc.partner())
    bown[...] = basis_rows(pc.f)
    store(bown, basis_next.at[c])
    for h in range(2):
        orth[h] = orth[h] * (math.sqrt(D / RANK) * inv)
    update_swaps = []
    for i in range(2):

        def send_part(j, carry, i=i):
            cols = pl.ds(pl.multiple_of(512 * i + 256 * j, 256), 256)
            usend[i, :, pl.ds(pl.multiple_of(256 * j, 256), 256)] = dot(orth[1 - c], right[:, cols], 1, 0, HIGH)
            return carry

        lax.fori_loop(0, 2, send_part, 0)
        update_swaps.append(pc.copy(usend.at[i], urecv.at[i], pc.partner()))
    momentum_swap.wait_recv()
    store(mrecv, momentum_next.at[1 - c])

    def direction(cols):
        upd[c, :, cols] = dot(orth[c], right[:, cols], 1, 0, HIGH).astype(jnp.bfloat16)

    columns(direction)
    store(upd.at[c], update.at[c])
    basis_out_swap.wait_recv()
    store(brecv, basis_next.at[1 - c])
    for i in range(2):
        update_swaps[i].wait_recv()
        upd[1 - c, :, 512 * i:512 * i + 512] = urecv[i].astype(jnp.bfloat16)
    store(upd.at[1 - c], update.at[1 - c])
    for cp in stores:
        cp.wait()
    pc.drain()


def place_kernel(update, momentum_next, basis_next, update_out, momentum_out, basis_out, uv, mv, bv, sem):
    parts = [(basis_next, bv, basis_out, pl.ds(0, 16))]
    for i in range(2):
        parts.append((momentum_next, mv, momentum_out, pl.ds(128 * i, 128)))
        parts.append((update, uv, update_out, pl.ds(128 * i, 128)))
    loads, stores = [], []
    for m in range(2):
        for src, held, dst, rows in parts:
            i = len(loads)
            loads.append(pltpu.make_async_copy(src.at[m, rows], held.at[m, rows], sem.at[2 * i]))
            stores.append(pltpu.make_async_copy(held.at[m, rows], dst.at[m, rows], sem.at[2 * i + 1]))
    for cp in loads:
        cp.start()
    for a, b in zip(loads, stores):
        a.wait()
        b.start()
    for cp in stores:
        cp.wait()


def shards(gradient, momentum, right_basis):
    vmem = pl.BlockSpec(memory_space=pltpu.VMEM)
    anywhere = pl.BlockSpec(memory_space=pl.ANY)
    shape = lambda s: jax.ShapeDtypeStruct(s, F32)
    buf = lambda *s: pltpu.VMEM(s, F32)
    half = pltpu.VMEM((2, 256, 1024), jnp.bfloat16)
    out_shape = (jax.ShapeDtypeStruct((2, 256, 1024), jnp.bfloat16), shape((2, 256, 1024)), shape((2, 16, 1024)))
    n = 208
    results = pl.pallas_call(
        kernel,
        out_shape=out_shape,
        in_specs=[anywhere, anywhere, vmem],
        out_specs=[anywhere] * 3,
        scratch_shapes=[
            half, buf(2, 256, 1024), half, buf(2, 256, 512), buf(2, 256, 512), buf(256, 1024),
            buf(16, 1024), buf(16, 1024), buf(16, 1024),
            buf(2, 256, 1024), buf(256, 1024), buf(4, 4, 2, 16, 1024),
            buf(4, 8, 64, 128), buf(2, 4, 32, 128), buf(6, 4, 64, 128), buf(2, 8, 64, 256), buf(RANK, RANK), buf(64, RANK), buf(RANK, RANK),
            buf(4, 4, 2, 40, 128), buf(2, 2, 2, 40, 128), buf(2, 2, 4, 40, 128), buf(2, 4, 40, 128), buf(2, 3, 40, 128),
            buf(8, 16, 128), buf(7, 16, 128), buf(8, 16, 128), buf(4, 4, 2, 40, 128),
            buf(2, 4, 4, 2, 8, 1024), buf(2, 2, 2, 2, 8, 1024), buf(2, 2, 2, 4, 8, 1024), buf(2, 2, 4, 8, 1024), buf(2, 2, 3, 8, 1024),
            buf(2, 4, 4, 2, 8, 1024),
            buf(10, 128, 128), buf(6, 128, 128), buf(128, 128), buf(RANK, RANK),
            buf(RANK, 1024), buf(2, 256, RANK), buf(8, 8, 128),
            pltpu.SemaphoreType.DMA((n,)), pltpu.SemaphoreType.DMA((n,)), pltpu.SemaphoreType.DMA((10,)),
        ],
        compiler_params=pltpu.CompilerParams(
            collective_id=0, has_side_effects=True, vmem_limit_bytes=VMEM_BYTES
        ),
        name="dion",
    )(gradient, momentum, right_basis)
    return pl.pallas_call(
        place_kernel,
        out_shape=out_shape,
        in_specs=[anywhere] * 3,
        out_specs=[anywhere] * 3,
        scratch_shapes=[half, buf(2, 256, 1024), buf(2, 16, 1024), pltpu.SemaphoreType.DMA((20,))],
        compiler_params=pltpu.CompilerParams(vmem_limit_bytes=VMEM_BYTES),
        name="place",
    )(*results)


def solution(mesh):
    placed = (P(None, "fsdp", "tp"), P(None, "fsdp", "tp"), P(None, "fsdp", "tp"))
    return jax.shard_map(
        shards,
        mesh=mesh,
        in_specs=placed,
        out_specs=placed,
        check_vma=False,
    )
```

```python
import math

import jax
import jax.numpy as jnp
from jax import lax
from jax.experimental import pallas as pl
from jax.experimental.pallas import tpu as pltpu
from jax.sharding import PartitionSpec as P

D = 8192
RANK = 512
momentum_decay = 0.8
epsilon_sq = 1e-06
MESH = pl.DeviceIdType.MESH
F32 = jnp.float32
HIGH = lax.Precision.HIGH
HIGHEST = lax.Precision.HIGHEST
VMEM_BYTES = 56 * 1024 * 1024


def dot(a, b, ca, cb, precision):
    return lax.dot_general(
        a, b, (((ca,), (cb,)), ((), ())), precision=precision, preferred_element_type=F32
    )


class Place:
    def __init__(self, send_sem, recv_sem):
        f = lax.axis_index("fsdp")
        self.f = f
        self.z = lax.axis_index("tp")
        self.c = lax.rem(f, 2)
        self.x = lax.rem(f // 2, 4)
        self.y = f // 8
        self.send_sem, self.recv_sem = send_sem, recv_sem
        self.count = 0
        self.open = []

    def dev(self, y=None, x=None, z=None, c=None):
        y = self.y if y is None else y
        x = self.x if x is None else x
        c = self.c if c is None else c
        z = self.z if z is None else z
        return ((y * 4 + x) * 2 + c, z)

    def partner(self):
        return self.dev(c=1 - self.c)

    def xs(self, d):
        return lax.rem(self.x + d, 4)

    def ys(self, d):
        return lax.rem(self.y + d, 4)

    def zs(self, d):
        return lax.rem(self.z + d, 8)

    def reserve(self, n):
        i = self.count
        self.count += n
        assert self.count <= self.send_sem.shape[0]
        return i

    def copy(self, src, dst, to, recv=None):
        i = self.reserve(1)
        cp = pltpu.make_async_remote_copy(
            src_ref=src,
            dst_ref=dst,
            send_sem=self.send_sem.at[i],
            recv_sem=self.recv_sem.at[i if recv is None else recv],
            device_id=to,
            device_id_type=MESH,
        )
        cp.start()
        self.open.append(cp)
        return cp

    def barrier(self, peers):
        sem = pltpu.get_barrier_semaphore()
        for p in peers:
            pl.semaphore_signal(sem, inc=1, device_id=p, device_id_type=MESH)
        pl.semaphore_wait(sem, len(peers))

    def drain(self, keep=0):
        n = len(self.open) - keep
        for cp in self.open[:n]:
            cp.wait_send()
        self.open = self.open[n:]


def received(copies):
    for cp in copies:
        cp.wait_recv()


class Gather:
    def __init__(self, pc, buf):
        self.pc, self.buf = pc, buf

    def first(self):
        pc, buf = self.pc, self.buf
        self.one = []
        for d in (1, 3, 2):
            a, b = buf.at[pc.y, pc.x, 0], buf.at[pc.y, pc.x, 1]
            self.one.append(pc.copy(a, a, pc.dev(x=pc.xs(d))))
            self.one.append(pc.copy(b, b, pc.dev(y=pc.ys(d))))

    def second(self):
        pc, buf = self.pc, self.buf
        received(self.one)
        self.two = {}
        for d in (1, 3, 2):
            a, b = buf.at[pc.y, :, 0], buf.at[:, pc.x, 1]
            self.two[d] = (pc.copy(a, a, pc.dev(y=pc.ys(d))), pc.copy(b, b, pc.dev(x=pc.xs(d))))

    def finish(self):
        for d in (1, 3, 2):
            received(self.two[d])


class Scatter:
    def __init__(self, pc, buf, r1, acc, r2):
        self.pc, self.buf, self.r1, self.acc, self.r2 = pc, buf, r1, acc, r2

    def first(self):
        pc, buf = self.pc, self.buf
        self.one = []
        for d in (1, 3, 2):
            self.one.append(pc.copy(buf.at[pc.ys(d), :, 0], self.r1.at[0, d - 1], pc.dev(y=pc.ys(d))))
            self.one.append(pc.copy(buf.at[:, pc.xs(d), 1], self.r1.at[1, d - 1], pc.dev(x=pc.xs(d))))

    def second(self):
        pc, buf, r1, acc = self.pc, self.buf, self.r1, self.acc
        received(self.one)
        acc[0] = buf[pc.y, :, 0] + r1[0, 0] + r1[0, 1] + r1[0, 2]
        acc[1] = buf[:, pc.x, 1] + r1[1, 0] + r1[1, 1] + r1[1, 2]
        self.two = []
        for d in (1, 3, 2):
            self.two.append(pc.copy(acc.at[0, pc.xs(d)], self.r2.at[0, d - 1], pc.dev(x=pc.xs(d))))
            self.two.append(pc.copy(acc.at[1, pc.ys(d)], self.r2.at[1, d - 1], pc.dev(y=pc.ys(d))))

    def finish(self):
        pc, acc, r2 = self.pc, self.acc, self.r2
        received(self.two)
        own0 = acc[0, pc.x] + r2[0, 0] + r2[0, 1] + r2[0, 2]
        own1 = acc[1, pc.y] + r2[1, 0] + r2[1, 1] + r2[1, 2]
        return own0, own1


def factor_block(load, tick):
    groups = 16
    a = [load(r) for r in range(groups)]
    lane = lax.broadcasted_iota(jnp.int32, (8, 128), 1)
    sub = lax.broadcasted_iota(jnp.int32, (8, 128), 0)
    out = [None] * groups

    def column(v, j):
        return jnp.broadcast_to(v[:, j:j + 1], (8, 128))

    def spread(v, i):
        return jnp.broadcast_to(v[i:i + 1, :], (8, 128))

    def recip(v):
        return pl.reciprocal(v, approx=True)

    for q in range(32):
        r0, s0, j0 = q // 2, 4 * (q % 2), 4 * q
        end = 4 * (r0 // 4) + 4
        rows = [spread(a[r0], s0 + s) for s in range(4)]
        cols = [column(a[r0], j0 + t) for t in range(4)]
        p = {(s, t): spread(cols[t], s0 + s) for s in range(4) for t in range(s, 4)}
        inside = (lane >= j0) & (lane < j0 + 4)
        sc = [lax.rsqrt(p[s, s]) for s in range(4)]
        v = [jnp.where(inside, jnp.where(lane == j0 + s, 1.0, 0.0), rows[s]) * sc[s] for s in range(4)]
        r = {(s, t): p[s, t] * (sc[s] * sc[t]) for s in range(4) for t in range(s + 1, 4)}
        l10, l20, l30 = r[0, 1], r[0, 2], r[0, 3]
        u11, u22, u33 = 1.0 - l10 * l10, 1.0 - l20 * l20, 1.0 - l30 * l30
        u12, u13, u23 = r[1, 2] - l10 * l20, r[1, 3] - l10 * l30, r[2, 3] - l20 * l30
        v22, v23, v33 = u11 * u22 - u12 * u12, u11 * u23 - u12 * u13, u11 * u33 - u13 * u13
        w33 = v22 * v33 - v23 * v23
        i1, i2, i3 = recip(u11), recip(v22), recip(w33)
        l21, l31, l32 = u12 * i1, u13 * i1, v23 * i2
        d1, d2, d3 = i1, u11 * i2, (u11 * v22) * i3
        n10, n21, n32 = -l10, -l21, -l32
        n20 = l21 * l10 - l20
        n31 = l32 * l21 - l31
        n30 = l31 * l10 - l30 - l32 * n20
        n = [[None] * 4, [n10], [n20, n21], [n30, n31, n32]]
        m = {}
        e1 = d1 * n10
        e20, e21 = d2 * n20, d2 * n21
        m[0, 0] = (1.0 + e1 * n10 + e20 * n20) + d3 * (n30 * n30)
        m[0, 1] = (e1 + e20 * n21) + d3 * (n30 * n31)
        m[0, 2] = e20 + d3 * (n30 * n32)
        m[0, 3] = d3 * n30
        m[1, 1] = (d1 + e21 * n21) + d3 * (n31 * n31)
        m[1, 2] = e21 + d3 * (n31 * n32)
        m[1, 3] = d3 * n31
        m[2, 2] = d2 + d3 * (n32 * n32)
        m[2, 3] = d3 * n32
        m[3, 3] = d3
        w = []
        for s in range(4):
            t = [m[min(s, t), max(s, t)] * v[t] for t in range(4)]
            w.append(((t[0] + t[1]) + (t[2] + t[3])) * sc[s])
        f = [None, d1 * lax.rsqrt(d1), d2 * lax.rsqrt(d2), d3 * lax.rsqrt(d3)]
        done = [v[0]]
        for s in range(1, 4):
            t = v[s]
            for k in range(s):
                t = t + n[s][k] * v[k]
            done.append(f[s] * t)
        o = done[0]
        for s in range(1, 4):
            o = jnp.where(sub == s0 + s, done[s], o)
        out[r0] = o if s0 == 0 else jnp.where(sub < 4, out[r0], o)
        for g in range(r0 if s0 == 0 else r0 + 1, end):
            if g > r0:
                cols = [column(a[g], j0 + t) for t in range(4)]
            t = [cols[t] * w[t] for t in range(4)]
            a[g] = jnp.where(inside, 0.0, a[g]) - ((t[0] + t[1]) + (t[2] + t[3]))
        if q % 8 == 7 and end < groups:
            new = jnp.concatenate(out[end - 4:end], axis=0)
            lanes = lax.broadcasted_iota(jnp.int32, (32, 128), 1)
            over = lanes > 8 * end - 32 + lax.broadcasted_iota(jnp.int32, (32, 128), 0)
            right = jnp.where(lanes >= 8 * end, new, 0.0)
            step = dot(right, jnp.where(over, right, new), 0, 0, HIGHEST)
            done_lanes = (lane >= 8 * end - 32) & (lane < 8 * end)
            for g in range(end, groups):
                a[g] = jnp.where(done_lanes, 0.0, a[g]) - step[8 * g:8 * g + 8]
        tick(q)
    return out


def kernel(
    grad, mom, rb, update, momentum_next, basis_next,
    gv, mv, upd, usend, urecv, mrecv, bown, bsend, brecv, blend, blend_send, basis, lpart, lrecv, left, perm,
    gbuf, gr1, gacc, gr2, zsrc, zpart, zfull, gfull,
    wbuf, wr1, wacc, wr2, wall,
    work, ybuf, tri, right, orth, squares,
    send_sem, recv_sem, local_sem,
):
    pc = Place(send_sem, recv_sem)
    c, x, y, z = pc.c, pc.x, pc.y, pc.z
    loads = []
    for i, m in enumerate((1 - c, c)):
        loads.append(
            (
                pltpu.make_async_copy(mom.at[m], mv.at[m], local_sem.at[2 * i]),
                pltpu.make_async_copy(grad.at[m], gv.at[m], local_sem.at[2 * i + 1]),
            )
        )
        for cp in loads[i]:
            cp.start()
    peers = [pc.partner()]
    peers += [pc.dev(x=pc.xs(d), c=m) for d in (1, 2, 3) for m in (0, 1)]
    peers += [pc.dev(y=pc.ys(d), c=m) for d in (1, 2, 3) for m in (0, 1)]
    peers += [pc.dev(z=pc.zs(d)) for d in range(1, 8)]
    pc.barrier(peers)

    first = pc.reserve(6)
    slot = lambda d, h: first + 2 * (d - 1) + h
    for d in (1, 3, 2):
        to_y, to_x = lax.rem(y + d * c, 4), lax.rem(x + d * (1 - c), 4)
        for m in range(2):
            pc.copy(rb.at[m], basis.at[y, x, c], pc.dev(y=to_y, x=to_x, c=m), recv=slot(d, c))
    basis_swap = pc.copy(rb.at[1 - c], basis.at[y, x, c], pc.partner())
    basis[y, x, c] = rb[c]
    for cp in loads[0]:
        cp.wait()
    blend_send[...] = mv[1 - c] + gv[1 - c].astype(F32)
    blend_swap = pc.copy(blend_send, blend.at[c], pc.partner())
    for cp in loads[1]:
        cp.wait()
    blend[c] = mv[c] + gv[c].astype(F32)
    basis_swap.wait_recv()
    for d in (1, 3, 2):
        for h in range(2):
            pltpu.make_async_remote_copy(
                src_ref=rb.at[0],
                dst_ref=basis.at[y, x, h],
                send_sem=send_sem.at[slot(d, h)],
                recv_sem=recv_sem.at[slot(d, h)],
                device_id=pc.partner(),
                device_id_type=MESH,
            ).wait_recv()
    gather = Gather(pc, basis)
    gather.one = []
    gather.second()
    at = lax.broadcasted_iota(jnp.int32, (RANK, RANK), 0)
    group, half = at // 128, (at // 64) % 2
    index, low = (at // 16) % 4, at % 16
    py = jnp.where(half == 0, (y + group) % 4, index)
    px = jnp.where(half == 0, index, (x + group) % 4)
    rank = ((py * 4 + px) * 2 + half) * 16 + low
    perm[...] = jnp.where(lax.broadcasted_iota(jnp.int32, (RANK, RANK), 1) == rank, 1.0, 0.0).astype(jnp.bfloat16)
    blend_swap.wait_recv()
    sums_in = []
    for d in (0, 3, 1, 2):
        if d:
            received(gather.two[4 - d])
        rows = jnp.concatenate(
            [basis[pc.ys(d), :, 0].reshape(64, 1024), basis[:, pc.xs(d), 1].reshape(64, 1024)], axis=0
        )
        part = dot(blend[...].reshape(512, 1024), rows, 1, 1, HIGH)
        lpart[d] = part.reshape(8, 64, 128)
        for e in (4, 3, 5, 2, 6, 1, 7):
            sums_in.append(pc.copy(lpart.at[d, pc.zs(e)], lrecv.at[e - 1, d], pc.dev(z=pc.zs(e))))
    received(sums_in)
    own = []
    for d in range(4):
        s = lpart[d, z]
        for e in range(7):
            s = s + lrecv[e, d]
        own.append(s)
    own = jnp.concatenate(own, axis=1)
    high = own.astype(jnp.bfloat16)
    rest = own - high.astype(F32)
    mid = rest.astype(jnp.bfloat16)
    low = (rest - mid.astype(F32)).astype(jnp.bfloat16)
    parts = dot(jnp.concatenate([high, mid, low], axis=0), perm[...], 1, 0, None)
    own = (parts[0:64] + parts[64:128]) + parts[128:192]
    for q in range(2):
        left[q, z] = own[:, 256 * q:256 * q + 256]

    def ring(step):
        up, down = pc.dev(z=pc.zs(1)), pc.dev(z=pc.zs(7))
        copies = []
        for q in range(2):
            a, b = left.at[q, pc.zs(9 - step)], left.at[q, pc.zs(step - 1)]
            if step == 4:
                a, b = a.at[pl.ds(0, 32)], b.at[pl.ds(32, 32)]
            copies += [pc.copy(a, a, up), pc.copy(b, b, down)]
        return copies

    blocks = []
    for i in range(4):
        row = dot(own[:, 128 * i:128 * i + 128], own[:, :128 * i + 128], 0, 0, HIGHEST)
        blocks += [row[:, 128 * j:128 * j + 128] for j in range(i + 1)]
    gbuf[...] = jnp.concatenate(blocks, axis=0).reshape(4, 4, 2, 40, 128)
    gscatter = Scatter(pc, gbuf, gr1, gacc, gr2)
    gscatter.first()
    lefts = ring(1)
    gscatter.second()
    received(lefts)
    lefts = ring(2)
    own0, own1 = gscatter.finish()
    zsrc[0:5] = jnp.concatenate([own0, own1], axis=0).reshape(5, 16, 128)
    zsrc[5:8] = jnp.zeros((3, 16, 128), F32)
    zs = []
    for d in (4, 3, 5, 2, 6, 1, 7):
        zs.append(pc.copy(zsrc.at[pc.zs(d)], zpart.at[d - 1], pc.dev(z=pc.zs(d))))
    received(lefts)
    lefts = ring(3)
    received(zs)
    total = zsrc[z]
    for d in range(7):
        total = total + zpart[d]
    zfull[z] = total
    zs = []
    for d in (4, 3, 5, 2, 6, 1, 7):
        zs.append(pc.copy(zfull.at[z], zfull.at[z], pc.dev(z=pc.zs(d))))
    received(lefts)
    lefts = ring(4)
    received(zs)
    gfull[y, x] = zfull[0:5].reshape(2, 40, 128)
    ggather = Gather(pc, gfull)
    ggather.first()
    received(lefts)
    ggather.second()
    wscatter, wgather = [], []
    for q in range(2):
        for i in range(2):
            lt = left[q, :, :, 128 * i:128 * i + 128].reshape(RANK, 128)
            part = dot(lt, blend[...].reshape(512, 1024), 0, 0, HIGH)
            wbuf[q, 2 * i:2 * i + 2] = part.reshape(2, 4, 2, 8, 1024)
        wscatter.append(Scatter(pc, wbuf.at[q], wr1.at[q], wacc.at[q], wr2.at[q]))
        wscatter[q].first()
        wgather.append(Gather(pc, wall.at[q]))
    pc.drain(keep=18)
    ggather.finish()

    def w_gather(q):
        o0, o1 = wscatter[q].finish()
        wall[q, y, x, 0] = o0
        wall[q, y, x, 1] = o1
        wgather[q].first()

    def w_step1():
        wscatter[0].second()

    def w_step2():
        wscatter[1].second()
        w_gather(0)

    def w_step3():
        w_gather(1)
        wgather[0].second()

    def w_step4():
        wgather[1].second()

    def w_last():
        wgather[0].finish()
        wgather[1].finish()
        pending.extend(raw_job(i, j) for j in range(4) for i in range(3))
        pending.extend(feed_job(h, j) for j in range(4) for h in range(2))

    def w_part(q, cols):
        return wall[q, :, :, :, :, cols].reshape(256, 256)

    def raw_job(i, j):
        def job():
            cols = pl.ds(256 * j, 256)
            n = 128 * (i + 1)
            wj = jnp.concatenate([w_part(q, cols) for q in range(2 if i > 1 else 1)], axis=0)[:n]
            right[128 * i:128 * i + 128, cols] = dot(tri[128 * i:128 * i + 128, 0:n], wj, 1, 0, HIGH)

        return job

    def feed_job(h, j):
        def job():
            cols = pl.ds(256 * j, 256)
            back = dot(orth[h, :, 0:384], right[0:384, cols], 1, 0, HIGH)
            blend[h, :, cols] = blend[h, :, cols] - (1.0 - momentum_decay) * back

        return job

    def orth_job(k, h):
        def job():
            n = 128 * (k + 1)
            rows = jnp.concatenate([left[q, 4 * h:4 * h + 4].reshape(256, 256) for q in range(2)], axis=1)[:, :n]
            orth[h, :, 128 * k:n] = dot(rows, tri[128 * k:n, 0:n], 1, 1, HIGH)

        return job

    events = {(0, 18): w_step1, (1, 4): w_step2, (1, 20): w_step3, (2, 6): w_step4, (3, 12): w_last}
    flat = gfull[...].reshape(1280, 128)
    for b in range(10):
        work[b] = flat[128 * b:128 * b + 128]
    at = lambda i, j: i * (i + 1) // 2 + j
    yat = lambda i, j: i * (i - 1) // 2 + j
    rowi = lax.broadcasted_iota(jnp.int32, (128, 128), 0)
    coli = lax.broadcasted_iota(jnp.int32, (128, 128), 1)
    pending = []

    def tri_row(k, inv):
        for j in range(k):
            tri[128 * k:128 * k + 128, 128 * j:128 * j + 128] = dot(inv, ybuf[yat(k, j)], 1, 0, HIGHEST)
        tri[128 * k:128 * k + 128, 128 * k:128 * k + 128] = inv

    def later(k, inv):
        def solve(i):
            work[at(i, k)] = dot(work[at(i, k)], inv, 1, 1, HIGHEST)

        def trail(i, j):
            work[at(i, j)] = work[at(i, j)] - dot(work[at(i, k)], work[at(j, k)], 1, 1, HIGHEST)

        def inverse(i, j):
            new = dot(work[at(i, k)], tri[128 * k:128 * k + 128, 128 * j:128 * j + 128], 1, 0, HIGHEST)
            ybuf[yat(i, j)] = -new if j == k else ybuf[yat(i, j)] - new

        jobs = [lambda: tri_row(k, inv)]
        for i in range(k + 2, 4):
            jobs.append(lambda i=i: solve(i))
        for i in range(k + 2, 4):
            for j in range(k + 1, i + 1):
                jobs.append(lambda i=i, j=j: trail(i, j))
        for i in range(k + 1, 4):
            for j in range(k + 1):
                jobs.append(lambda i=i, j=j: inverse(i, j))
        return jobs + [orth_job(k, h) for h in range(2)]

    for k in range(4):

        def tick(q, k=k):
            if (k, q) in events:
                events[k, q]()
            if pending and q >= 1:
                pending.pop(0)()

        rows = factor_block(lambda r: work[at(k, k), 8 * r:8 * r + 8, :], tick)
        while pending:
            pending.pop(0)()
        inv = jnp.where(rowi >= coli, jnp.concatenate(rows, axis=0), 0.0)
        if k < 3:
            below = dot(work[at(k + 1, k)], inv, 1, 1, HIGHEST)
            work[at(k + 1, k)] = below
            work[at(k + 1, k + 1)] = work[at(k + 1, k + 1)] - dot(below, below, 1, 1, HIGHEST)
            pending = later(k, inv)
        else:
            tri_row(k, inv)


    def columns(body):
        def step(j, carry):
            body(pl.ds(pl.multiple_of(j * 256, 256), 256))
            return carry

        lax.fori_loop(0, 4, step, 0)

    def raw_end(cols):
        wj = jnp.concatenate([w_part(q, cols) for q in range(2)], axis=0)
        new = dot(tri[384:, :], wj, 1, 0, HIGH)
        right[384:, cols] = new

    columns(raw_end)
    fold = right[:, 0:128] * right[:, 0:128]
    for j in range(1, 8):
        fold = fold + right[:, 128 * j:128 * j + 128] * right[:, 128 * j:128 * j + 128]
    sums = dot(jnp.ones((8, 128), F32), fold, 1, 1, HIGHEST)
    squares[z] = jnp.concatenate([sums[0:1, 128 * j:128 * j + 128] for j in range(4)] * 2, axis=0)
    zs = []
    for d in (4, 3, 5, 2, 6, 1, 7):
        zs.append(pc.copy(squares.at[z], squares.at[z], pc.dev(z=pc.zs(d))))
    stores = []

    def store(src, dst):
        cp = pltpu.make_async_copy(src, dst, local_sem.at[4 + len(stores)])
        cp.start()
        stores.append(cp)

    for h in range(2):
        orth_job(3, h)()

    def feed(h):
        def part(cols):
            back = dot(orth[h, :, 384:], right[384:, cols], 1, 0, HIGH)
            blend[h, :, cols] = blend[h, :, cols] - (1.0 - momentum_decay) * back

        columns(part)

    feed(1 - c)
    momentum_swap = pc.copy(blend.at[1 - c], mrecv, pc.partner())
    feed(c)
    store(blend.at[c], momentum_next.at[c])
    pc.drain(keep=8)
    received(zs)
    total = squares[0]
    for d in range(1, 8):
        total = total + squares[d]
    inverse = lax.rsqrt(total / D + epsilon_sq)
    inv = jnp.concatenate([inverse[j:j + 1] for j in range(4)], axis=1)
    lane = lax.broadcasted_iota(jnp.int32, (16, RANK), 1)
    sub = lax.broadcasted_iota(jnp.int32, (16, RANK), 0)

    def basis_rows(f):
        pick = jnp.sum(jnp.where(lane == f * 16 + sub, inv, 0.0), axis=1, keepdims=True)
        return right[pl.ds(pl.multiple_of(f * 16, 16), 16), :] * pick

    other = pc.f + 1 - 2 * c
    bsend[...] = basis_rows(other)
    basis_out_swap = pc.copy(bsend, brecv, pc.partner())
    bown[...] = basis_rows(pc.f)
    store(bown, basis_next.at[c])
    for h in range(2):
        orth[h] = orth[h] * (math.sqrt(D / RANK) * inv)
    update_swaps = []
    for i in range(2):
        for j in range(2):
            cols = pl.ds(512 * i + 256 * j, 256)
            usend[i, :, 256 * j:256 * j + 256] = dot(orth[1 - c], right[:, cols], 1, 0, HIGH)
        update_swaps.append(pc.copy(usend.at[i], urecv.at[i], pc.partner()))
    momentum_swap.wait_recv()
    store(mrecv, momentum_next.at[1 - c])

    def direction(cols):
        upd[c, :, cols] = dot(orth[c], right[:, cols], 1, 0, HIGH).astype(jnp.bfloat16)

    columns(direction)
    store(upd.at[c], update.at[c])
    basis_out_swap.wait_recv()
    store(brecv, basis_next.at[1 - c])
    for i in range(2):
        update_swaps[i].wait_recv()
        upd[1 - c, :, 512 * i:512 * i + 512] = urecv[i].astype(jnp.bfloat16)
    store(upd.at[1 - c], update.at[1 - c])
    for cp in stores:
        cp.wait()
    pc.drain()


def place_kernel(update, momentum_next, basis_next, update_out, momentum_out, basis_out, uv, mv, bv, sem):
    parts = [(basis_next, bv, basis_out, pl.ds(0, 16))]
    for i in range(2):
        parts.append((momentum_next, mv, momentum_out, pl.ds(128 * i, 128)))
        parts.append((update, uv, update_out, pl.ds(128 * i, 128)))
    loads, stores = [], []
    for m in range(2):
        for src, held, dst, rows in parts:
            i = len(loads)
            loads.append(pltpu.make_async_copy(src.at[m, rows], held.at[m, rows], sem.at[2 * i]))
            stores.append(pltpu.make_async_copy(held.at[m, rows], dst.at[m, rows], sem.at[2 * i + 1]))
    for cp in loads:
        cp.start()
    for a, b in zip(loads, stores):
        a.wait()
        b.start()
    for cp in stores:
        cp.wait()


def shards(gradient, momentum, right_basis):
    vmem = pl.BlockSpec(memory_space=pltpu.VMEM)
    anywhere = pl.BlockSpec(memory_space=pl.ANY)
    shape = lambda s: jax.ShapeDtypeStruct(s, F32)
    buf = lambda *s: pltpu.VMEM(s, F32)
    half = pltpu.VMEM((2, 256, 1024), jnp.bfloat16)
    out_shape = (jax.ShapeDtypeStruct((2, 256, 1024), jnp.bfloat16), shape((2, 256, 1024)), shape((2, 16, 1024)))
    n = 208
    results = pl.pallas_call(
        kernel,
        out_shape=out_shape,
        in_specs=[anywhere, anywhere, vmem],
        out_specs=[anywhere] * 3,
        scratch_shapes=[
            half, buf(2, 256, 1024), half, buf(2, 256, 512), buf(2, 256, 512), buf(256, 1024),
            buf(16, 1024), buf(16, 1024), buf(16, 1024),
            buf(2, 256, 1024), buf(256, 1024), buf(4, 4, 2, 16, 1024),
            buf(4, 8, 64, 128), buf(7, 4, 64, 128), buf(2, 8, 64, 256), pltpu.VMEM((RANK, RANK), jnp.bfloat16),
            buf(4, 4, 2, 40, 128), buf(2, 3, 4, 40, 128), buf(2, 4, 40, 128), buf(2, 3, 40, 128),
            buf(8, 16, 128), buf(7, 16, 128), buf(8, 16, 128), buf(4, 4, 2, 40, 128),
            buf(2, 4, 4, 2, 8, 1024), buf(2, 2, 3, 4, 8, 1024), buf(2, 2, 4, 8, 1024), buf(2, 2, 3, 8, 1024),
            buf(2, 4, 4, 2, 8, 1024),
            buf(10, 128, 128), buf(6, 128, 128), buf(RANK, RANK),
            buf(RANK, 1024), buf(2, 256, RANK), buf(8, 8, 128),
            pltpu.SemaphoreType.DMA((n,)), pltpu.SemaphoreType.DMA((n,)), pltpu.SemaphoreType.DMA((10,)),
        ],
        compiler_params=pltpu.CompilerParams(
            collective_id=0, has_side_effects=True, vmem_limit_bytes=VMEM_BYTES
        ),
        name="dion",
    )(gradient, momentum, right_basis)
    return pl.pallas_call(
        place_kernel,
        out_shape=out_shape,
        in_specs=[anywhere] * 3,
        out_specs=[anywhere] * 3,
        scratch_shapes=[half, buf(2, 256, 1024), buf(2, 16, 1024), pltpu.SemaphoreType.DMA((20,))],
        compiler_params=pltpu.CompilerParams(vmem_limit_bytes=VMEM_BYTES),
        name="place",
    )(*results)


def solution(mesh):
    placed = (P(None, "fsdp", "tp"), P(None, "fsdp", "tp"), P(None, "fsdp", "tp"))
    return jax.shard_map(
        shards,
        mesh=mesh,
        in_specs=placed,
        out_specs=placed,
        check_vma=False,
    )
```

```python
import math

import jax
import jax.numpy as jnp
from jax import lax
from jax.experimental import pallas as pl
from jax.experimental.pallas import tpu as pltpu
from jax.sharding import PartitionSpec as P

D = 8192
RANK = 512
momentum_decay = 0.8
epsilon_sq = 1e-06
MESH = pl.DeviceIdType.MESH
F32 = jnp.float32
HIGH = lax.Precision.HIGH
HIGHEST = lax.Precision.HIGHEST
VMEM_BYTES = 56 * 1024 * 1024


def dot(a, b, ca, cb, precision):
    return lax.dot_general(
        a, b, (((ca,), (cb,)), ((), ())), precision=precision, preferred_element_type=F32
    )


class Place:
    def __init__(self, send_sem, recv_sem):
        f = lax.axis_index("fsdp")
        self.f = f
        self.z = lax.axis_index("tp")
        self.c = lax.rem(f, 2)
        self.x = lax.rem(f // 2, 4)
        self.y = f // 8
        self.send_sem, self.recv_sem = send_sem, recv_sem
        self.count = 0
        self.open = []

    def dev(self, y=None, x=None, z=None, c=None):
        y = self.y if y is None else y
        x = self.x if x is None else x
        c = self.c if c is None else c
        z = self.z if z is None else z
        return ((y * 4 + x) * 2 + c, z)

    def partner(self):
        return self.dev(c=1 - self.c)

    def xs(self, d):
        return lax.rem(self.x + d, 4)

    def ys(self, d):
        return lax.rem(self.y + d, 4)

    def zs(self, d):
        return lax.rem(self.z + d, 8)

    def reserve(self, n):
        i = self.count
        self.count += n
        assert self.count <= self.send_sem.shape[0]
        return i

    def copy(self, src, dst, to, recv=None):
        i = self.reserve(1)
        cp = pltpu.make_async_remote_copy(
            src_ref=src,
            dst_ref=dst,
            send_sem=self.send_sem.at[i],
            recv_sem=self.recv_sem.at[i if recv is None else recv],
            device_id=to,
            device_id_type=MESH,
        )
        cp.start()
        self.open.append(cp)
        return cp

    def barrier(self, peers):
        sem = pltpu.get_barrier_semaphore()
        for p in peers:
            pl.semaphore_signal(sem, inc=1, device_id=p, device_id_type=MESH)
        pl.semaphore_wait(sem, len(peers))

    def drain(self, keep=0):
        n = len(self.open) - keep
        for cp in self.open[:n]:
            cp.wait_send()
        self.open = self.open[n:]


def received(copies):
    for cp in copies:
        cp.wait_recv()


class Gather:
    def __init__(self, pc, buf):
        self.pc, self.buf = pc, buf

    def first(self):
        pc, buf = self.pc, self.buf
        self.one = []
        for d in (1, 3, 2):
            a, b = buf.at[pc.y, pc.x, 0], buf.at[pc.y, pc.x, 1]
            self.one.append(pc.copy(a, a, pc.dev(x=pc.xs(d))))
            self.one.append(pc.copy(b, b, pc.dev(y=pc.ys(d))))

    def second(self, ways=(1, 3, 2)):
        received(self.one)
        self.two = {}
        self.send_on(ways)

    def send_on(self, ways):
        pc, buf = self.pc, self.buf
        for d in ways:
            a, b = buf.at[pc.y, :, 0], buf.at[:, pc.x, 1]
            self.two[d] = (pc.copy(a, a, pc.dev(y=pc.ys(d))), pc.copy(b, b, pc.dev(x=pc.xs(d))))

    def finish(self):
        for d in (1, 3, 2):
            received(self.two[d])


class Scatter:
    def __init__(self, pc, buf, r1, acc, r2):
        self.pc, self.buf, self.r1, self.acc, self.r2 = pc, buf, r1, acc, r2

    def first(self):
        pc, buf = self.pc, self.buf
        self.one = []
        for d in (1, 3, 2):
            self.one.append(pc.copy(buf.at[pc.ys(d), :, 0], self.r1.at[0, d - 1], pc.dev(y=pc.ys(d))))
            self.one.append(pc.copy(buf.at[:, pc.xs(d), 1], self.r1.at[1, d - 1], pc.dev(x=pc.xs(d))))

    def second(self):
        pc, buf, r1, acc = self.pc, self.buf, self.r1, self.acc
        received(self.one)
        acc[0] = buf[pc.y, :, 0] + r1[0, 0] + r1[0, 1] + r1[0, 2]
        acc[1] = buf[:, pc.x, 1] + r1[1, 0] + r1[1, 1] + r1[1, 2]
        self.two = []
        for d in (1, 3, 2):
            self.two.append(pc.copy(acc.at[0, pc.xs(d)], self.r2.at[0, d - 1], pc.dev(x=pc.xs(d))))
            self.two.append(pc.copy(acc.at[1, pc.ys(d)], self.r2.at[1, d - 1], pc.dev(y=pc.ys(d))))

    def finish(self):
        pc, acc, r2 = self.pc, self.acc, self.r2
        received(self.two)
        own0 = acc[0, pc.x] + r2[0, 0] + r2[0, 1] + r2[0, 2]
        own1 = acc[1, pc.y] + r2[1, 0] + r2[1, 1] + r2[1, 2]
        return own0, own1


def factor_block(load, tick):
    groups = 16
    a = [load(r) for r in range(groups)]
    lane = lax.broadcasted_iota(jnp.int32, (8, 128), 1)
    sub = lax.broadcasted_iota(jnp.int32, (8, 128), 0)
    out = [None] * groups

    def column(v, j):
        return jnp.broadcast_to(v[:, j:j + 1], (8, 128))

    def spread(v, i):
        return jnp.broadcast_to(v[i:i + 1, :], (8, 128))

    def recip(v):
        return pl.reciprocal(v, approx=True)

    for q in range(32):
        r0, s0, j0 = q // 2, 4 * (q % 2), 4 * q
        end = 4 * (r0 // 4) + 4
        rows = [spread(a[r0], s0 + s) for s in range(4)]
        cols = [column(a[r0], j0 + t) for t in range(4)]
        p = {(s, t): spread(cols[t], s0 + s) for s in range(4) for t in range(s, 4)}
        inside = (lane >= j0) & (lane < j0 + 4)
        sc = [lax.rsqrt(p[s, s]) for s in range(4)]
        v = [jnp.where(inside, jnp.where(lane == j0 + s, 1.0, 0.0), rows[s]) * sc[s] for s in range(4)]
        r = {(s, t): p[s, t] * (sc[s] * sc[t]) for s in range(4) for t in range(s + 1, 4)}
        l10, l20, l30 = r[0, 1], r[0, 2], r[0, 3]
        u11, u22, u33 = 1.0 - l10 * l10, 1.0 - l20 * l20, 1.0 - l30 * l30
        u12, u13, u23 = r[1, 2] - l10 * l20, r[1, 3] - l10 * l30, r[2, 3] - l20 * l30
        v22, v23, v33 = u11 * u22 - u12 * u12, u11 * u23 - u12 * u13, u11 * u33 - u13 * u13
        w33 = v22 * v33 - v23 * v23
        i1, i2, i3 = recip(u11), recip(v22), recip(w33)
        l21, l31, l32 = u12 * i1, u13 * i1, v23 * i2
        d1, d2, d3 = i1, u11 * i2, (u11 * v22) * i3
        n10, n21, n32 = -l10, -l21, -l32
        n20 = l21 * l10 - l20
        n31 = l32 * l21 - l31
        n30 = l31 * l10 - l30 - l32 * n20
        n = [[None] * 4, [n10], [n20, n21], [n30, n31, n32]]
        m = {}
        e1 = d1 * n10
        e20, e21 = d2 * n20, d2 * n21
        m[0, 0] = (1.0 + e1 * n10 + e20 * n20) + d3 * (n30 * n30)
        m[0, 1] = (e1 + e20 * n21) + d3 * (n30 * n31)
        m[0, 2] = e20 + d3 * (n30 * n32)
        m[0, 3] = d3 * n30
        m[1, 1] = (d1 + e21 * n21) + d3 * (n31 * n31)
        m[1, 2] = e21 + d3 * (n31 * n32)
        m[1, 3] = d3 * n31
        m[2, 2] = d2 + d3 * (n32 * n32)
        m[2, 3] = d3 * n32
        m[3, 3] = d3
        w = []
        for s in range(4):
            t = [m[min(s, t), max(s, t)] * v[t] for t in range(4)]
            w.append(((t[0] + t[1]) + (t[2] + t[3])) * sc[s])
        f = [None, d1 * lax.rsqrt(d1), d2 * lax.rsqrt(d2), d3 * lax.rsqrt(d3)]
        done = [v[0]]
        for s in range(1, 4):
            t = v[s]
            for k in range(s):
                t = t + n[s][k] * v[k]
            done.append(f[s] * t)
        o = done[0]
        for s in range(1, 4):
            o = jnp.where(sub == s0 + s, done[s], o)
        out[r0] = o if s0 == 0 else jnp.where(sub < 4, out[r0], o)
        for g in range(r0 if s0 == 0 else r0 + 1, end):
            if g > r0:
                cols = [column(a[g], j0 + t) for t in range(4)]
            t = [cols[t] * w[t] for t in range(4)]
            a[g] = jnp.where(inside, 0.0, a[g]) - ((t[0] + t[1]) + (t[2] + t[3]))
        if q % 8 == 7 and end < groups:
            new = jnp.concatenate(out[end - 4:end], axis=0)
            lanes = lax.broadcasted_iota(jnp.int32, (32, 128), 1)
            over = lanes > 8 * end - 32 + lax.broadcasted_iota(jnp.int32, (32, 128), 0)
            right = jnp.where(lanes >= 8 * end, new, 0.0)
            step = dot(right, jnp.where(over, right, new), 0, 0, HIGHEST)
            done_lanes = (lane >= 8 * end - 32) & (lane < 8 * end)
            for g in range(end, groups):
                a[g] = jnp.where(done_lanes, 0.0, a[g]) - step[8 * g:8 * g + 8]
        tick(q)
    return out


def kernel(
    grad, mom, rb, update, momentum_next, basis_next,
    gv, mv, upd, usend, urecv, mrecv, bown, bsend, brecv, blend, blend_send, basis, lpart, lrecv, left, perm,
    gbuf, gr1, gacc, gr2, zsrc, zpart, zfull, gfull,
    wbuf, wr1, wacc, wr2, wall,
    work, ybuf, tri, right, orth, squares,
    send_sem, recv_sem, local_sem,
):
    pc = Place(send_sem, recv_sem)
    c, x, y, z = pc.c, pc.x, pc.y, pc.z
    loads = []
    for i, m in enumerate((1 - c, c)):
        loads.append(
            (
                pltpu.make_async_copy(mom.at[m], mv.at[m], local_sem.at[2 * i]),
                pltpu.make_async_copy(grad.at[m], gv.at[m], local_sem.at[2 * i + 1]),
            )
        )
        for cp in loads[i]:
            cp.start()
    peers = [pc.partner()]
    peers += [pc.dev(x=pc.xs(d), c=m) for d in (1, 2, 3) for m in (0, 1)]
    peers += [pc.dev(y=pc.ys(d), c=m) for d in (1, 2, 3) for m in (0, 1)]
    peers += [pc.dev(z=pc.zs(d)) for d in range(1, 8)]
    pc.barrier(peers)

    first = pc.reserve(6)
    slot = lambda d, h: first + 2 * (d - 1) + h
    for d in (1, 3, 2):
        to_y, to_x = lax.rem(y + d * c, 4), lax.rem(x + d * (1 - c), 4)
        for m in range(2):
            pc.copy(rb.at[m], basis.at[y, x, c], pc.dev(y=to_y, x=to_x, c=m), recv=slot(d, c))
    basis_swap = pc.copy(rb.at[1 - c], basis.at[y, x, c], pc.partner())
    basis[y, x, c] = rb[c]
    for cp in loads[0]:
        cp.wait()
    blend_send[...] = mv[1 - c] + gv[1 - c].astype(F32)
    blend_swap = pc.copy(blend_send, blend.at[c], pc.partner())
    for cp in loads[1]:
        cp.wait()
    blend[c] = mv[c] + gv[c].astype(F32)
    basis_swap.wait_recv()
    for d in (1, 3, 2):
        for h in range(2):
            pltpu.make_async_remote_copy(
                src_ref=rb.at[0],
                dst_ref=basis.at[y, x, h],
                send_sem=send_sem.at[slot(d, h)],
                recv_sem=recv_sem.at[slot(d, h)],
                device_id=pc.partner(),
                device_id_type=MESH,
            ).wait_recv()
    gather = Gather(pc, basis)
    gather.one = []
    gather.second((1, 3))
    at = lax.broadcasted_iota(jnp.int32, (RANK, RANK), 0)
    group, half = at // 128, (at // 64) % 2
    index, low = (at // 16) % 4, at % 16
    py = jnp.where(half == 0, (y + group) % 4, index)
    px = jnp.where(half == 0, index, (x + group) % 4)
    rank = ((py * 4 + px) * 2 + half) * 16 + low
    perm[...] = jnp.where(lax.broadcasted_iota(jnp.int32, (RANK, RANK), 1) == rank, 1.0, 0.0).astype(jnp.bfloat16)
    blend_swap.wait_recv()
    sums_in = []
    for d in (0, 3, 1, 2):
        if d:
            received(gather.two[4 - d])
        if d == 3:
            gather.send_on((2,))
        rows = jnp.concatenate(
            [basis[pc.ys(d), :, 0].reshape(64, 1024), basis[:, pc.xs(d), 1].reshape(64, 1024)], axis=0
        )
        part = dot(blend[...].reshape(512, 1024), rows, 1, 1, HIGH)
        lpart[d] = part.reshape(8, 64, 128)
        for e in (4, 3, 5, 2, 6, 1, 7):
            sums_in.append(pc.copy(lpart.at[d, pc.zs(e)], lrecv.at[e - 1, d], pc.dev(z=pc.zs(e))))
    received(sums_in)
    own = []
    for d in range(4):
        s = lpart[d, z]
        for e in range(7):
            s = s + lrecv[e, d]
        own.append(s)
    own = jnp.concatenate(own, axis=1)
    high = own.astype(jnp.bfloat16)
    rest = own - high.astype(F32)
    mid = rest.astype(jnp.bfloat16)
    low = (rest - mid.astype(F32)).astype(jnp.bfloat16)
    parts = dot(jnp.concatenate([high, mid, low], axis=0), perm[...], 1, 0, None)
    own = (parts[0:64] + parts[64:128]) + parts[128:192]
    for q in range(2):
        left[q, z] = own[:, 256 * q:256 * q + 256]

    def ring(step):
        up, down = pc.dev(z=pc.zs(1)), pc.dev(z=pc.zs(7))
        copies = []
        for q in range(2):
            a, b = left.at[q, pc.zs(9 - step)], left.at[q, pc.zs(step - 1)]
            if step == 4:
                a, b = a.at[pl.ds(0, 32)], b.at[pl.ds(32, 32)]
            copies += [pc.copy(a, a, up), pc.copy(b, b, down)]
        return copies

    blocks = []
    for i in range(4):
        row = dot(own[:, 128 * i:128 * i + 128], own[:, :128 * i + 128], 0, 0, HIGHEST)
        blocks += [row[:, 128 * j:128 * j + 128] for j in range(i + 1)]
    gbuf[...] = jnp.concatenate(blocks, axis=0).reshape(4, 4, 2, 40, 128)
    gscatter = Scatter(pc, gbuf, gr1, gacc, gr2)
    gscatter.first()
    lefts = ring(1)
    gscatter.second()
    received(lefts)
    lefts = ring(2)
    own0, own1 = gscatter.finish()
    zsrc[0:5] = jnp.concatenate([own0, own1], axis=0).reshape(5, 16, 128)
    zsrc[5:8] = jnp.zeros((3, 16, 128), F32)
    zs = []
    for d in (4, 3, 5, 2, 6, 1, 7):
        zs.append(pc.copy(zsrc.at[pc.zs(d)], zpart.at[d - 1], pc.dev(z=pc.zs(d))))
    received(lefts)
    lefts = ring(3)
    received(zs)
    total = zsrc[z]
    for d in range(7):
        total = total + zpart[d]
    zfull[z] = total
    zs = []
    for d in (4, 3, 5, 2, 6, 1, 7):
        zs.append(pc.copy(zfull.at[z], zfull.at[z], pc.dev(z=pc.zs(d))))
    received(lefts)
    lefts = ring(4)
    received(zs)
    gfull[y, x] = zfull[0:5].reshape(2, 40, 128)
    ggather = Gather(pc, gfull)
    ggather.first()
    received(lefts)
    ggather.second()
    wscatter, wgather = [], []
    for q in range(2):
        for i in range(2):
            lt = left[q, :, :, 128 * i:128 * i + 128].reshape(RANK, 128)
            part = dot(lt, blend[...].reshape(512, 1024), 0, 0, HIGH)
            wbuf[q, 2 * i:2 * i + 2] = part.reshape(2, 4, 2, 8, 1024)
        wscatter.append(Scatter(pc, wbuf.at[q], wr1.at[q], wacc.at[q], wr2.at[q]))
        wscatter[q].first()
        wgather.append(Gather(pc, wall.at[q]))
    pc.drain(keep=18)
    ggather.finish()

    def w_gather(q):
        o0, o1 = wscatter[q].finish()
        wall[q, y, x, 0] = o0
        wall[q, y, x, 1] = o1
        wgather[q].first()

    def w_step1():
        wscatter[0].second()

    def w_step2():
        wscatter[1].second()
        w_gather(0)

    def w_step3():
        w_gather(1)
        wgather[0].second()

    def w_step4():
        wgather[1].second()

    def w_last():
        wgather[0].finish()
        wgather[1].finish()
        pending.extend(raw_job(i, j) for j in range(4) for i in range(3))
        pending.extend(feed_job(h, j) for j in range(4) for h in range(2))

    def w_part(q, cols):
        return wall[q, :, :, :, :, cols].reshape(256, 256)

    def raw_job(i, j):
        def job():
            cols = pl.ds(256 * j, 256)
            n = 128 * (i + 1)
            wj = jnp.concatenate([w_part(q, cols) for q in range(2 if i > 1 else 1)], axis=0)[:n]
            right[128 * i:128 * i + 128, cols] = dot(tri[128 * i:128 * i + 128, 0:n], wj, 1, 0, HIGH)

        return job

    def feed_job(h, j):
        def job():
            cols = pl.ds(256 * j, 256)
            back = dot(orth[h, :, 0:384], right[0:384, cols], 1, 0, HIGH)
            blend[h, :, cols] = blend[h, :, cols] - (1.0 - momentum_decay) * back

        return job

    def orth_job(k, h):
        def job():
            n = 128 * (k + 1)
            rows = jnp.concatenate([left[q, 4 * h:4 * h + 4].reshape(256, 256) for q in range(2)], axis=1)[:, :n]
            orth[h, :, 128 * k:n] = dot(rows, tri[128 * k:n, 0:n], 1, 1, HIGH)

        return job

    events = {(0, 18): w_step1, (1, 4): w_step2, (1, 20): w_step3, (2, 6): w_step4, (3, 12): w_last}
    flat = gfull[...].reshape(1280, 128)
    for b in range(10):
        work[b] = flat[128 * b:128 * b + 128]
    at = lambda i, j: i * (i + 1) // 2 + j
    yat = lambda i, j: i * (i - 1) // 2 + j
    rowi = lax.broadcasted_iota(jnp.int32, (128, 128), 0)
    coli = lax.broadcasted_iota(jnp.int32, (128, 128), 1)
    pending = []

    def tri_row(k, inv):
        for j in range(k):
            tri[128 * k:128 * k + 128, 128 * j:128 * j + 128] = dot(inv, ybuf[yat(k, j)], 1, 0, HIGHEST)
        tri[128 * k:128 * k + 128, 128 * k:128 * k + 128] = inv

    def later(k, inv):
        def solve(i):
            work[at(i, k)] = dot(work[at(i, k)], inv, 1, 1, HIGHEST)

        def trail(i, j):
            work[at(i, j)] = work[at(i, j)] - dot(work[at(i, k)], work[at(j, k)], 1, 1, HIGHEST)

        def inverse(i, j):
            new = dot(work[at(i, k)], tri[128 * k:128 * k + 128, 128 * j:128 * j + 128], 1, 0, HIGHEST)
            ybuf[yat(i, j)] = -new if j == k else ybuf[yat(i, j)] - new

        jobs = [lambda: tri_row(k, inv)]
        for i in range(k + 2, 4):
            jobs.append(lambda i=i: solve(i))
        for i in range(k + 2, 4):
            for j in range(k + 1, i + 1):
                jobs.append(lambda i=i, j=j: trail(i, j))
        for i in range(k + 1, 4):
            for j in range(k + 1):
                jobs.append(lambda i=i, j=j: inverse(i, j))
        return jobs + [orth_job(k, h) for h in range(2)]

    for k in range(4):

        def tick(q, k=k):
            if (k, q) in events:
                events[k, q]()
            if pending and q >= 1:
                pending.pop(0)()

        rows = factor_block(lambda r: work[at(k, k), 8 * r:8 * r + 8, :], tick)
        while pending:
            pending.pop(0)()
        inv = jnp.where(rowi >= coli, jnp.concatenate(rows, axis=0), 0.0)
        if k < 3:
            below = dot(work[at(k + 1, k)], inv, 1, 1, HIGHEST)
            work[at(k + 1, k)] = below
            work[at(k + 1, k + 1)] = work[at(k + 1, k + 1)] - dot(below, below, 1, 1, HIGHEST)
            pending = later(k, inv)
        else:
            tri_row(k, inv)


    def columns(body):
        def step(j, carry):
            body(pl.ds(pl.multiple_of(j * 256, 256), 256))
            return carry

        lax.fori_loop(0, 4, step, 0)

    def raw_end(cols):
        wj = jnp.concatenate([w_part(q, cols) for q in range(2)], axis=0)
        new = dot(tri[384:, :], wj, 1, 0, HIGH)
        right[384:, cols] = new

    columns(raw_end)
    fold = right[:, 0:128] * right[:, 0:128]
    for j in range(1, 8):
        fold = fold + right[:, 128 * j:128 * j + 128] * right[:, 128 * j:128 * j + 128]
    sums = dot(jnp.ones((8, 128), F32), fold, 1, 1, HIGHEST)
    squares[z] = jnp.concatenate([sums[0:1, 128 * j:128 * j + 128] for j in range(4)] * 2, axis=0)
    zs = []
    for d in (4, 3, 5, 2, 6, 1, 7):
        zs.append(pc.copy(squares.at[z], squares.at[z], pc.dev(z=pc.zs(d))))
    stores = []

    def store(src, dst):
        cp = pltpu.make_async_copy(src, dst, local_sem.at[4 + len(stores)])
        cp.start()
        stores.append(cp)

    for h in range(2):
        orth_job(3, h)()

    def feed(h):
        def part(cols):
            back = dot(orth[h, :, 384:], right[384:, cols], 1, 0, HIGH)
            blend[h, :, cols] = blend[h, :, cols] - (1.0 - momentum_decay) * back

        columns(part)

    feed(1 - c)
    momentum_swap = pc.copy(blend.at[1 - c], mrecv, pc.partner())
    feed(c)
    store(blend.at[c], momentum_next.at[c])
    pc.drain(keep=8)
    received(zs)
    total = squares[0]
    for d in range(1, 8):
        total = total + squares[d]
    inverse = lax.rsqrt(total / D + epsilon_sq)
    inv = jnp.concatenate([inverse[j:j + 1] for j in range(4)], axis=1)
    lane = lax.broadcasted_iota(jnp.int32, (16, RANK), 1)
    sub = lax.broadcasted_iota(jnp.int32, (16, RANK), 0)

    def basis_rows(f):
        pick = jnp.sum(jnp.where(lane == f * 16 + sub, inv, 0.0), axis=1, keepdims=True)
        return right[pl.ds(pl.multiple_of(f * 16, 16), 16), :] * pick

    other = pc.f + 1 - 2 * c
    bsend[...] = basis_rows(other)
    basis_out_swap = pc.copy(bsend, brecv, pc.partner())
    bown[...] = basis_rows(pc.f)
    store(bown, basis_next.at[c])
    for h in range(2):
        orth[h] = orth[h] * (math.sqrt(D / RANK) * inv)
    update_swaps = []
    for i in range(2):
        for j in range(2):
            cols = pl.ds(512 * i + 256 * j, 256)
            usend[i, :, 256 * j:256 * j + 256] = dot(orth[1 - c], right[:, cols], 1, 0, HIGH)
        update_swaps.append(pc.copy(usend.at[i], urecv.at[i], pc.partner()))
    momentum_swap.wait_recv()
    store(mrecv, momentum_next.at[1 - c])

    def direction(cols):
        upd[c, :, cols] = dot(orth[c], right[:, cols], 1, 0, HIGH).astype(jnp.bfloat16)

    columns(direction)
    store(upd.at[c], update.at[c])
    basis_out_swap.wait_recv()
    store(brecv, basis_next.at[1 - c])
    for i in range(2):
        update_swaps[i].wait_recv()
        upd[1 - c, :, 512 * i:512 * i + 512] = urecv[i].astype(jnp.bfloat16)
    store(upd.at[1 - c], update.at[1 - c])
    for cp in stores:
        cp.wait()
    pc.drain()


def place_kernel(update, momentum_next, basis_next, update_out, momentum_out, basis_out, uv, mv, bv, sem):
    parts = [(basis_next, bv, basis_out, pl.ds(0, 16))]
    for i in range(2):
        parts.append((momentum_next, mv, momentum_out, pl.ds(128 * i, 128)))
        parts.append((update, uv, update_out, pl.ds(128 * i, 128)))
    loads, stores = [], []
    for m in range(2):
        for src, held, dst, rows in parts:
            i = len(loads)
            loads.append(pltpu.make_async_copy(src.at[m, rows], held.at[m, rows], sem.at[2 * i]))
            stores.append(pltpu.make_async_copy(held.at[m, rows], dst.at[m, rows], sem.at[2 * i + 1]))
    for cp in loads:
        cp.start()
    for a, b in zip(loads, stores):
        a.wait()
        b.start()
    for cp in stores:
        cp.wait()


def shards(gradient, momentum, right_basis):
    vmem = pl.BlockSpec(memory_space=pltpu.VMEM)
    anywhere = pl.BlockSpec(memory_space=pl.ANY)
    shape = lambda s: jax.ShapeDtypeStruct(s, F32)
    buf = lambda *s: pltpu.VMEM(s, F32)
    half = pltpu.VMEM((2, 256, 1024), jnp.bfloat16)
    out_shape = (jax.ShapeDtypeStruct((2, 256, 1024), jnp.bfloat16), shape((2, 256, 1024)), shape((2, 16, 1024)))
    n = 208
    results = pl.pallas_call(
        kernel,
        out_shape=out_shape,
        in_specs=[anywhere, anywhere, vmem],
        out_specs=[anywhere] * 3,
        scratch_shapes=[
            half, buf(2, 256, 1024), half, buf(2, 256, 512), buf(2, 256, 512), buf(256, 1024),
            buf(16, 1024), buf(16, 1024), buf(16, 1024),
            buf(2, 256, 1024), buf(256, 1024), buf(4, 4, 2, 16, 1024),
            buf(4, 8, 64, 128), buf(7, 4, 64, 128), buf(2, 8, 64, 256), pltpu.VMEM((RANK, RANK), jnp.bfloat16),
            buf(4, 4, 2, 40, 128), buf(2, 3, 4, 40, 128), buf(2, 4, 40, 128), buf(2, 3, 40, 128),
            buf(8, 16, 128), buf(7, 16, 128), buf(8, 16, 128), buf(4, 4, 2, 40, 128),
            buf(2, 4, 4, 2, 8, 1024), buf(2, 2, 3, 4, 8, 1024), buf(2, 2, 4, 8, 1024), buf(2, 2, 3, 8, 1024),
            buf(2, 4, 4, 2, 8, 1024),
            buf(10, 128, 128), buf(6, 128, 128), buf(RANK, RANK),
            buf(RANK, 1024), buf(2, 256, RANK), buf(8, 8, 128),
            pltpu.SemaphoreType.DMA((n,)), pltpu.SemaphoreType.DMA((n,)), pltpu.SemaphoreType.DMA((10,)),
        ],
        compiler_params=pltpu.CompilerParams(
            collective_id=0, has_side_effects=True, vmem_limit_bytes=VMEM_BYTES
        ),
        name="dion",
    )(gradient, momentum, right_basis)
    return pl.pallas_call(
        place_kernel,
        out_shape=out_shape,
        in_specs=[anywhere] * 3,
        out_specs=[anywhere] * 3,
        scratch_shapes=[half, buf(2, 256, 1024), buf(2, 16, 1024), pltpu.SemaphoreType.DMA((20,))],
        compiler_params=pltpu.CompilerParams(vmem_limit_bytes=VMEM_BYTES),
        name="place",
    )(*results)


def solution(mesh):
    placed = (P(None, "fsdp", "tp"), P(None, "fsdp", "tp"), P(None, "fsdp", "tp"))
    return jax.shard_map(
        shards,
        mesh=mesh,
        in_specs=placed,
        out_specs=placed,
        check_vma=False,
    )
```

```python
import math

import jax
import jax.numpy as jnp
from jax import lax
from jax.experimental import pallas as pl
from jax.experimental.pallas import tpu as pltpu
from jax.sharding import PartitionSpec as P

D = 8192
RANK = 512
momentum_decay = 0.8
epsilon_sq = 1e-06
MESH = pl.DeviceIdType.MESH
F32 = jnp.float32
HIGH = lax.Precision.HIGH
HIGHEST = lax.Precision.HIGHEST
VMEM_BYTES = 56 * 1024 * 1024


def dot(a, b, ca, cb, precision):
    return lax.dot_general(
        a, b, (((ca,), (cb,)), ((), ())), precision=precision, preferred_element_type=F32
    )


class Place:
    def __init__(self, send_sem, recv_sem):
        f = lax.axis_index("fsdp")
        self.f = f
        self.z = lax.axis_index("tp")
        self.c = lax.rem(f, 2)
        self.x = lax.rem(f // 2, 4)
        self.y = f // 8
        self.send_sem, self.recv_sem = send_sem, recv_sem
        self.count = 0
        self.open = []

    def dev(self, y=None, x=None, z=None, c=None):
        y = self.y if y is None else y
        x = self.x if x is None else x
        c = self.c if c is None else c
        z = self.z if z is None else z
        return ((y * 4 + x) * 2 + c, z)

    def partner(self):
        return self.dev(c=1 - self.c)

    def xs(self, d):
        return lax.rem(self.x + d, 4)

    def ys(self, d):
        return lax.rem(self.y + d, 4)

    def zs(self, d):
        return lax.rem(self.z + d, 8)

    def reserve(self, n):
        i = self.count
        self.count += n
        assert self.count <= self.send_sem.shape[0]
        return i

    def copy(self, src, dst, to, recv=None):
        i = self.reserve(1)
        cp = pltpu.make_async_remote_copy(
            src_ref=src,
            dst_ref=dst,
            send_sem=self.send_sem.at[i],
            recv_sem=self.recv_sem.at[i if recv is None else recv],
            device_id=to,
            device_id_type=MESH,
        )
        cp.start()
        self.open.append(cp)
        return cp

    def barrier(self, peers):
        sem = pltpu.get_barrier_semaphore()
        for p in peers:
            pl.semaphore_signal(sem, inc=1, device_id=p, device_id_type=MESH)
        pl.semaphore_wait(sem, len(peers))

    def drain(self, keep=0):
        n = len(self.open) - keep
        for cp in self.open[:n]:
            cp.wait_send()
        self.open = self.open[n:]


def received(copies):
    for cp in copies:
        cp.wait_recv()


class Gather:
    def __init__(self, pc, buf):
        self.pc, self.buf = pc, buf

    def first(self):
        pc, buf = self.pc, self.buf
        self.one = []
        for d in (1, 3, 2):
            a, b = buf.at[pc.y, pc.x, 0], buf.at[pc.y, pc.x, 1]
            self.one.append(pc.copy(a, a, pc.dev(x=pc.xs(d))))
            self.one.append(pc.copy(b, b, pc.dev(y=pc.ys(d))))

    def second(self, ways=(1, 3, 2)):
        received(self.one)
        self.two = {}
        self.send_on(ways)

    def send_on(self, ways):
        pc, buf = self.pc, self.buf
        for d in ways:
            a, b = buf.at[pc.y, :, 0], buf.at[:, pc.x, 1]
            self.two[d] = (pc.copy(a, a, pc.dev(y=pc.ys(d))), pc.copy(b, b, pc.dev(x=pc.xs(d))))

    def finish(self):
        for d in (1, 3, 2):
            received(self.two[d])


class Scatter:
    def __init__(self, pc, buf, r1, acc, r2):
        self.pc, self.buf, self.r1, self.acc, self.r2 = pc, buf, r1, acc, r2

    def first(self):
        pc, buf = self.pc, self.buf
        self.one = []
        for d in (1, 3, 2):
            self.one.append(pc.copy(buf.at[pc.ys(d), :, 0], self.r1.at[0, d - 1], pc.dev(y=pc.ys(d))))
            self.one.append(pc.copy(buf.at[:, pc.xs(d), 1], self.r1.at[1, d - 1], pc.dev(x=pc.xs(d))))

    def second(self):
        pc, buf, r1, acc = self.pc, self.buf, self.r1, self.acc
        received(self.one)
        acc[0] = buf[pc.y, :, 0] + r1[0, 0] + r1[0, 1] + r1[0, 2]
        acc[1] = buf[:, pc.x, 1] + r1[1, 0] + r1[1, 1] + r1[1, 2]
        self.two = []
        for d in (1, 3, 2):
            self.two.append(pc.copy(acc.at[0, pc.xs(d)], self.r2.at[0, d - 1], pc.dev(x=pc.xs(d))))
            self.two.append(pc.copy(acc.at[1, pc.ys(d)], self.r2.at[1, d - 1], pc.dev(y=pc.ys(d))))

    def finish(self):
        pc, acc, r2 = self.pc, self.acc, self.r2
        received(self.two)
        own0 = acc[0, pc.x] + r2[0, 0] + r2[0, 1] + r2[0, 2]
        own1 = acc[1, pc.y] + r2[1, 0] + r2[1, 1] + r2[1, 2]
        return own0, own1


def factor_block(load, tick):
    groups = 16
    a = [load(r) for r in range(groups)]
    lane = lax.broadcasted_iota(jnp.int32, (8, 128), 1)
    sub = lax.broadcasted_iota(jnp.int32, (8, 128), 0)
    out = [None] * groups

    def column(v, j):
        return jnp.broadcast_to(v[:, j:j + 1], (8, 128))

    def spread(v, i):
        return jnp.broadcast_to(v[i:i + 1, :], (8, 128))

    def recip(v):
        return pl.reciprocal(v, approx=True)

    for q in range(32):
        r0, s0, j0 = q // 2, 4 * (q % 2), 4 * q
        end = 4 * (r0 // 4) + 4
        rows = [spread(a[r0], s0 + s) for s in range(4)]
        cols = [column(a[r0], j0 + t) for t in range(4)]
        p = {(s, t): spread(cols[t], s0 + s) for s in range(4) for t in range(s, 4)}
        inside = (lane >= j0) & (lane < j0 + 4)
        sc = [lax.rsqrt(p[s, s]) for s in range(4)]
        v = [jnp.where(inside, jnp.where(lane == j0 + s, 1.0, 0.0), rows[s]) * sc[s] for s in range(4)]
        r = {(s, t): p[s, t] * (sc[s] * sc[t]) for s in range(4) for t in range(s + 1, 4)}
        l10, l20, l30 = r[0, 1], r[0, 2], r[0, 3]
        u11, u22, u33 = 1.0 - l10 * l10, 1.0 - l20 * l20, 1.0 - l30 * l30
        u12, u13, u23 = r[1, 2] - l10 * l20, r[1, 3] - l10 * l30, r[2, 3] - l20 * l30
        v22, v23, v33 = u11 * u22 - u12 * u12, u11 * u23 - u12 * u13, u11 * u33 - u13 * u13
        w33 = v22 * v33 - v23 * v23
        i1, i2, i3 = recip(u11), recip(v22), recip(w33)
        l21, l31, l32 = u12 * i1, u13 * i1, v23 * i2
        d1, d2, d3 = i1, u11 * i2, (u11 * v22) * i3
        n10, n21, n32 = -l10, -l21, -l32
        n20 = l21 * l10 - l20
        n31 = l32 * l21 - l31
        n30 = l31 * l10 - l30 - l32 * n20
        n = [[None] * 4, [n10], [n20, n21], [n30, n31, n32]]
        m = {}
        e1 = d1 * n10
        e20, e21 = d2 * n20, d2 * n21
        m[0, 0] = (1.0 + e1 * n10 + e20 * n20) + d3 * (n30 * n30)
        m[0, 1] = (e1 + e20 * n21) + d3 * (n30 * n31)
        m[0, 2] = e20 + d3 * (n30 * n32)
        m[0, 3] = d3 * n30
        m[1, 1] = (d1 + e21 * n21) + d3 * (n31 * n31)
        m[1, 2] = e21 + d3 * (n31 * n32)
        m[1, 3] = d3 * n31
        m[2, 2] = d2 + d3 * (n32 * n32)
        m[2, 3] = d3 * n32
        m[3, 3] = d3
        w = []
        for s in range(4):
            t = [m[min(s, t), max(s, t)] * v[t] for t in range(4)]
            w.append(((t[0] + t[1]) + (t[2] + t[3])) * sc[s])
        f = [None, d1 * lax.rsqrt(d1), d2 * lax.rsqrt(d2), d3 * lax.rsqrt(d3)]
        done = [v[0]]
        for s in range(1, 4):
            t = v[s]
            for k in range(s):
                t = t + n[s][k] * v[k]
            done.append(f[s] * t)
        o = done[0]
        for s in range(1, 4):
            o = jnp.where(sub == s0 + s, done[s], o)
        out[r0] = o if s0 == 0 else jnp.where(sub < 4, out[r0], o)
        for g in range(r0 if s0 == 0 else r0 + 1, end):
            if g > r0:
                cols = [column(a[g], j0 + t) for t in range(4)]
            t = [cols[t] * w[t] for t in range(4)]
            a[g] = jnp.where(inside, 0.0, a[g]) - ((t[0] + t[1]) + (t[2] + t[3]))
        if q % 8 == 7 and end < groups:
            new = jnp.concatenate(out[end - 4:end], axis=0)
            lanes = lax.broadcasted_iota(jnp.int32, (32, 128), 1)
            over = lanes > 8 * end - 32 + lax.broadcasted_iota(jnp.int32, (32, 128), 0)
            right = jnp.where(lanes >= 8 * end, new, 0.0)
            step = dot(right, jnp.where(over, right, new), 0, 0, HIGHEST)
            done_lanes = (lane >= 8 * end - 32) & (lane < 8 * end)
            for g in range(end, groups):
                a[g] = jnp.where(done_lanes, 0.0, a[g]) - step[8 * g:8 * g + 8]
        tick(q)
    return out


def kernel(
    grad, mom, rb, update, momentum_next, basis_next,
    gv, mv, upd, usend, urecv, mrecv, bown, bsend, brecv, blend, blend_send, basis, lpart, lrecv, left, perm,
    gbuf, gr1, gacc, gr2, zsrc, zpart, zfull, gfull,
    wbuf, wr1, wacc, wr2, wall,
    work, ybuf, tri, right, orth, squares,
    send_sem, recv_sem, local_sem,
):
    pc = Place(send_sem, recv_sem)
    c, x, y, z = pc.c, pc.x, pc.y, pc.z
    loads = []
    for i, m in enumerate((1 - c, c)):
        loads.append(
            (
                pltpu.make_async_copy(mom.at[m], mv.at[m], local_sem.at[2 * i]),
                pltpu.make_async_copy(grad.at[m], gv.at[m], local_sem.at[2 * i + 1]),
            )
        )
        for cp in loads[i]:
            cp.start()
    peers = [pc.partner()]
    peers += [pc.dev(x=pc.xs(d), c=m) for d in (1, 2, 3) for m in (0, 1)]
    peers += [pc.dev(y=pc.ys(d), c=m) for d in (1, 2, 3) for m in (0, 1)]
    peers += [pc.dev(z=pc.zs(d)) for d in range(1, 8)]
    pc.barrier(peers)

    first = pc.reserve(6)
    slot = lambda d, h: first + 2 * (d - 1) + h
    for d in (1, 3, 2):
        to_y, to_x = lax.rem(y + d * c, 4), lax.rem(x + d * (1 - c), 4)
        for m in range(2):
            pc.copy(rb.at[m], basis.at[y, x, c], pc.dev(y=to_y, x=to_x, c=m), recv=slot(d, c))
    basis_swap = pc.copy(rb.at[1 - c], basis.at[y, x, c], pc.partner())
    basis[y, x, c] = rb[c]
    for cp in loads[0]:
        cp.wait()
    blend_send[...] = mv[1 - c] + gv[1 - c].astype(F32)
    blend_swap = pc.copy(blend_send, blend.at[c], pc.partner())
    for cp in loads[1]:
        cp.wait()
    blend[c] = mv[c] + gv[c].astype(F32)
    basis_swap.wait_recv()
    for d in (1, 3, 2):
        for h in range(2):
            pltpu.make_async_remote_copy(
                src_ref=rb.at[0],
                dst_ref=basis.at[y, x, h],
                send_sem=send_sem.at[slot(d, h)],
                recv_sem=recv_sem.at[slot(d, h)],
                device_id=pc.partner(),
                device_id_type=MESH,
            ).wait_recv()
    gather = Gather(pc, basis)
    gather.one = []
    gather.second((1, 3))
    at = lax.broadcasted_iota(jnp.int32, (RANK, RANK), 0)
    group, half = at // 128, (at // 64) % 2
    index, low = (at // 16) % 4, at % 16
    py = jnp.where(half == 0, (y + group) % 4, index)
    px = jnp.where(half == 0, index, (x + group) % 4)
    rank = ((py * 4 + px) * 2 + half) * 16 + low
    perm[...] = jnp.where(lax.broadcasted_iota(jnp.int32, (RANK, RANK), 1) == rank, 1.0, 0.0).astype(jnp.bfloat16)
    blend_swap.wait_recv()
    sums_in = []
    for d in (0, 3, 1, 2):
        if d:
            received(gather.two[4 - d])
        if d == 3:
            gather.send_on((2,))
        rows = jnp.concatenate(
            [basis[pc.ys(d), :, 0].reshape(64, 1024), basis[:, pc.xs(d), 1].reshape(64, 1024)], axis=0
        )
        part = dot(blend[...].reshape(512, 1024), rows, 1, 1, HIGH)
        lpart[d] = part.reshape(8, 64, 128)
        for e in (4, 3, 5, 2, 6, 1, 7):
            sums_in.append(pc.copy(lpart.at[d, pc.zs(e)], lrecv.at[e - 1, d], pc.dev(z=pc.zs(e))))
    received(sums_in)
    own = []
    for d in range(4):
        s = lpart[d, z]
        for e in range(7):
            s = s + lrecv[e, d]
        own.append(s)
    own = jnp.concatenate(own, axis=1)
    high = own.astype(jnp.bfloat16)
    rest = own - high.astype(F32)
    mid = rest.astype(jnp.bfloat16)
    low = (rest - mid.astype(F32)).astype(jnp.bfloat16)
    parts = dot(jnp.concatenate([high, mid, low], axis=0), perm[...], 1, 0, None)
    own = (parts[0:64] + parts[64:128]) + parts[128:192]
    for q in range(2):
        left[q, z] = own[:, 256 * q:256 * q + 256]

    def ring(step):
        up, down = pc.dev(z=pc.zs(1)), pc.dev(z=pc.zs(7))
        copies = []
        for q in range(2):
            a, b = left.at[q, pc.zs(9 - step)], left.at[q, pc.zs(step - 1)]
            if step == 4:
                a, b = a.at[pl.ds(0, 32)], b.at[pl.ds(32, 32)]
            copies += [pc.copy(a, a, up), pc.copy(b, b, down)]
        return copies

    blocks = []
    for i in range(4):
        row = dot(own[:, 128 * i:128 * i + 128], own[:, :128 * i + 128], 0, 0, HIGHEST)
        blocks += [row[:, 128 * j:128 * j + 128] for j in range(i + 1)]
    gbuf[...] = jnp.concatenate(blocks, axis=0).reshape(4, 4, 2, 40, 128)
    gscatter = Scatter(pc, gbuf, gr1, gacc, gr2)
    gscatter.first()
    lefts = ring(1)
    received(lefts)
    lefts = ring(2)
    gscatter.second()
    own0, own1 = gscatter.finish()
    zsrc[0:5] = jnp.concatenate([own0, own1], axis=0).reshape(5, 16, 128)
    zsrc[5:8] = jnp.zeros((3, 16, 128), F32)
    zs = []
    for d in (4, 3, 5, 2, 6, 1, 7):
        zs.append(pc.copy(zsrc.at[pc.zs(d)], zpart.at[d - 1], pc.dev(z=pc.zs(d))))
    received(zs)
    total = zsrc[z]
    for d in range(7):
        total = total + zpart[d]
    zfull[z] = total
    zs = []
    for d in (4, 3, 5, 2, 6, 1, 7):
        zs.append(pc.copy(zfull.at[z], zfull.at[z], pc.dev(z=pc.zs(d))))
    received(lefts)
    lefts = ring(3)
    received(zs)
    gfull[y, x] = zfull[0:5].reshape(2, 40, 128)
    ggather = Gather(pc, gfull)
    ggather.first()
    received(lefts)
    lefts = ring(4)
    ggather.second()
    received(lefts)
    wscatter, wgather = [], []
    for q in range(2):
        for i in range(2):
            lt = left[q, :, :, 128 * i:128 * i + 128].reshape(RANK, 128)
            part = dot(lt, blend[...].reshape(512, 1024), 0, 0, HIGH)
            wbuf[q, 2 * i:2 * i + 2] = part.reshape(2, 4, 2, 8, 1024)
        wscatter.append(Scatter(pc, wbuf.at[q], wr1.at[q], wacc.at[q], wr2.at[q]))
        wgather.append(Gather(pc, wall.at[q]))
    pc.drain(keep=6)
    ggather.finish()
    for q in range(2):
        wscatter[q].first()

    def w_gather(q):
        o0, o1 = wscatter[q].finish()
        wall[q, y, x, 0] = o0
        wall[q, y, x, 1] = o1
        wgather[q].first()

    def w_step1():
        wscatter[0].second()

    def w_step2():
        wscatter[1].second()
        w_gather(0)

    def w_step3():
        w_gather(1)
        wgather[0].second()

    def w_step4():
        wgather[1].second()

    def w_last():
        wgather[0].finish()
        wgather[1].finish()
        pending.extend(raw_job(i, j) for j in range(4) for i in range(3))
        pending.extend(feed_job(h, j) for j in range(4) for h in range(2))

    def w_part(q, cols):
        return wall[q, :, :, :, :, cols].reshape(256, 256)

    def raw_job(i, j):
        def job():
            cols = pl.ds(256 * j, 256)
            n = 128 * (i + 1)
            wj = jnp.concatenate([w_part(q, cols) for q in range(2 if i > 1 else 1)], axis=0)[:n]
            right[128 * i:128 * i + 128, cols] = dot(tri[128 * i:128 * i + 128, 0:n], wj, 1, 0, HIGH)

        return job

    def feed_job(h, j):
        def job():
            cols = pl.ds(256 * j, 256)
            back = dot(orth[h, :, 0:384], right[0:384, cols], 1, 0, HIGH)
            blend[h, :, cols] = blend[h, :, cols] - (1.0 - momentum_decay) * back

        return job

    def orth_job(k, h):
        def job():
            n = 128 * (k + 1)
            rows = jnp.concatenate([left[q, 4 * h:4 * h + 4].reshape(256, 256) for q in range(2)], axis=1)[:, :n]
            orth[h, :, 128 * k:n] = dot(rows, tri[128 * k:n, 0:n], 1, 1, HIGH)

        return job

    events = {(1, 0): w_step1, (1, 12): w_step2, (1, 26): w_step3, (2, 12): w_step4, (3, 12): w_last}
    flat = gfull[...].reshape(1280, 128)
    for b in range(10):
        work[b] = flat[128 * b:128 * b + 128]
    at = lambda i, j: i * (i + 1) // 2 + j
    yat = lambda i, j: i * (i - 1) // 2 + j
    rowi = lax.broadcasted_iota(jnp.int32, (128, 128), 0)
    coli = lax.broadcasted_iota(jnp.int32, (128, 128), 1)
    pending = []

    def tri_row(k, inv):
        for j in range(k):
            tri[128 * k:128 * k + 128, 128 * j:128 * j + 128] = dot(inv, ybuf[yat(k, j)], 1, 0, HIGHEST)
        tri[128 * k:128 * k + 128, 128 * k:128 * k + 128] = inv

    def later(k, inv):
        def solve(i):
            work[at(i, k)] = dot(work[at(i, k)], inv, 1, 1, HIGHEST)

        def trail(i, j):
            work[at(i, j)] = work[at(i, j)] - dot(work[at(i, k)], work[at(j, k)], 1, 1, HIGHEST)

        def inverse(i, j):
            new = dot(work[at(i, k)], tri[128 * k:128 * k + 128, 128 * j:128 * j + 128], 1, 0, HIGHEST)
            ybuf[yat(i, j)] = -new if j == k else ybuf[yat(i, j)] - new

        jobs = [lambda: tri_row(k, inv)]
        for i in range(k + 2, 4):
            jobs.append(lambda i=i: solve(i))
        for i in range(k + 2, 4):
            for j in range(k + 1, i + 1):
                jobs.append(lambda i=i, j=j: trail(i, j))
        for i in range(k + 1, 4):
            for j in range(k + 1):
                jobs.append(lambda i=i, j=j: inverse(i, j))
        return jobs + [orth_job(k, h) for h in range(2)]

    for k in range(4):

        def tick(q, k=k):
            if (k, q) in events:
                events[k, q]()
            if pending and q >= 1:
                pending.pop(0)()

        rows = factor_block(lambda r: work[at(k, k), 8 * r:8 * r + 8, :], tick)
        while pending:
            pending.pop(0)()
        inv = jnp.where(rowi >= coli, jnp.concatenate(rows, axis=0), 0.0)
        if k < 3:
            below = dot(work[at(k + 1, k)], inv, 1, 1, HIGHEST)
            work[at(k + 1, k)] = below
            work[at(k + 1, k + 1)] = work[at(k + 1, k + 1)] - dot(below, below, 1, 1, HIGHEST)
            pending = later(k, inv)
        else:
            tri_row(k, inv)


    def columns(body):
        def step(j, carry):
            body(pl.ds(pl.multiple_of(j * 256, 256), 256))
            return carry

        lax.fori_loop(0, 4, step, 0)

    def raw_end(cols):
        wj = jnp.concatenate([w_part(q, cols) for q in range(2)], axis=0)
        new = dot(tri[384:, :], wj, 1, 0, HIGH)
        right[384:, cols] = new

    columns(raw_end)
    fold = right[:, 0:128] * right[:, 0:128]
    for j in range(1, 8):
        fold = fold + right[:, 128 * j:128 * j + 128] * right[:, 128 * j:128 * j + 128]
    sums = dot(jnp.ones((8, 128), F32), fold, 1, 1, HIGHEST)
    squares[z] = jnp.concatenate([sums[0:1, 128 * j:128 * j + 128] for j in range(4)] * 2, axis=0)
    zs = []
    for d in (4, 3, 5, 2, 6, 1, 7):
        zs.append(pc.copy(squares.at[z], squares.at[z], pc.dev(z=pc.zs(d))))
    stores = []

    def store(src, dst):
        cp = pltpu.make_async_copy(src, dst, local_sem.at[4 + len(stores)])
        cp.start()
        stores.append(cp)

    for h in range(2):
        orth_job(3, h)()

    def feed(h):
        def part(cols):
            back = dot(orth[h, :, 384:], right[384:, cols], 1, 0, HIGH)
            blend[h, :, cols] = blend[h, :, cols] - (1.0 - momentum_decay) * back

        columns(part)

    feed(1 - c)
    momentum_swap = pc.copy(blend.at[1 - c], mrecv, pc.partner())
    feed(c)
    store(blend.at[c], momentum_next.at[c])
    pc.drain(keep=8)
    received(zs)
    total = squares[0]
    for d in range(1, 8):
        total = total + squares[d]
    inverse = lax.rsqrt(total / D + epsilon_sq)
    inv = jnp.concatenate([inverse[j:j + 1] for j in range(4)], axis=1)
    lane = lax.broadcasted_iota(jnp.int32, (16, RANK), 1)
    sub = lax.broadcasted_iota(jnp.int32, (16, RANK), 0)

    def basis_rows(f):
        pick = jnp.sum(jnp.where(lane == f * 16 + sub, inv, 0.0), axis=1, keepdims=True)
        return right[pl.ds(pl.multiple_of(f * 16, 16), 16), :] * pick

    other = pc.f + 1 - 2 * c
    bsend[...] = basis_rows(other)
    basis_out_swap = pc.copy(bsend, brecv, pc.partner())
    bown[...] = basis_rows(pc.f)
    store(bown, basis_next.at[c])
    for h in range(2):
        orth[h] = orth[h] * (math.sqrt(D / RANK) * inv)
    update_swaps = []
    for i in range(2):
        for j in range(2):
            cols = pl.ds(512 * i + 256 * j, 256)
            usend[i, :, 256 * j:256 * j + 256] = dot(orth[1 - c], right[:, cols], 1, 0, HIGH)
        update_swaps.append(pc.copy(usend.at[i], urecv.at[i], pc.partner()))
    momentum_swap.wait_recv()
    store(mrecv, momentum_next.at[1 - c])

    def direction(cols):
        upd[c, :, cols] = dot(orth[c], right[:, cols], 1, 0, HIGH).astype(jnp.bfloat16)

    columns(direction)
    store(upd.at[c], update.at[c])
    basis_out_swap.wait_recv()
    store(brecv, basis_next.at[1 - c])
    for i in range(2):
        update_swaps[i].wait_recv()
        upd[1 - c, :, 512 * i:512 * i + 512] = urecv[i].astype(jnp.bfloat16)
    store(upd.at[1 - c], update.at[1 - c])
    for cp in stores:
        cp.wait()
    pc.drain()


def place_kernel(update, momentum_next, basis_next, update_out, momentum_out, basis_out, uv, mv, bv, sem):
    parts = [(basis_next, bv, basis_out, pl.ds(0, 16))]
    for i in range(2):
        parts.append((momentum_next, mv, momentum_out, pl.ds(128 * i, 128)))
        parts.append((update, uv, update_out, pl.ds(128 * i, 128)))
    loads, stores = [], []
    for m in range(2):
        for src, held, dst, rows in parts:
            i = len(loads)
            loads.append(pltpu.make_async_copy(src.at[m, rows], held.at[m, rows], sem.at[2 * i]))
            stores.append(pltpu.make_async_copy(held.at[m, rows], dst.at[m, rows], sem.at[2 * i + 1]))
    for cp in loads:
        cp.start()
    for a, b in zip(loads, stores):
        a.wait()
        b.start()
    for cp in stores:
        cp.wait()


def shards(gradient, momentum, right_basis):
    vmem = pl.BlockSpec(memory_space=pltpu.VMEM)
    anywhere = pl.BlockSpec(memory_space=pl.ANY)
    shape = lambda s: jax.ShapeDtypeStruct(s, F32)
    buf = lambda *s: pltpu.VMEM(s, F32)
    half = pltpu.VMEM((2, 256, 1024), jnp.bfloat16)
    out_shape = (jax.ShapeDtypeStruct((2, 256, 1024), jnp.bfloat16), shape((2, 256, 1024)), shape((2, 16, 1024)))
    n = 208
    results = pl.pallas_call(
        kernel,
        out_shape=out_shape,
        in_specs=[anywhere, anywhere, vmem],
        out_specs=[anywhere] * 3,
        scratch_shapes=[
            half, buf(2, 256, 1024), half, buf(2, 256, 512), buf(2, 256, 512), buf(256, 1024),
            buf(16, 1024), buf(16, 1024), buf(16, 1024),
            buf(2, 256, 1024), buf(256, 1024), buf(4, 4, 2, 16, 1024),
            buf(4, 8, 64, 128), buf(7, 4, 64, 128), buf(2, 8, 64, 256), pltpu.VMEM((RANK, RANK), jnp.bfloat16),
            buf(4, 4, 2, 40, 128), buf(2, 3, 4, 40, 128), buf(2, 4, 40, 128), buf(2, 3, 40, 128),
            buf(8, 16, 128), buf(7, 16, 128), buf(8, 16, 128), buf(4, 4, 2, 40, 128),
            buf(2, 4, 4, 2, 8, 1024), buf(2, 2, 3, 4, 8, 1024), buf(2, 2, 4, 8, 1024), buf(2, 2, 3, 8, 1024),
            buf(2, 4, 4, 2, 8, 1024),
            buf(10, 128, 128), buf(6, 128, 128), buf(RANK, RANK),
            buf(RANK, 1024), buf(2, 256, RANK), buf(8, 8, 128),
            pltpu.SemaphoreType.DMA((n,)), pltpu.SemaphoreType.DMA((n,)), pltpu.SemaphoreType.DMA((10,)),
        ],
        compiler_params=pltpu.CompilerParams(
            collective_id=0, has_side_effects=True, vmem_limit_bytes=VMEM_BYTES
        ),
        name="dion",
    )(gradient, momentum, right_basis)
    return pl.pallas_call(
        place_kernel,
        out_shape=out_shape,
        in_specs=[anywhere] * 3,
        out_specs=[anywhere] * 3,
        scratch_shapes=[half, buf(2, 256, 1024), buf(2, 16, 1024), pltpu.SemaphoreType.DMA((20,))],
        compiler_params=pltpu.CompilerParams(vmem_limit_bytes=VMEM_BYTES),
        name="place",
    )(*results)


def solution(mesh):
    placed = (P(None, "fsdp", "tp"), P(None, "fsdp", "tp"), P(None, "fsdp", "tp"))
    return jax.shard_map(
        shards,
        mesh=mesh,
        in_specs=placed,
        out_specs=placed,
        check_vma=False,
    )
```

```python
import math

import jax
import jax.numpy as jnp
from jax import lax
from jax.experimental import pallas as pl
from jax.experimental.pallas import tpu as pltpu
from jax.sharding import PartitionSpec as P

D = 8192
RANK = 512
momentum_decay = 0.8
epsilon_sq = 1e-06
MESH = pl.DeviceIdType.MESH
F32 = jnp.float32
HIGH = lax.Precision.HIGH
HIGHEST = lax.Precision.HIGHEST
VMEM_BYTES = 56 * 1024 * 1024


def dot(a, b, ca, cb, precision):
    return lax.dot_general(
        a, b, (((ca,), (cb,)), ((), ())), precision=precision, preferred_element_type=F32
    )


class Place:
    def __init__(self, send_sem, recv_sem):
        f = lax.axis_index("fsdp")
        self.f = f
        self.z = lax.axis_index("tp")
        self.c = lax.rem(f, 2)
        self.x = lax.rem(f // 2, 4)
        self.y = f // 8
        self.send_sem, self.recv_sem = send_sem, recv_sem
        self.count = 0
        self.open = []

    def dev(self, y=None, x=None, z=None, c=None):
        y = self.y if y is None else y
        x = self.x if x is None else x
        c = self.c if c is None else c
        z = self.z if z is None else z
        return ((y * 4 + x) * 2 + c, z)

    def partner(self):
        return self.dev(c=1 - self.c)

    def xs(self, d):
        return lax.rem(self.x + d, 4)

    def ys(self, d):
        return lax.rem(self.y + d, 4)

    def zs(self, d):
        return lax.rem(self.z + d, 8)

    def reserve(self, n):
        i = self.count
        self.count += n
        assert self.count <= self.send_sem.shape[0]
        return i

    def copy(self, src, dst, to, recv=None):
        i = self.reserve(1)
        cp = pltpu.make_async_remote_copy(
            src_ref=src,
            dst_ref=dst,
            send_sem=self.send_sem.at[i],
            recv_sem=self.recv_sem.at[i if recv is None else recv],
            device_id=to,
            device_id_type=MESH,
        )
        cp.start()
        self.open.append(cp)
        return cp

    def barrier(self, peers):
        sem = pltpu.get_barrier_semaphore()
        for p in peers:
            pl.semaphore_signal(sem, inc=1, device_id=p, device_id_type=MESH)
        pl.semaphore_wait(sem, len(peers))

    def drain(self, keep=0):
        n = len(self.open) - keep
        for cp in self.open[:n]:
            cp.wait_send()
        self.open = self.open[n:]


def received(copies):
    for cp in copies:
        cp.wait_recv()


class Gather:
    def __init__(self, pc, buf):
        self.pc, self.buf = pc, buf

    def first(self):
        pc, buf = self.pc, self.buf
        self.one = []
        for d in (1, 3, 2):
            a, b = buf.at[pc.y, pc.x, 0], buf.at[pc.y, pc.x, 1]
            self.one.append(pc.copy(a, a, pc.dev(x=pc.xs(d))))
            self.one.append(pc.copy(b, b, pc.dev(y=pc.ys(d))))

    def second(self, ways=(1, 3, 2)):
        received(self.one)
        self.two = {}
        self.send_on(ways)

    def send_on(self, ways):
        pc, buf = self.pc, self.buf
        for d in ways:
            a, b = buf.at[pc.y, :, 0], buf.at[:, pc.x, 1]
            self.two[d] = (pc.copy(a, a, pc.dev(y=pc.ys(d))), pc.copy(b, b, pc.dev(x=pc.xs(d))))

    def finish(self):
        for d in (1, 3, 2):
            received(self.two[d])


class Scatter:
    def __init__(self, pc, buf, r1, acc, r2):
        self.pc, self.buf, self.r1, self.acc, self.r2 = pc, buf, r1, acc, r2

    def first(self):
        pc, buf = self.pc, self.buf
        self.one = []
        for d in (1, 3, 2):
            self.one.append(pc.copy(buf.at[pc.ys(d), :, 0], self.r1.at[0, d - 1], pc.dev(y=pc.ys(d))))
            self.one.append(pc.copy(buf.at[:, pc.xs(d), 1], self.r1.at[1, d - 1], pc.dev(x=pc.xs(d))))

    def second(self):
        pc, buf, r1, acc = self.pc, self.buf, self.r1, self.acc
        received(self.one)
        acc[0] = buf[pc.y, :, 0] + r1[0, 0] + r1[0, 1] + r1[0, 2]
        acc[1] = buf[:, pc.x, 1] + r1[1, 0] + r1[1, 1] + r1[1, 2]
        self.two = []
        for d in (1, 3, 2):
            self.two.append(pc.copy(acc.at[0, pc.xs(d)], self.r2.at[0, d - 1], pc.dev(x=pc.xs(d))))
            self.two.append(pc.copy(acc.at[1, pc.ys(d)], self.r2.at[1, d - 1], pc.dev(y=pc.ys(d))))

    def finish(self):
        pc, acc, r2 = self.pc, self.acc, self.r2
        received(self.two)
        own0 = acc[0, pc.x] + r2[0, 0] + r2[0, 1] + r2[0, 2]
        own1 = acc[1, pc.y] + r2[1, 0] + r2[1, 1] + r2[1, 2]
        return own0, own1


def factor_block(load, tick):
    groups = 16
    a = [load(r) for r in range(groups)]
    lane = lax.broadcasted_iota(jnp.int32, (8, 128), 1)
    sub = lax.broadcasted_iota(jnp.int32, (8, 128), 0)
    out = [None] * groups

    def column(v, j):
        return jnp.broadcast_to(v[:, j:j + 1], (8, 128))

    def spread(v, i):
        return jnp.broadcast_to(v[i:i + 1, :], (8, 128))

    def recip(v):
        return pl.reciprocal(v, approx=True)

    for q in range(32):
        r0, s0, j0 = q // 2, 4 * (q % 2), 4 * q
        end = 4 * (r0 // 4) + 4
        rows = [spread(a[r0], s0 + s) for s in range(4)]
        cols = [column(a[r0], j0 + t) for t in range(4)]
        p = {(s, t): spread(cols[t], s0 + s) for s in range(4) for t in range(s, 4)}
        inside = (lane >= j0) & (lane < j0 + 4)
        sc = [lax.rsqrt(p[s, s]) for s in range(4)]
        v = [jnp.where(inside, jnp.where(lane == j0 + s, 1.0, 0.0), rows[s]) * sc[s] for s in range(4)]
        r = {(s, t): p[s, t] * (sc[s] * sc[t]) for s in range(4) for t in range(s + 1, 4)}
        l10, l20, l30 = r[0, 1], r[0, 2], r[0, 3]
        u11, u22, u33 = 1.0 - l10 * l10, 1.0 - l20 * l20, 1.0 - l30 * l30
        u12, u13, u23 = r[1, 2] - l10 * l20, r[1, 3] - l10 * l30, r[2, 3] - l20 * l30
        v22, v23, v33 = u11 * u22 - u12 * u12, u11 * u23 - u12 * u13, u11 * u33 - u13 * u13
        w33 = v22 * v33 - v23 * v23
        i1, i2, i3 = recip(u11), recip(v22), recip(w33)
        l21, l31, l32 = u12 * i1, u13 * i1, v23 * i2
        d1, d2, d3 = i1, u11 * i2, (u11 * v22) * i3
        n10, n21, n32 = -l10, -l21, -l32
        n20 = l21 * l10 - l20
        n31 = l32 * l21 - l31
        n30 = l31 * l10 - l30 - l32 * n20
        n = [[None] * 4, [n10], [n20, n21], [n30, n31, n32]]
        m = {}
        e1 = d1 * n10
        e20, e21 = d2 * n20, d2 * n21
        m[0, 0] = (1.0 + e1 * n10 + e20 * n20) + d3 * (n30 * n30)
        m[0, 1] = (e1 + e20 * n21) + d3 * (n30 * n31)
        m[0, 2] = e20 + d3 * (n30 * n32)
        m[0, 3] = d3 * n30
        m[1, 1] = (d1 + e21 * n21) + d3 * (n31 * n31)
        m[1, 2] = e21 + d3 * (n31 * n32)
        m[1, 3] = d3 * n31
        m[2, 2] = d2 + d3 * (n32 * n32)
        m[2, 3] = d3 * n32
        m[3, 3] = d3
        w = []
        for s in range(4):
            t = [m[min(s, t), max(s, t)] * v[t] for t in range(4)]
            w.append(((t[0] + t[1]) + (t[2] + t[3])) * sc[s])
        f = [None, d1 * lax.rsqrt(d1), d2 * lax.rsqrt(d2), d3 * lax.rsqrt(d3)]
        done = [v[0]]
        for s in range(1, 4):
            t = v[s]
            for k in range(s):
                t = t + n[s][k] * v[k]
            done.append(f[s] * t)
        o = done[0]
        for s in range(1, 4):
            o = jnp.where(sub == s0 + s, done[s], o)
        out[r0] = o if s0 == 0 else jnp.where(sub < 4, out[r0], o)
        for g in range(r0 if s0 == 0 else r0 + 1, end):
            if g > r0:
                cols = [column(a[g], j0 + t) for t in range(4)]
            t = [cols[t] * w[t] for t in range(4)]
            a[g] = jnp.where(inside, 0.0, a[g]) - ((t[0] + t[1]) + (t[2] + t[3]))
        if q % 8 == 7 and end < groups:
            new = jnp.concatenate(out[end - 4:end], axis=0)
            lanes = lax.broadcasted_iota(jnp.int32, (32, 128), 1)
            over = lanes > 8 * end - 32 + lax.broadcasted_iota(jnp.int32, (32, 128), 0)
            right = jnp.where(lanes >= 8 * end, new, 0.0)
            step = dot(right, jnp.where(over, right, new), 0, 0, HIGHEST)
            done_lanes = (lane >= 8 * end - 32) & (lane < 8 * end)
            for g in range(end, groups):
                a[g] = jnp.where(done_lanes, 0.0, a[g]) - step[8 * g:8 * g + 8]
        tick(q)
    return out


def kernel(
    grad, mom, rb, update, momentum_next, basis_next,
    gv, mv, upd, usend, urecv, mrecv, bown, bsend, brecv, blend, blend_send, basis, lpart, lrecv, left, perm,
    gbuf, gr1, gacc, gr2, zsrc, zpart, zfull, gfull,
    wbuf, wr1, wacc, wr2, wall,
    work, ybuf, tri, right, orth, squares,
    send_sem, recv_sem, local_sem,
):
    pc = Place(send_sem, recv_sem)
    c, x, y, z = pc.c, pc.x, pc.y, pc.z
    loads = []
    for i, m in enumerate((1 - c, c)):
        loads.append(
            (
                pltpu.make_async_copy(mom.at[m], mv.at[m], local_sem.at[2 * i]),
                pltpu.make_async_copy(grad.at[m], gv.at[m], local_sem.at[2 * i + 1]),
            )
        )
        for cp in loads[i]:
            cp.start()
    peers = [pc.partner()]
    peers += [pc.dev(x=pc.xs(d), c=m) for d in (1, 2, 3) for m in (0, 1)]
    peers += [pc.dev(y=pc.ys(d), c=m) for d in (1, 2, 3) for m in (0, 1)]
    peers += [pc.dev(z=pc.zs(d)) for d in range(1, 8)]
    pc.barrier(peers)

    first = pc.reserve(6)
    slot = lambda d, h: first + 2 * (d - 1) + h
    for d in (1, 3, 2):
        to_y, to_x = lax.rem(y + d * c, 4), lax.rem(x + d * (1 - c), 4)
        for m in range(2):
            pc.copy(rb.at[m], basis.at[y, x, c], pc.dev(y=to_y, x=to_x, c=m), recv=slot(d, c))
    basis_swap = pc.copy(rb.at[1 - c], basis.at[y, x, c], pc.partner())
    basis[y, x, c] = rb[c]
    for cp in loads[0]:
        cp.wait()
    blend_send[...] = mv[1 - c] + gv[1 - c].astype(F32)
    blend_swap = pc.copy(blend_send, blend.at[c], pc.partner())
    for cp in loads[1]:
        cp.wait()
    blend[c] = mv[c] + gv[c].astype(F32)
    basis_swap.wait_recv()
    for d in (1, 3, 2):
        for h in range(2):
            pltpu.make_async_remote_copy(
                src_ref=rb.at[0],
                dst_ref=basis.at[y, x, h],
                send_sem=send_sem.at[slot(d, h)],
                recv_sem=recv_sem.at[slot(d, h)],
                device_id=pc.partner(),
                device_id_type=MESH,
            ).wait_recv()
    gather = Gather(pc, basis)
    gather.one = []
    gather.second((1, 3))
    at = lax.broadcasted_iota(jnp.int32, (RANK, RANK), 0)
    group, half = at // 128, (at // 64) % 2
    index, low = (at // 16) % 4, at % 16
    py = jnp.where(half == 0, (y + group) % 4, index)
    px = jnp.where(half == 0, index, (x + group) % 4)
    rank = ((py * 4 + px) * 2 + half) * 16 + low
    perm[...] = jnp.where(lax.broadcasted_iota(jnp.int32, (RANK, RANK), 1) == rank, 1.0, 0.0).astype(jnp.bfloat16)
    blend_swap.wait_recv()
    sums_in = []
    for d in (0, 3, 1, 2):
        if d:
            received(gather.two[4 - d])
        if d == 3:
            gather.send_on((2,))
        rows = jnp.concatenate(
            [basis[pc.ys(d), :, 0].reshape(64, 1024), basis[:, pc.xs(d), 1].reshape(64, 1024)], axis=0
        )
        part = dot(blend[...].reshape(512, 1024), rows, 1, 1, HIGH)
        lpart[d] = part.reshape(8, 64, 128)
        for e in (4, 3, 5, 2, 6, 1, 7):
            sums_in.append(pc.copy(lpart.at[d, pc.zs(e)], lrecv.at[e - 1, d], pc.dev(z=pc.zs(e))))
    received(sums_in)
    own = []
    for d in range(4):
        s = lpart[d, z]
        for e in range(7):
            s = s + lrecv[e, d]
        own.append(s)
    own = jnp.concatenate(own, axis=1)
    high = own.astype(jnp.bfloat16)
    rest = own - high.astype(F32)
    mid = rest.astype(jnp.bfloat16)
    low = (rest - mid.astype(F32)).astype(jnp.bfloat16)
    parts = dot(jnp.concatenate([high, mid, low], axis=0), perm[...], 1, 0, None)
    own = (parts[0:64] + parts[64:128]) + parts[128:192]
    for q in range(2):
        left[q, z] = own[:, 256 * q:256 * q + 256]

    def ring(step):
        up, down = pc.dev(z=pc.zs(1)), pc.dev(z=pc.zs(7))
        copies = []
        for q in range(2):
            a, b = left.at[q, pc.zs(9 - step)], left.at[q, pc.zs(step - 1)]
            if step == 4:
                a, b = a.at[pl.ds(0, 32)], b.at[pl.ds(32, 32)]
            copies += [pc.copy(a, a, up), pc.copy(b, b, down)]
        return copies

    blocks = []
    for i in range(4):
        row = dot(own[:, 128 * i:128 * i + 128], own[:, :128 * i + 128], 0, 0, HIGHEST)
        blocks += [row[:, 128 * j:128 * j + 128] for j in range(i + 1)]
    gbuf[...] = jnp.concatenate(blocks, axis=0).reshape(4, 4, 2, 40, 128)
    gscatter = Scatter(pc, gbuf, gr1, gacc, gr2)
    gscatter.first()
    lefts = ring(1)
    received(lefts)
    lefts = ring(2)
    gscatter.second()
    own0, own1 = gscatter.finish()
    zsrc[0:5] = jnp.concatenate([own0, own1], axis=0).reshape(5, 16, 128)
    zsrc[5:8] = jnp.zeros((3, 16, 128), F32)
    zs = []
    for d in (4, 3, 5, 2, 6, 1, 7):
        zs.append(pc.copy(zsrc.at[pc.zs(d)], zpart.at[d - 1], pc.dev(z=pc.zs(d))))
    received(lefts)
    lefts = ring(3)
    received(zs)
    total = zsrc[z]
    for d in range(7):
        total = total + zpart[d]
    zfull[z] = total
    zs = []
    for d in (4, 3, 5, 2, 6, 1, 7):
        zs.append(pc.copy(zfull.at[z], zfull.at[z], pc.dev(z=pc.zs(d))))
    received(lefts)
    lefts = ring(4)
    received(zs)
    gfull[y, x] = zfull[0:5].reshape(2, 40, 128)
    ggather = Gather(pc, gfull)
    ggather.first()
    received(lefts)
    wscatter, wgather = [], []
    for q in range(2):
        for i in range(2):
            lt = left[q, :, :, 128 * i:128 * i + 128].reshape(RANK, 128)
            part = dot(lt, blend[...].reshape(512, 1024), 0, 0, HIGH)
            wbuf[q, 2 * i:2 * i + 2] = part.reshape(2, 4, 2, 8, 1024)
        wscatter.append(Scatter(pc, wbuf.at[q], wr1.at[q], wacc.at[q], wr2.at[q]))
        if q == 0:
            ggather.second()
        wscatter[q].first()
        wgather.append(Gather(pc, wall.at[q]))
    pc.drain(keep=18)
    ggather.finish()

    def w_gather(q):
        o0, o1 = wscatter[q].finish()
        wall[q, y, x, 0] = o0
        wall[q, y, x, 1] = o1
        wgather[q].first()

    def w_step1():
        wscatter[0].second()

    def w_step2():
        wscatter[1].second()
        w_gather(0)

    def w_step3():
        w_gather(1)
        wgather[0].second()

    def w_step4():
        wgather[1].second()

    def w_last():
        wgather[0].finish()
        wgather[1].finish()
        pending.extend(raw_job(i, j) for j in range(4) for i in range(3))
        pending.extend(feed_job(h, j) for j in range(4) for h in range(2))

    def w_part(q, cols):
        return wall[q, :, :, :, :, cols].reshape(256, 256)

    def raw_job(i, j):
        def job():
            cols = pl.ds(256 * j, 256)
            n = 128 * (i + 1)
            wj = jnp.concatenate([w_part(q, cols) for q in range(2 if i > 1 else 1)], axis=0)[:n]
            right[128 * i:128 * i + 128, cols] = dot(tri[128 * i:128 * i + 128, 0:n], wj, 1, 0, HIGH)

        return job

    def feed_job(h, j):
        def job():
            cols = pl.ds(256 * j, 256)
            back = dot(orth[h, :, 0:384], right[0:384, cols], 1, 0, HIGH)
            blend[h, :, cols] = blend[h, :, cols] - (1.0 - momentum_decay) * back

        return job

    def orth_job(k, h):
        def job():
            n = 128 * (k + 1)
            rows = jnp.concatenate([left[q, 4 * h:4 * h + 4].reshape(256, 256) for q in range(2)], axis=1)[:, :n]
            orth[h, :, 128 * k:n] = dot(rows, tri[128 * k:n, 0:n], 1, 1, HIGH)

        return job

    events = {(0, 28): w_step1, (1, 8): w_step2, (1, 20): w_step3, (2, 4): w_step4, (3, 12): w_last}
    flat = gfull[...].reshape(1280, 128)
    for b in range(10):
        work[b] = flat[128 * b:128 * b + 128]
    at = lambda i, j: i * (i + 1) // 2 + j
    yat = lambda i, j: i * (i - 1) // 2 + j
    rowi = lax.broadcasted_iota(jnp.int32, (128, 128), 0)
    coli = lax.broadcasted_iota(jnp.int32, (128, 128), 1)
    pending = []

    def tri_row(k, inv):
        for j in range(k):
            tri[128 * k:128 * k + 128, 128 * j:128 * j + 128] = dot(inv, ybuf[yat(k, j)], 1, 0, HIGHEST)
        tri[128 * k:128 * k + 128, 128 * k:128 * k + 128] = inv

    def later(k, inv):
        def solve(i):
            work[at(i, k)] = dot(work[at(i, k)], inv, 1, 1, HIGHEST)

        def trail(i, j):
            work[at(i, j)] = work[at(i, j)] - dot(work[at(i, k)], work[at(j, k)], 1, 1, HIGHEST)

        def inverse(i, j):
            new = dot(work[at(i, k)], tri[128 * k:128 * k + 128, 128 * j:128 * j + 128], 1, 0, HIGHEST)
            ybuf[yat(i, j)] = -new if j == k else ybuf[yat(i, j)] - new

        jobs = [lambda: tri_row(k, inv)]
        for i in range(k + 2, 4):
            jobs.append(lambda i=i: solve(i))
        for i in range(k + 2, 4):
            for j in range(k + 1, i + 1):
                jobs.append(lambda i=i, j=j: trail(i, j))
        for i in range(k + 1, 4):
            for j in range(k + 1):
                jobs.append(lambda i=i, j=j: inverse(i, j))
        return jobs + [orth_job(k, h) for h in range(2)]

    for k in range(4):

        def tick(q, k=k):
            if (k, q) in events:
                events[k, q]()
            if pending and q >= 1:
                pending.pop(0)()

        rows = factor_block(lambda r: work[at(k, k), 8 * r:8 * r + 8, :], tick)
        while pending:
            pending.pop(0)()
        inv = jnp.where(rowi >= coli, jnp.concatenate(rows, axis=0), 0.0)
        if k < 3:
            below = dot(work[at(k + 1, k)], inv, 1, 1, HIGHEST)
            work[at(k + 1, k)] = below
            work[at(k + 1, k + 1)] = work[at(k + 1, k + 1)] - dot(below, below, 1, 1, HIGHEST)
            pending = later(k, inv)
        else:
            tri_row(k, inv)


    def columns(body):
        def step(j, carry):
            body(pl.ds(pl.multiple_of(j * 256, 256), 256))
            return carry

        lax.fori_loop(0, 4, step, 0)

    def raw_end(cols):
        wj = jnp.concatenate([w_part(q, cols) for q in range(2)], axis=0)
        new = dot(tri[384:, :], wj, 1, 0, HIGH)
        right[384:, cols] = new

    columns(raw_end)
    fold = right[:, 0:128] * right[:, 0:128]
    for j in range(1, 8):
        fold = fold + right[:, 128 * j:128 * j + 128] * right[:, 128 * j:128 * j + 128]
    sums = dot(jnp.ones((8, 128), F32), fold, 1, 1, HIGHEST)
    squares[z] = jnp.concatenate([sums[0:1, 128 * j:128 * j + 128] for j in range(4)] * 2, axis=0)
    zs = []
    for d in (4, 3, 5, 2, 6, 1, 7):
        zs.append(pc.copy(squares.at[z], squares.at[z], pc.dev(z=pc.zs(d))))
    stores = []

    def store(src, dst):
        cp = pltpu.make_async_copy(src, dst, local_sem.at[4 + len(stores)])
        cp.start()
        stores.append(cp)

    for h in range(2):
        orth_job(3, h)()

    def feed(h):
        def part(cols):
            back = dot(orth[h, :, 384:], right[384:, cols], 1, 0, HIGH)
            blend[h, :, cols] = blend[h, :, cols] - (1.0 - momentum_decay) * back

        columns(part)

    feed(1 - c)
    momentum_swap = pc.copy(blend.at[1 - c], mrecv, pc.partner())
    feed(c)
    store(blend.at[c], momentum_next.at[c])
    pc.drain(keep=8)
    received(zs)
    total = squares[0]
    for d in range(1, 8):
        total = total + squares[d]
    inverse = lax.rsqrt(total / D + epsilon_sq)
    inv = jnp.concatenate([inverse[j:j + 1] for j in range(4)], axis=1)
    lane = lax.broadcasted_iota(jnp.int32, (16, RANK), 1)
    sub = lax.broadcasted_iota(jnp.int32, (16, RANK), 0)

    def basis_rows(f):
        pick = jnp.sum(jnp.where(lane == f * 16 + sub, inv, 0.0), axis=1, keepdims=True)
        return right[pl.ds(pl.multiple_of(f * 16, 16), 16), :] * pick

    other = pc.f + 1 - 2 * c
    bsend[...] = basis_rows(other)
    basis_out_swap = pc.copy(bsend, brecv, pc.partner())
    bown[...] = basis_rows(pc.f)
    store(bown, basis_next.at[c])
    for h in range(2):
        orth[h] = orth[h] * (math.sqrt(D / RANK) * inv)
    update_swaps = []
    for i in range(2):
        for j in range(2):
            cols = pl.ds(512 * i + 256 * j, 256)
            usend[i, :, 256 * j:256 * j + 256] = dot(orth[1 - c], right[:, cols], 1, 0, HIGH)
        update_swaps.append(pc.copy(usend.at[i], urecv.at[i], pc.partner()))
    momentum_swap.wait_recv()
    store(mrecv, momentum_next.at[1 - c])

    def direction(cols):
        upd[c, :, cols] = dot(orth[c], right[:, cols], 1, 0, HIGH).astype(jnp.bfloat16)

    columns(direction)
    store(upd.at[c], update.at[c])
    basis_out_swap.wait_recv()
    store(brecv, basis_next.at[1 - c])
    for i in range(2):
        update_swaps[i].wait_recv()
        upd[1 - c, :, 512 * i:512 * i + 512] = urecv[i].astype(jnp.bfloat16)
    store(upd.at[1 - c], update.at[1 - c])
    for cp in stores:
        cp.wait()
    pc.drain()


def place_kernel(update, momentum_next, basis_next, update_out, momentum_out, basis_out, uv, mv, bv, sem):
    parts = [(basis_next, bv, basis_out, pl.ds(0, 16))]
    for i in range(2):
        parts.append((momentum_next, mv, momentum_out, pl.ds(128 * i, 128)))
        parts.append((update, uv, update_out, pl.ds(128 * i, 128)))
    loads, stores = [], []
    for m in range(2):
        for src, held, dst, rows in parts:
            i = len(loads)
            loads.append(pltpu.make_async_copy(src.at[m, rows], held.at[m, rows], sem.at[2 * i]))
            stores.append(pltpu.make_async_copy(held.at[m, rows], dst.at[m, rows], sem.at[2 * i + 1]))
    for cp in loads:
        cp.start()
    for a, b in zip(loads, stores):
        a.wait()
        b.start()
    for cp in stores:
        cp.wait()


def shards(gradient, momentum, right_basis):
    vmem = pl.BlockSpec(memory_space=pltpu.VMEM)
    anywhere = pl.BlockSpec(memory_space=pl.ANY)
    shape = lambda s: jax.ShapeDtypeStruct(s, F32)
    buf = lambda *s: pltpu.VMEM(s, F32)
    half = pltpu.VMEM((2, 256, 1024), jnp.bfloat16)
    out_shape = (jax.ShapeDtypeStruct((2, 256, 1024), jnp.bfloat16), shape((2, 256, 1024)), shape((2, 16, 1024)))
    n = 208
    results = pl.pallas_call(
        kernel,
        out_shape=out_shape,
        in_specs=[anywhere, anywhere, vmem],
        out_specs=[anywhere] * 3,
        scratch_shapes=[
            half, buf(2, 256, 1024), half, buf(2, 256, 512), buf(2, 256, 512), buf(256, 1024),
            buf(16, 1024), buf(16, 1024), buf(16, 1024),
            buf(2, 256, 1024), buf(256, 1024), buf(4, 4, 2, 16, 1024),
            buf(4, 8, 64, 128), buf(7, 4, 64, 128), buf(2, 8, 64, 256), pltpu.VMEM((RANK, RANK), jnp.bfloat16),
            buf(4, 4, 2, 40, 128), buf(2, 3, 4, 40, 128), buf(2, 4, 40, 128), buf(2, 3, 40, 128),
            buf(8, 16, 128), buf(7, 16, 128), buf(8, 16, 128), buf(4, 4, 2, 40, 128),
            buf(2, 4, 4, 2, 8, 1024), buf(2, 2, 3, 4, 8, 1024), buf(2, 2, 4, 8, 1024), buf(2, 2, 3, 8, 1024),
            buf(2, 4, 4, 2, 8, 1024),
            buf(10, 128, 128), buf(6, 128, 128), buf(RANK, RANK),
            buf(RANK, 1024), buf(2, 256, RANK), buf(8, 8, 128),
            pltpu.SemaphoreType.DMA((n,)), pltpu.SemaphoreType.DMA((n,)), pltpu.SemaphoreType.DMA((10,)),
        ],
        compiler_params=pltpu.CompilerParams(
            collective_id=0, has_side_effects=True, vmem_limit_bytes=VMEM_BYTES
        ),
        name="dion",
    )(gradient, momentum, right_basis)
    return pl.pallas_call(
        place_kernel,
        out_shape=out_shape,
        in_specs=[anywhere] * 3,
        out_specs=[anywhere] * 3,
        scratch_shapes=[half, buf(2, 256, 1024), buf(2, 16, 1024), pltpu.SemaphoreType.DMA((20,))],
        compiler_params=pltpu.CompilerParams(vmem_limit_bytes=VMEM_BYTES),
        name="place",
    )(*results)


def solution(mesh):
    placed = (P(None, "fsdp", "tp"), P(None, "fsdp", "tp"), P(None, "fsdp", "tp"))
    return jax.shard_map(
        shards,
        mesh=mesh,
        in_specs=placed,
        out_specs=placed,
        check_vma=False,
    )
```
